32 devices in a mesh: dp: 4 (over z), seq: 8 (over y, x, core).
Axes of the slice: x: 2, y: 2, z: 4, core: 2. Of those that a mesh axis runs over, the one named last changes fastest.
Arguments:
- query_tiles: bfloat16 [4, 8, 128, 2048], P('dp', 'seq'), may hold values from -20 to 20
- key_tiles: bfloat16 [4, 8, 128, 2048], P('dp', 'seq'), may hold values from -6 to 6
- value_tiles: bfloat16 [4, 8, 128, 2048], P('dp', 'seq'), may hold values from -6 to 6
- attn_grad: bfloat16 [4, 8, 128, 2048], P('dp', 'seq'), may hold values from -6 to 6
- proj_grad: bfloat16 [4, 8, 128, 3072], P('dp', 'seq'), may hold values from -6 to 6
- neighbour: int32 [4, 8], P('dp'), may hold values from 0 to 7, as said below
Outputs:
- query_grad: bfloat16 [4, 8, 128, 2048], P('dp', 'seq')
- key_grad: bfloat16 [4, 8, 128, 2048], P('dp', 'seq')
- value_grad: bfloat16 [4, 8, 128, 2048], P('dp', 'seq')
- update: float32 [2048, 3072], P('dp', 'seq')
The draws below stay inside these ranges and needn't reach their ends.
Inputs may be any that keep to these rules, and one draw needn't show every extreme that they name: neighbour[v, t] is t - 1 or t + 1; tile 0 names tile 1, tile 1 names tile 0, tile 8 - 2 names tile 8 - 1 and tile 8 - 1 names tile 8 - 2.
All inputs are finite; a program needn't handle non-finite values.
Results may differ from the reference program's by a relative error of at most 0.024.
Values may be sent and summed in bfloat16 or wider, within the bound.
No kernel may reach another device: no remote copies, remote signals or barrier semaphores. Data moves between devices by JAX's collectives and lax.ppermute only.
A program may use at most 128 MiB of HBM per device.

```python
import jax
import jax.numpy as jnp
from jax import lax

D = 3072
HEADS = 16
HEAD_DIM = 128
TILE = 128
NS_STEPS = 5
HD = 2048
VIDEOS = 4
TILES = 8


def draw_query_tiles(key, part):
    key = jax.random.fold_in(key, 11)
    first = jax.random.fold_in(key, 0)
    shape = (VIDEOS, TILES, TILE, HEADS * HEAD_DIM)
    result = jnp.clip(jax.random.normal(first, shape, jnp.float32), -6.0, 6.0)
    return result.astype(jnp.bfloat16)


def draw_key_tiles(key, part):
    key = jax.random.fold_in(key, 23)
    first = jax.random.fold_in(key, 0)
    shape = (VIDEOS, TILES, TILE, HEADS * HEAD_DIM)
    result = jnp.clip(jax.random.normal(first, shape, jnp.float32), -6.0, 6.0)
    return result.astype(jnp.bfloat16)


def draw_neighbour(key, part):
    key = jax.random.fold_in(key, 5)
    side = jax.random.randint(key, (VIDEOS, TILES), 0, 2)
    tile_ids = jnp.arange(TILES, dtype=jnp.int32)[None, :]
    target = tile_ids - 1 + 2 * side
    target = jnp.where(tile_ids == 1, 0, target)
    target = jnp.where(tile_ids == TILES - 2, TILES - 1, target)
    target = jnp.where(tile_ids == 0, 1, target)
    target = jnp.where(tile_ids == TILES - 1, TILES - 2, target)
    return target.astype(jnp.int32)


def spiked(values, own_key, source, target, parts, factor):
    owner, partner = [(jnp.arange(values.shape[position]) // (values.shape[position] // parts)).reshape([-1 if axis == position else 1 for axis in range(values.ndim)]) for position in (source, target)]
    chosen = jax.random.permutation(own_key, parts)[partner]
    strong = (owner == chosen) | (owner == (partner + parts // 2) % parts)
    return jnp.where(strong, factor * values, values)


def block_scale(own_key, shape, cuts, smallest, top_value):
    loudness = 1.0
    for position, blocks in cuts:
        heights = jax.random.uniform(jax.random.fold_in(jax.random.fold_in(own_key, 6), position), (blocks,), jnp.float32, smallest / len(cuts), top_value / len(cuts))
        loudness = loudness * jnp.repeat(jnp.exp(heights), shape[position] // blocks).reshape((-1,) + (1,) * (len(shape) - 1 - position))
    return loudness


def scatter_about(own_key, dims, spread, limit, cuts=(), kind=jnp.bfloat16):
    values = spread * jax.random.normal(own_key, dims, jnp.float32)
    if cuts:
        values = values * block_scale(own_key, dims, cuts, -0.22, 0.18)
    return jnp.clip(values, -limit, limit).astype(kind)


def gaussian_with(stream_key, shape, deviation, reach, cuts, heavy, kind=jnp.bfloat16):
    entries = deviation * jax.random.normal(stream_key, shape, jnp.float32)
    if cuts:
        entries = entries * block_scale(stream_key, shape, cuts, -0.22, 0.18)
    return jnp.clip(spiked(entries, jax.random.fold_in(stream_key, 3), *heavy), -reach, reach).astype(kind)


def setup_inputs(seed: int = 0) -> dict:
    seeds = jax.random.split(jax.random.key(seed), 7)
    query_tiles = draw_query_tiles(jax.random.fold_in(seeds[6], 71), 0)
    key_tiles = draw_key_tiles(jax.random.fold_in(seeds[6], 71), 0)
    value_tiles = scatter_about(seeds[2], (VIDEOS, TILES, TILE, HD), 1.0, 6.0, ((0, 4), (1, 8)))
    attn_grad = scatter_about(seeds[3], (VIDEOS, TILES, TILE, HD), 1.0, 6.0, ((0, 4), (1, 8)))
    proj_grad = gaussian_with(seeds[4], (VIDEOS, TILES, TILE, D), 1.0, 6.0, ((0, 4), (1, 8)), (1, 3, 8, 2.0))
    neighbour = draw_neighbour(jax.random.fold_in(seeds[6], 71), 0)
    return dict(query_tiles=query_tiles, key_tiles=key_tiles, value_tiles=value_tiles, attn_grad=attn_grad, proj_grad=proj_grad, neighbour=neighbour)


coeff_a = 3.4445
coeff_b = -4.775
coeff_c = 2.0315

def rounded(array):
    return lax.optimization_barrier(array.astype(jnp.bfloat16)).astype(jnp.float32)

def tile_grads(query_rows, key_own, value_own, key_far, value_far, out_grad):
    score_scale = HEAD_DIM ** (-0.5)
    query_h = query_rows.astype(jnp.float32).reshape(TILE, HEADS, HEAD_DIM)
    keys_all = jnp.concatenate([key_own, key_far], 0).astype(jnp.float32).reshape(2 * TILE, HEADS, HEAD_DIM)
    values_all = jnp.concatenate([value_own, value_far], 0).astype(jnp.float32).reshape(2 * TILE, HEADS, HEAD_DIM)
    grad_h = out_grad.astype(jnp.float32).reshape(TILE, HEADS, HEAD_DIM)
    scores = jnp.einsum('ihd,jhd->hij', query_h, keys_all) * score_scale
    row_max = lax.optimization_barrier(jnp.max(scores, axis=-1, keepdims=True))
    exp_scores = jnp.exp(scores - row_max)
    weights = exp_scores / lax.optimization_barrier(jnp.sum(exp_scores, axis=-1, keepdims=True))
    weights_b = rounded(weights)
    attended = rounded(jnp.einsum('hij,jhd->ihd', weights_b, values_all))
    row_delta = lax.optimization_barrier(jnp.sum(grad_h * attended, axis=-1)).T
    dweights = jnp.einsum('ihd,jhd->hij', grad_h, values_all)
    dscore_b = rounded(weights * (dweights - row_delta[:, :, None]))
    query_grad = jnp.einsum('hij,jhd->ihd', dscore_b, keys_all) * score_scale
    key_grad = jnp.einsum('hij,ihd->jhd', dscore_b, query_h) * score_scale
    value_grad = jnp.einsum('hij,ihd->jhd', weights_b, grad_h)
    width = HEADS * HEAD_DIM
    key_grad = key_grad.reshape(2 * TILE, width)
    value_grad = value_grad.reshape(2 * TILE, width)
    return (query_grad.reshape(TILE, width).astype(jnp.bfloat16), key_grad[:TILE], value_grad[:TILE], key_grad[TILE:].astype(jnp.bfloat16), value_grad[TILE:].astype(jnp.bfloat16), attended.reshape(TILE, width).astype(jnp.bfloat16))

def orthogonalize(grad_w):
    blocks = grad_w.reshape(HEADS, HEAD_DIM, D)
    frob_norm = jnp.sqrt(lax.optimization_barrier(jnp.sum(blocks * blocks, axis=(1, 2), keepdims=True))) + 1e-07
    iterate = blocks / frob_norm
    best = lax.Precision.HIGHEST
    for turn in range(NS_STEPS):
        gram_matrix = jnp.einsum('hid,hjd->hij', iterate, iterate, precision=best)
        polynomial = coeff_b * gram_matrix + coeff_c * jnp.einsum('hij,hjk->hik', gram_matrix, gram_matrix, precision=best)
        iterate = coeff_a * iterate + jnp.einsum('hij,hjd->hid', polynomial, iterate, precision=best)
    return (iterate * (0.2 * D ** 0.5)).reshape(HEADS * HEAD_DIM, D)

def reference(query_tiles, key_tiles, value_tiles, attn_grad, proj_grad, neighbour):
    width = HEADS * HEAD_DIM

    def advance(running, flat_index):
        pair_id = flat_index // TILES
        tile_id = flat_index % TILES
        total = jnp.zeros((width, D), jnp.float32)
        pieces = []
        for member in range(2):
            video_id = 2 * pair_id + member
            far_id = neighbour[video_id, tile_id]
            results = tile_grads(query_tiles[video_id, tile_id], key_tiles[video_id, tile_id], value_tiles[video_id, tile_id], key_tiles[video_id, far_id], value_tiles[video_id, far_id], attn_grad[video_id, tile_id])
            total = total + jnp.dot(results[5].T, proj_grad[video_id, tile_id], preferred_element_type=jnp.float32)
            pieces.append(results[:5])
        stacked = tuple((jnp.stack([pieces[0][k], pieces[1][k]]) for k in range(5)))
        return (running + rounded(total), stacked)
    start = jnp.zeros((width, D), jnp.float32)
    grad_w, outputs = lax.scan(advance, start, jnp.arange(VIDEOS // 2 * TILES, dtype=jnp.int32))
    shape = (VIDEOS, TILES, TILE, width)

    def unpair(array):
        return array.reshape(VIDEOS // 2, TILES, 2, TILE, width).transpose(0, 2, 1, 3, 4).reshape(shape)
    query_grad = unpair(outputs[0])
    key_own = unpair(outputs[1])
    value_own = unpair(outputs[2])
    key_far = unpair(outputs[3]).astype(jnp.float32)
    value_far = unpair(outputs[4]).astype(jnp.float32)
    tile_ids = jnp.arange(TILES, dtype=jnp.int32)[None, :]
    from_left = jnp.concatenate([jnp.zeros((VIDEOS, 1), bool), neighbour[:, :-1] == tile_ids[:, 1:]], 1)
    from_right = jnp.concatenate([neighbour[:, 1:] == tile_ids[:, :-1], jnp.zeros((VIDEOS, 1), bool)], 1)
    left_mask = from_left[:, :, None, None]
    right_mask = from_right[:, :, None, None]
    zeros_tile = jnp.zeros((VIDEOS, 1, TILE, width), jnp.float32)

    def combine(own, far):
        previous = jnp.concatenate([zeros_tile, far[:, :-1]], 1)
        following = jnp.concatenate([far[:, 1:], zeros_tile], 1)
        total = own + jnp.where(left_mask, previous, 0.0) + jnp.where(right_mask, following, 0.0)
        return total.astype(jnp.bfloat16)
    key_grad = combine(key_own, key_far)
    value_grad = combine(value_own, value_far)
    return (query_grad, key_grad, value_grad, orthogonalize(grad_w))
```

```python
import functools

import jax
import jax.numpy as jnp
from jax import lax
from jax.experimental import pallas as pl
from jax.experimental.pallas import tpu as pltpu
from jax.sharding import PartitionSpec as P

HEAD_DIM = 128
NS_STEPS = 5
SCALE = HEAD_DIM ** (-0.5)
coeff_a = 3.4445
coeff_b = -4.775
coeff_c = 2.0315
f32 = jnp.float32
bf16 = jnp.bfloat16
VMEM_LIMIT = 48 * 1024 * 1024


def whole(count):
    return [pl.BlockSpec(memory_space=pltpu.VMEM)] * count


def smem():
    return pl.BlockSpec(memory_space=pltpu.SMEM)


def params():
    return pltpu.CompilerParams(vmem_limit_bytes=VMEM_LIMIT)


def cost(flops, moved, exps=0):
    return pl.CostEstimate(flops=int(flops), bytes_accessed=int(moved), transcendentals=int(exps))


def dot_t(a, b):
    return lax.dot_general(a, b, (((1,), (1,)), ((), ())), preferred_element_type=f32)


def dot_n(a, b):
    return lax.dot_general(a, b, (((1,), (0,)), ((), ())), preferred_element_type=f32)


def dot_l(a, b):
    return lax.dot_general(a, b, (((0,), (0,)), ((), ())), preferred_element_type=f32)


def exact(a, b, dims=((1,), (0,))):
    return lax.dot_general(
        a, b, (dims, ((), ())), precision=lax.Precision.HIGHEST, preferred_element_type=f32
    )


class Plan:
    def __init__(self, head_count):
        self.seq = lax.axis_size("seq")
        self.dp = lax.axis_size("dp")
        self.per_target = head_count // self.dp
        self.low = 2
        self.high = self.per_target // 2
        self.col = self.seq // self.per_target
        self.col_bits = self.col.bit_length() - 1

    def row_part(self, place):
        return (place >> (1 + self.col_bits)) * 2 + (place & 1)

    def row_mask(self, part):
        return ((part >> 1) << (1 + self.col_bits)) | (part & 1)

    def col_part(self, place):
        return (place >> 1) & (self.col - 1)

    def high_part(self, place):
        return place >> (1 + self.col_bits)

    def split_place(self, place):
        return place & 1, self.col_part(place), self.high_part(place)


def shift(value, axis, mask):
    return lax.ppermute(value, axis, [(i, i ^ mask) for i in range(lax.axis_size(axis))])


def head_slice(index):
    return pl.ds(pl.multiple_of(index * HEAD_DIM, HEAD_DIM), HEAD_DIM)


def softmax_pair(query, key_own, key_far):
    s_own = dot_t(query, key_own) * SCALE
    s_far = dot_t(query, key_far) * SCALE
    top = jnp.max(jnp.maximum(s_own, s_far), axis=-1, keepdims=True)
    e_own = jnp.exp(s_own - top)
    e_far = jnp.exp(s_far - top)
    inverse = 1.0 / jnp.sum(e_own + e_far, axis=-1, keepdims=True)
    return e_own * inverse, e_far * inverse


def forward_kernel(plan, near_ref, q, ko, vo, kl, vl, kr, vr, *outs):
    place = lax.axis_index("seq")
    layer = lax.axis_index("dp")
    go_left = near_ref[0, place] < place
    mine = plan.row_part(place)
    for j in range(plan.per_target):
        for i in range(plan.dp):
            at = head_slice((layer ^ i) * plan.per_target + (mine ^ j))
            key_far = jnp.where(go_left, kl[:, at], kr[:, at])
            value_far = jnp.where(go_left, vl[:, at], vr[:, at])
            p_own, p_far = softmax_pair(q[:, at], ko[:, at], key_far)
            att = dot_n(p_own.astype(bf16), vo[:, at]) + dot_n(p_far.astype(bf16), value_far)
            outs[j][:, i * HEAD_DIM : (i + 1) * HEAD_DIM] = att.astype(bf16)


def backward_kernel(near_ref, q, ko, vo, kl, vl, kr, vr, g, dq, dko, dvo, dkf, dvf):
    place = lax.axis_index("seq")
    go_left = near_ref[0, place] < place
    for h in range(q.shape[1] // HEAD_DIM):
        at = slice(h * HEAD_DIM, (h + 1) * HEAD_DIM)
        query, key_own, value_own, grad = q[:, at], ko[:, at], vo[:, at], g[:, at]
        key_far = jnp.where(go_left, kl[:, at], kr[:, at])
        value_far = jnp.where(go_left, vl[:, at], vr[:, at])
        p_own, p_far = softmax_pair(query, key_own, key_far)
        pb_own = p_own.astype(bf16)
        pb_far = p_far.astype(bf16)
        att = (dot_n(pb_own, value_own) + dot_n(pb_far, value_far)).astype(bf16)
        delta = jnp.sum(grad.astype(f32) * att.astype(f32), axis=-1, keepdims=True)
        ds_own = (p_own * (dot_t(grad, value_own) - delta)).astype(bf16)
        ds_far = (p_far * (dot_t(grad, value_far) - delta)).astype(bf16)
        dq[:, at] = ((dot_n(ds_own, key_own) + dot_n(ds_far, key_far)) * SCALE).astype(bf16)
        dko[:, at] = dot_l(ds_own, query) * SCALE
        dvo[:, at] = dot_l(pb_own, grad)
        dkf[:, at] = (dot_l(ds_far, query) * SCALE).astype(bf16)
        dvf[:, at] = dot_l(pb_far, grad).astype(bf16)


def combine_kernel(near_ref, dko, dvo, kl, vl, kr, vr, dk, dv):
    place = lax.axis_index("seq")
    last = lax.axis_size("seq") - 1
    before = near_ref[0, jnp.maximum(place - 1, 0)]
    after = near_ref[0, jnp.minimum(place + 1, last)]
    from_left = (place > 0) & (before == place)
    from_right = (place < last) & (after == place)
    for own, left, right, out in ((dko, kl, kr, dk), (dvo, vl, vr, dv)):
        total = own[...] + jnp.where(from_left, left[...].astype(f32), 0.0)
        out[...] = (total + jnp.where(from_right, right[...].astype(f32), 0.0)).astype(bf16)


def product_kernel(plan, *refs):
    att = refs[: plan.seq]
    cols = refs[plan.seq : plan.seq + 2]
    own = refs[plan.seq + 2]
    outs = refs[plan.seq + 3 : plan.seq + 2 + plan.dp]
    turned = refs[plan.seq + 2 + plan.dp :]
    for k in range(plan.seq):
        core, q, high = plan.split_place(k)
        t = high * plan.col + q
        turned[core][:, t * HEAD_DIM : (t + 1) * HEAD_DIM] = att[k][...].T
    tokens = turned[0].shape[1]
    width = own.shape[1]
    step = 512 if width % 512 == 0 else width
    for i in range(plan.dp):
        rows = slice(i * HEAD_DIM, (i + 1) * HEAD_DIM)
        for c in range(0, width, step):
            total = None
            for core in range(2):
                block = cols[core][:, :, :, c : c + step].reshape(tokens, step)
                part = dot_n(turned[core][rows, :], block)
                total = part if total is None else total + part
            if i == 0:
                own[:, c : c + step] = total
            else:
                outs[i - 1][:, c : c + step] = total.astype(bf16)


def gram_kernel(own, *refs):
    *parts, x, gram = refs
    total = own[...]
    for part in parts:
        total = total + part[...].astype(f32)
    x[...] = total
    gram[...] = exact(total, total, ((1,), (1,)))


def polynomial(gram):
    eye = (
        lax.broadcasted_iota(jnp.int32, gram.shape, 0)
        == lax.broadcasted_iota(jnp.int32, gram.shape, 1)
    ).astype(f32)
    square = jnp.sum(jnp.sum(gram * eye, axis=1, keepdims=True), axis=0, keepdims=True)
    inverse = 1.0 / (jnp.sqrt(square) + 1e-07)
    a = gram * inverse * inverse
    p = None
    for turn in range(NS_STEPS):
        q = coeff_a * eye + coeff_b * a + coeff_c * exact(a, a)
        p = q if p is None else exact(q, p)
        if turn + 1 < NS_STEPS:
            a = exact(exact(q, a), q)
    return p, inverse


def update_kernel(plan, factor, x, gram, gram_other, *outs):
    mine = plan.row_part(lax.axis_index("seq"))
    p, inverse = polynomial(gram[...] + gram_other[...])
    p = p * (inverse * factor)
    width = outs[0].shape[1]
    for j in range(plan.per_target):
        if width % HEAD_DIM == 0:
            block = x[:, pl.ds(pl.multiple_of((mine ^ j) * width, width), width)]
        else:
            block = jnp.zeros((HEAD_DIM, width), f32)
            for r in range(plan.per_target):
                part = x[:, r * width : (r + 1) * width]
                block = jnp.where((mine ^ j) == r, part, block)
        outs[j][...] = exact(p, block).astype(outs[j].dtype)


def place_kernel(plan, *refs):
    *parts, out = refs
    mine = plan.row_part(lax.axis_index("seq"))
    for j, part in enumerate(parts):
        at = pl.ds(pl.multiple_of((mine ^ j) * HEAD_DIM, HEAD_DIM), HEAD_DIM)
        out[at, :] = part[...].astype(f32)


def local(query_tiles, key_tiles, value_tiles, attn_grad, proj_grad, neighbour):
    tile, width = query_tiles.shape[2:]
    depth = proj_grad.shape[3]
    head_count = width // HEAD_DIM
    plan = Plan(head_count)
    n, m, per = plan.seq, plan.dp, plan.per_target
    place = lax.axis_index("seq")
    struct = jax.ShapeDtypeStruct
    query, key, value, grad = (
        a.reshape(tile, width) for a in (query_tiles, key_tiles, value_tiles, attn_grad)
    )

    to_right = [(i, i + 1) for i in range(n - 1) if i + 1 != n - 2]
    to_left = [(i + 1, i) for i in range(n - 1) if i != 1]
    key_left = lax.ppermute(key, "seq", to_right)
    key_right = lax.ppermute(key, "seq", to_left)
    value_left = lax.ppermute(value, "seq", to_right)
    value_right = lax.ppermute(value, "seq", to_left)

    slot = depth // n
    view = proj_grad.reshape(tile, plan.high, plan.col, 2, slot)
    mine = plan.col_part(place)
    columns = [lax.dynamic_index_in_dim(view, mine, 2, keepdims=False).reshape(tile, per * slot)]
    for q in range(1, plan.col):
        give = lax.dynamic_index_in_dim(view, mine ^ q, 2, keepdims=False)
        columns.append(shift(give.reshape(tile, per * slot), "seq", q << 1))
    held = jnp.stack(columns)[None]
    bit = 1
    while bit < plan.high:
        other = shift(held, "seq", bit << (1 + plan.col_bits))
        held = jnp.concatenate([held, other], 0)
        bit *= 2
    held_other = shift(held, "seq", 1)

    attended = pl.pallas_call(
        functools.partial(forward_kernel, plan),
        out_shape=[struct((tile, m * HEAD_DIM), bf16)] * per,
        in_specs=[smem()] + whole(7),
        out_specs=whole(per),
        compiler_params=params(),
        cost_estimate=cost(8 * tile * tile * width, 16 * tile * width, 2 * tile * tile * head_count),
        name="attention_forward",
    )(neighbour, query, key, value, key_left, value_left, key_right, value_right)

    rows = [attended[0]] + [shift(attended[plan.row_part(k)], "seq", k) for k in range(1, n)]

    dq, dko, dvo, dkf, dvf = pl.pallas_call(
        backward_kernel,
        out_shape=[
            struct((tile, width), bf16),
            struct((tile, width), f32),
            struct((tile, width), f32),
            struct((tile, width), bf16),
            struct((tile, width), bf16),
        ],
        in_specs=[smem()] + whole(8),
        out_specs=whole(5),
        compiler_params=params(),
        cost_estimate=cost(28 * tile * tile * width, 30 * tile * width, 2 * tile * tile * head_count),
        name="attention_backward",
    )(neighbour, query, key, value, key_left, value_left, key_right, value_right, grad)

    mine_width = per * slot
    own, *sent = pl.pallas_call(
        functools.partial(product_kernel, plan),
        out_shape=[struct((HEAD_DIM, mine_width), f32)]
        + [struct((HEAD_DIM, mine_width), bf16)] * (m - 1),
        in_specs=whole(n + 2),
        out_specs=whole(m),
        scratch_shapes=[pltpu.VMEM((m * HEAD_DIM, n // 2 * tile), bf16)] * 2,
        compiler_params=params(),
        cost_estimate=cost(
            2 * m * HEAD_DIM * n * tile * mine_width, 2 * n * tile * (mine_width + m * HEAD_DIM)
        ),
        name="gradient_product",
    )(*rows, held, held_other)

    came = [shift(part, "dp", i + 1) for i, part in enumerate(sent)]
    x, gram = pl.pallas_call(
        gram_kernel,
        out_shape=[struct((HEAD_DIM, mine_width), f32), struct((HEAD_DIM, HEAD_DIM), f32)],
        in_specs=whole(m),
        out_specs=whole(2),
        compiler_params=params(),
        cost_estimate=cost(12 * HEAD_DIM * HEAD_DIM * mine_width, 14 * HEAD_DIM * mine_width),
        name="gradient_sum",
    )(own, *came)

    gram_other = jnp.zeros_like(gram)
    for b in range(plan.col_bits):
        gram = gram + gram_other
        gram_other = shift(gram, "seq", 2 << b)

    factor = 0.2 * depth**0.5
    pieces = pl.pallas_call(
        functools.partial(update_kernel, plan, factor),
        out_shape=[struct((HEAD_DIM, slot), f32)] + [struct((HEAD_DIM, slot), bf16)] * (per - 1),
        in_specs=whole(3),
        out_specs=whole(per),
        compiler_params=params(),
        cost_estimate=cost(12 * HEAD_DIM * HEAD_DIM * mine_width, 8 * HEAD_DIM * mine_width),
        name="newton_schulz",
    )(x, gram, gram_other)
    pieces = [pieces[0]] + [
        shift(pieces[j], "seq", plan.row_mask(j)) for j in range(1, per)
    ]
    update = pl.pallas_call(
        functools.partial(place_kernel, plan),
        out_shape=struct((per * HEAD_DIM, slot), f32),
        in_specs=whole(per),
        out_specs=pl.BlockSpec(memory_space=pltpu.VMEM),
        compiler_params=params(),
        cost_estimate=cost(1, 8 * per * HEAD_DIM * slot),
        name="update_rows",
    )(*pieces)

    far_right = [(i, i + 1) for i in range(n - 1) if i != 1]
    far_left = [(i + 1, i) for i in range(n - 1) if i + 1 != n - 2]
    far = [lax.ppermute(a, "seq", p) for p in (far_right, far_left) for a in (dkf, dvf)]
    dk, dv = pl.pallas_call(
        combine_kernel,
        out_shape=[struct((tile, width), bf16)] * 2,
        in_specs=[smem()] + whole(6),
        out_specs=whole(2),
        compiler_params=params(),
        cost_estimate=cost(6 * tile * width, 20 * tile * width),
        name="key_value_sum",
    )(neighbour, dko, dvo, far[0], far[1], far[2], far[3])

    shape = query_tiles.shape
    return dq.reshape(shape), dk.reshape(shape), dv.reshape(shape), update


def solution(mesh):
    tiles = P("dp", "seq", None, None)
    return jax.shard_map(
        local,
        mesh=mesh,
        in_specs=(tiles, tiles, tiles, tiles, tiles, P("dp", None)),
        out_specs=(tiles, tiles, tiles, P("dp", "seq")),
        check_vma=False,
    )
```

```python
import functools
import math

import jax
import jax.numpy as jnp
from jax import lax
from jax.experimental import pallas as pl
from jax.experimental.pallas import tpu as pltpu
from jax.sharding import PartitionSpec as P

HEAD_DIM = 128
NS_STEPS = 5
SCALE = HEAD_DIM ** (-0.5)
LOG2E = math.log2(math.e)
GROUP = 4
coeff_a = 3.4445
coeff_b = -4.775
coeff_c = 2.0315
f32 = jnp.float32
bf16 = jnp.bfloat16
VMEM_LIMIT = 48 * 1024 * 1024


def whole(count):
    return [pl.BlockSpec(memory_space=pltpu.VMEM)] * count


def smem():
    return pl.BlockSpec(memory_space=pltpu.SMEM)


def params():
    return pltpu.CompilerParams(vmem_limit_bytes=VMEM_LIMIT)


def cost(flops, moved, exps=0):
    return pl.CostEstimate(flops=int(flops), bytes_accessed=int(moved), transcendentals=int(exps))


def dot_t(a, b):
    return lax.dot_general(a, b, (((1,), (1,)), ((), ())), preferred_element_type=f32)


def dot_n(a, b):
    return lax.dot_general(a, b, (((1,), (0,)), ((), ())), preferred_element_type=f32)


def dot_l(a, b):
    return lax.dot_general(a, b, (((0,), (0,)), ((), ())), preferred_element_type=f32)


def exact(a, b, dims=((1,), (0,))):
    return lax.dot_general(
        a, b, (dims, ((), ())), precision=lax.Precision.HIGHEST, preferred_element_type=f32
    )


class Plan:
    def __init__(self, head_count):
        self.seq = lax.axis_size("seq")
        self.dp = lax.axis_size("dp")
        self.per_target = head_count // self.dp
        self.high = self.per_target // 2
        self.col = self.seq // self.per_target
        self.col_bits = self.col.bit_length() - 1
        self.pairs = self.seq // 2

    def row_part(self, place):
        return (place >> (1 + self.col_bits)) * 2 + (place & 1)

    def row_mask(self, part):
        return ((part >> 1) << (1 + self.col_bits)) | (part & 1)

    def col_part(self, place):
        return (place >> 1) & (self.col - 1)


def after(value, *others):
    return lax.optimization_barrier((value, *others))[0]


def shift(value, axis, mask):
    return lax.ppermute(value, axis, [(i, i ^ mask) for i in range(lax.axis_size(axis))])


def head_slice(index):
    return pl.ds(pl.multiple_of(index * HEAD_DIM, HEAD_DIM), HEAD_DIM)


def softmax_keys(query, keys):
    scores = dot_t(keys, query)
    top = jnp.max(scores, axis=0, keepdims=True)
    powers = jnp.exp2((scores - top) * (SCALE * LOG2E))
    return powers * (1.0 / jnp.sum(powers, axis=0, keepdims=True))


def choose_far(near_ref, left, right, far):
    place = lax.axis_index("seq")
    go_left = near_ref[0, place] < place

    @pl.when(go_left)
    def _():
        far[...] = left[...]

    @pl.when(jnp.logical_not(go_left))
    def _():
        far[...] = right[...]


def forward_kernel(plan, near_ref, q, ko, vo, left, right, keep, give, far):
    layer = lax.axis_index("dp")
    choose_far(near_ref, left, right, far)
    mine = plan.row_part(lax.axis_index("seq"))
    jobs = [(j, i) for j in range(plan.per_target) for i in range(plan.dp)]
    for first in range(0, len(jobs), GROUP):
        group = jobs[first : first + GROUP]
        spots = [head_slice((layer ^ i) * plan.per_target + (mine ^ j)) for j, i in group]
        weights = [
            softmax_keys(q[:, at], jnp.concatenate([ko[:, at], far[0, :, at]], 0)).astype(bf16)
            for at in spots
        ]
        for (j, i), at, p in zip(group, spots, weights, strict=True):
            values = jnp.concatenate([vo[:, at], far[1, :, at]], 0)
            out = give if j & 1 else keep
            out[j >> 1, i * HEAD_DIM : (i + 1) * HEAD_DIM, :] = dot_l(values, p).astype(bf16)


def backward_kernel(near_ref, q, ko, vo, left, right, g, dq, dko, dvo, dfar, far):
    choose_far(near_ref, left, right, far)
    tile = q.shape[0]
    count = q.shape[1] // HEAD_DIM
    for first in range(0, count, GROUP):
        spots = [
            slice(h * HEAD_DIM, (h + 1) * HEAD_DIM)
            for h in range(first, min(first + GROUP, count))
        ]
        weights, slopes = [], []
        for at in spots:
            values = jnp.concatenate([vo[:, at], far[1, :, at]], 0)
            keys = jnp.concatenate([ko[:, at], far[0, :, at]], 0)
            weights.append(softmax_keys(q[:, at], keys))
            slopes.append(dot_t(values, g[:, at]))
        for at, p, dp in zip(spots, weights, slopes, strict=True):
            pb = p.astype(bf16)
            delta = jnp.sum(pb.astype(f32) * dp, axis=0, keepdims=True)
            ds = (p * (dp - delta)).astype(bf16)
            keys = jnp.concatenate([ko[:, at], far[0, :, at]], 0)
            dk = dot_n(ds, q[:, at]) * SCALE
            dv = dot_n(pb, g[:, at])
            dq[:, at] = (dot_l(ds, keys) * SCALE).astype(bf16)
            dko[:, at] = dk[:tile]
            dvo[:, at] = dv[:tile]
            dfar[0, :, at] = dk[tile:].astype(bf16)
            dfar[1, :, at] = dv[tile:].astype(bf16)


def combine_kernel(near_ref, dko, dvo, left, right, dk, dv):
    place = lax.axis_index("seq")
    last = lax.axis_size("seq") - 1
    before = near_ref[0, jnp.maximum(place - 1, 0)]
    beyond = near_ref[0, jnp.minimum(place + 1, last)]
    from_left = (place > 0) & (before == place)
    from_right = (place < last) & (beyond == place)
    for which, (own, out) in enumerate(((dko, dk), (dvo, dv))):
        total = own[...] + jnp.where(from_left, left[which].astype(f32), 0.0)
        out[...] = (total + jnp.where(from_right, right[which].astype(f32), 0.0)).astype(bf16)


def product_kernel(plan, spots, *refs):
    att = refs[: plan.pairs]
    cols = refs[plan.pairs : plan.pairs + 2]
    outs = refs[plan.pairs + 2 : plan.pairs + 2 + len(spots)]
    turned = refs[plan.pairs + 2 + len(spots) :]
    for t in range(plan.pairs):
        for core in range(2):
            turned[core][:, t * HEAD_DIM : (t + 1) * HEAD_DIM] = att[t][core]
    tokens = turned[0].shape[1]
    for (i, start, size), out in zip(spots, outs, strict=True):
        rows = slice(i * HEAD_DIM, (i + 1) * HEAD_DIM)
        step = 256 if size % 256 == 0 else size
        for c in range(0, size, step):
            total = None
            for core in range(2):
                block = cols[core][:, :, start + c : start + c + step].reshape(tokens, step)
                part = dot_n(turned[core][rows, :], block)
                total = part if total is None else total + part
            out[:, c : c + step] = total.astype(out.dtype)


def gram_kernel(starts, own, *refs):
    *parts, x, gram = refs
    x[...] = own[...]
    for start, part in zip(starts, parts, strict=True):
        at = slice(start, start + part.shape[1])
        x[:, at] += part[...].astype(f32)
    gram[...] = exact(x[...], x[...], ((1,), (1,)))


def polynomial(gram):
    eye = (
        lax.broadcasted_iota(jnp.int32, gram.shape, 0)
        == lax.broadcasted_iota(jnp.int32, gram.shape, 1)
    ).astype(f32)
    square = jnp.sum(jnp.sum(gram * eye, axis=1, keepdims=True), axis=0, keepdims=True)
    inverse = 1.0 / (jnp.sqrt(square) + 1e-07)
    a = gram * inverse * inverse
    p = None
    for turn in range(NS_STEPS):
        q = coeff_a * eye + coeff_b * a + coeff_c * exact(a, a)
        p = q if p is None else exact(q, p)
        if turn + 1 < NS_STEPS:
            a = exact(exact(q, a), q)
    return p, inverse


def update_kernel(plan, factor, x, gram, gram_other, *outs):
    mine = plan.row_part(lax.axis_index("seq"))
    p, inverse = polynomial(gram[...] + gram_other[...])
    p = p * (inverse * factor)
    width = outs[0].shape[1]
    for j in range(plan.per_target):
        if width % HEAD_DIM == 0:
            block = x[:, pl.ds(pl.multiple_of((mine ^ j) * width, width), width)]
        else:
            block = jnp.zeros((HEAD_DIM, width), f32)
            for r in range(plan.per_target):
                part = x[:, r * width : (r + 1) * width]
                block = jnp.where((mine ^ j) == r, part, block)
        outs[j][...] = exact(p, block).astype(outs[j].dtype)


def place_kernel(plan, *refs):
    *parts, out = refs
    mine = plan.row_part(lax.axis_index("seq"))
    for j, part in enumerate(parts):
        at = pl.ds(pl.multiple_of((mine ^ j) * HEAD_DIM, HEAD_DIM), HEAD_DIM)
        out[at, :] = part[...].astype(f32)


def local(query_tiles, key_tiles, value_tiles, attn_grad, proj_grad, neighbour):
    tile, width = query_tiles.shape[2:]
    depth = proj_grad.shape[3]
    head_count = width // HEAD_DIM
    plan = Plan(head_count)
    n, m, per = plan.seq, plan.dp, plan.per_target
    place = lax.axis_index("seq")
    struct = jax.ShapeDtypeStruct
    query, key, value, grad = (
        a.reshape(tile, width) for a in (query_tiles, key_tiles, value_tiles, attn_grad)
    )

    to_right = [(i, i + 1) for i in range(n - 1) if i + 1 != n - 2]
    to_left = [(i + 1, i) for i in range(n - 1) if i != 1]
    stacked = jnp.stack([key, value])
    left = lax.ppermute(stacked, "seq", to_right)
    right = lax.ppermute(stacked, "seq", to_left)

    slot = depth // n
    flat = proj_grad.reshape(tile, depth)
    mine = plan.col_part(place)
    mine_width = per * slot

    def column_part(part):
        return jnp.concatenate(
            [
                lax.dynamic_slice_in_dim(flat, (high * plan.col + part) * 2 * slot, 2 * slot, 1)
                for high in range(plan.high)
            ],
            1,
        )

    columns = [column_part(mine)] + [
        shift(column_part(mine ^ (t & (plan.col - 1))), "seq", t << 1)
        for t in range(1, plan.pairs)
    ]

    keep, give = pl.pallas_call(
        functools.partial(forward_kernel, plan),
        out_shape=[struct((plan.high, m * HEAD_DIM, tile), bf16)] * 2,
        in_specs=[smem()] + whole(5),
        out_specs=whole(2),
        scratch_shapes=[pltpu.VMEM((2, tile, width), bf16)],
        compiler_params=params(),
        cost_estimate=cost(8 * tile * tile * width, 16 * tile * width, 2 * tile * tile * head_count),
        name="attention_forward",
    )(neighbour, query, key, value, left, right)

    got = shift(give, "seq", 1)
    rows = [jnp.stack([keep[high], got[high]]) for high in range(plan.high)]
    pairs = [rows[0]] + [
        shift(rows[t >> plan.col_bits], "seq", t << 1) for t in range(1, plan.pairs)
    ]
    held = after(jnp.stack(columns), got)
    held_other = shift(held, "seq", 1)

    dq, dko, dvo, dfar = pl.pallas_call(
        backward_kernel,
        out_shape=[
            struct((tile, width), bf16),
            struct((tile, width), f32),
            struct((tile, width), f32),
            struct((2, tile, width), bf16),
        ],
        in_specs=[smem()] + whole(6),
        out_specs=whole(4),
        scratch_shapes=[pltpu.VMEM((2, tile, width), bf16)],
        compiler_params=params(),
        cost_estimate=cost(28 * tile * tile * width, 30 * tile * width, 2 * tile * tile * head_count),
        name="attention_backward",
    )(neighbour, query, key, value, left, right, grad)

    half = mine_width // 2
    spots = [(0, 0, mine_width), (1, 0, mine_width)]
    spots += [(i, start, half) for i in range(2, m) for start in (0, half)]
    blocks = pl.pallas_call(
        functools.partial(product_kernel, plan, spots),
        out_shape=[
            struct((HEAD_DIM, size), bf16 if i & 1 else f32) for i, start, size in spots
        ],
        in_specs=whole(plan.pairs + 2),
        out_specs=whole(len(spots)),
        scratch_shapes=[pltpu.VMEM((m * HEAD_DIM, plan.pairs * tile), bf16)] * 2,
        compiler_params=params(),
        cost_estimate=cost(
            2 * m * HEAD_DIM * n * tile * mine_width, 2 * n * tile * (mine_width + m * HEAD_DIM)
        ),
        name="gradient_product",
    )(after(pairs[0], dq), *pairs[1:], held, held_other)

    total = dict(zip([spot[:2] for spot in spots], blocks, strict=True))
    came = []
    first_step = []
    bit = 1
    while bit < m:
        for i in range(m - 1, 1, -1):
            if i & -i == bit:
                for start in (0, half):
                    part = shift(total[i, start].astype(bf16), "dp", bit)
                    if bit == 1:
                        first_step.append(part)
                    if i == bit:
                        came.append((start, part))
                    else:
                        total[i ^ bit, start] = total[i ^ bit, start] + part.astype(f32)
        bit *= 2
    came.append((0, shift(after(total[1, 0], *first_step), "dp", 1)))

    x, gram = pl.pallas_call(
        functools.partial(gram_kernel, [start for start, part in came]),
        out_shape=[struct((HEAD_DIM, mine_width), f32), struct((HEAD_DIM, HEAD_DIM), f32)],
        in_specs=whole(1 + len(came)),
        out_specs=whole(2),
        compiler_params=params(),
        cost_estimate=cost(12 * HEAD_DIM * HEAD_DIM * mine_width, 14 * HEAD_DIM * mine_width),
        name="gradient_sum",
    )(total[0, 0], *[part for start, part in came])

    gram_other = jnp.zeros_like(gram)
    for b in range(plan.col_bits):
        gram = gram + gram_other
        gram_other = shift(gram, "seq", 2 << b)

    factor = 0.2 * depth**0.5
    pieces = pl.pallas_call(
        functools.partial(update_kernel, plan, factor),
        out_shape=[struct((HEAD_DIM, slot), f32)] + [struct((HEAD_DIM, slot), bf16)] * (per - 1),
        in_specs=whole(3),
        out_specs=whole(per),
        compiler_params=params(),
        cost_estimate=cost(12 * HEAD_DIM * HEAD_DIM * mine_width, 8 * HEAD_DIM * mine_width),
        name="newton_schulz",
    )(x, gram, gram_other)
    pieces = [pieces[0]] + [
        shift(pieces[j], "seq", plan.row_mask(j)) for j in range(1, per)
    ]
    update = pl.pallas_call(
        functools.partial(place_kernel, plan),
        out_shape=struct((per * HEAD_DIM, slot), f32),
        in_specs=whole(per),
        out_specs=pl.BlockSpec(memory_space=pltpu.VMEM),
        compiler_params=params(),
        cost_estimate=cost(1, 8 * per * HEAD_DIM * slot),
        name="update_rows",
    )(*pieces)

    far_right = [(i, i + 1) for i in range(n - 1) if i != 1]
    far_left = [(i + 1, i) for i in range(n - 1) if i + 1 != n - 2]
    dfar = after(dfar, *first_step)
    dk, dv = pl.pallas_call(
        combine_kernel,
        out_shape=[struct((tile, width), bf16)] * 2,
        in_specs=[smem()] + whole(4),
        out_specs=whole(2),
        compiler_params=params(),
        cost_estimate=cost(6 * tile * width, 20 * tile * width),
        name="key_value_sum",
    )(
        neighbour,
        dko,
        dvo,
        lax.ppermute(dfar, "seq", far_right),
        lax.ppermute(dfar, "seq", far_left),
    )

    shape = query_tiles.shape
    return dq.reshape(shape), dk.reshape(shape), dv.reshape(shape), update


def solution(mesh):
    tiles = P("dp", "seq", None, None)
    return jax.shard_map(
        local,
        mesh=mesh,
        in_specs=(tiles, tiles, tiles, tiles, tiles, P("dp", None)),
        out_specs=(tiles, tiles, tiles, P("dp", "seq")),
        check_vma=False,
    )
```

```python
import functools
import math

import jax
import jax.numpy as jnp
from jax import lax
from jax.experimental import pallas as pl
from jax.experimental.pallas import tpu as pltpu
from jax.sharding import PartitionSpec as P

HEAD_DIM = 128
NS_STEPS = 5
SCALE = HEAD_DIM ** (-0.5)
LOG2E = math.log2(math.e)
GROUP = 4
coeff_a = 3.4445
coeff_b = -4.775
coeff_c = 2.0315
f32 = jnp.float32
bf16 = jnp.bfloat16
VMEM_LIMIT = 24 * 1024 * 1024


def whole(count):
    return [pl.BlockSpec(memory_space=pltpu.VMEM)] * count


def smem():
    return pl.BlockSpec(memory_space=pltpu.SMEM)


def params():
    return pltpu.CompilerParams(vmem_limit_bytes=VMEM_LIMIT)


def cost(flops, moved, exps=0):
    return pl.CostEstimate(flops=int(flops), bytes_accessed=int(moved), transcendentals=int(exps))


def dot_t(a, b):
    return lax.dot_general(a, b, (((1,), (1,)), ((), ())), preferred_element_type=f32)


def dot_n(a, b):
    return lax.dot_general(a, b, (((1,), (0,)), ((), ())), preferred_element_type=f32)


def dot_l(a, b):
    return lax.dot_general(a, b, (((0,), (0,)), ((), ())), preferred_element_type=f32)


def exact(a, b, dims=((1,), (0,))):
    return lax.dot_general(
        a, b, (dims, ((), ())), precision=lax.Precision.HIGHEST, preferred_element_type=f32
    )


class Plan:
    def __init__(self, head_count):
        self.seq = lax.axis_size("seq")
        self.dp = lax.axis_size("dp")
        self.per_target = head_count // self.dp
        self.high = self.per_target // 2
        self.col = self.seq // self.per_target
        self.col_bits = self.col.bit_length() - 1
        self.pairs = self.seq // 2

    def row_part(self, place):
        return (place >> (1 + self.col_bits)) * 2 + (place & 1)

    def row_mask(self, part):
        return ((part >> 1) << (1 + self.col_bits)) | (part & 1)

    def col_part(self, place):
        return (place >> 1) & (self.col - 1)


def after(value, *others):
    return lax.optimization_barrier((value, *others))[0]


def shift(value, axis, mask):
    return lax.ppermute(value, axis, [(i, i ^ mask) for i in range(lax.axis_size(axis))])


def head_slice(index):
    return pl.ds(pl.multiple_of(index * HEAD_DIM, HEAD_DIM), HEAD_DIM)


def softmax_keys(query, keys):
    scores = dot_t(keys, query)
    top = jnp.max(scores, axis=0, keepdims=True)
    powers = jnp.exp2((scores - top) * (SCALE * LOG2E))
    return powers * (1.0 / jnp.sum(powers, axis=0, keepdims=True))


def choose_far(near_ref, key_left, value_left, key_right, value_right, far):
    place = lax.axis_index("seq")
    go_left = near_ref[0, place] < place

    @pl.when(go_left)
    def _():
        far[0] = key_left[...]
        far[1] = value_left[...]

    @pl.when(jnp.logical_not(go_left))
    def _():
        far[0] = key_right[...]
        far[1] = value_right[...]


def forward_kernel(plan, near_ref, q, ko, vo, kl, vl, kr, vr, keep, give, far):
    layer = lax.axis_index("dp")
    choose_far(near_ref, kl, vl, kr, vr, far)
    mine = plan.row_part(lax.axis_index("seq"))
    jobs = [(j, i) for j in range(plan.per_target) for i in range(plan.dp)]
    for first in range(0, len(jobs), GROUP):
        group = jobs[first : first + GROUP]
        spots = [head_slice((layer ^ i) * plan.per_target + (mine ^ j)) for j, i in group]
        weights = [
            softmax_keys(q[:, at], jnp.concatenate([ko[:, at], far[0, :, at]], 0)).astype(bf16)
            for at in spots
        ]
        for (j, i), at, p in zip(group, spots, weights, strict=True):
            values = jnp.concatenate([vo[:, at], far[1, :, at]], 0)
            out = give if j & 1 else keep
            out[j >> 1, i * HEAD_DIM : (i + 1) * HEAD_DIM, :] = dot_l(values, p).astype(bf16)


def backward_kernel(near_ref, q, ko, vo, kl, vl, kr, vr, g, dq, dko, dvo, dfar, far):
    choose_far(near_ref, kl, vl, kr, vr, far)
    tile = q.shape[0]
    count = q.shape[1] // HEAD_DIM
    for first in range(0, count, GROUP):
        spots = [
            slice(h * HEAD_DIM, (h + 1) * HEAD_DIM)
            for h in range(first, min(first + GROUP, count))
        ]
        weights, slopes = [], []
        for at in spots:
            values = jnp.concatenate([vo[:, at], far[1, :, at]], 0)
            keys = jnp.concatenate([ko[:, at], far[0, :, at]], 0)
            weights.append(softmax_keys(q[:, at], keys))
            slopes.append(dot_t(values, g[:, at]))
        for at, p, dp in zip(spots, weights, slopes, strict=True):
            pb = p.astype(bf16)
            delta = jnp.sum(pb.astype(f32) * dp, axis=0, keepdims=True)
            ds = (p * (dp - delta)).astype(bf16)
            keys = jnp.concatenate([ko[:, at], far[0, :, at]], 0)
            dk = dot_n(ds, q[:, at]) * SCALE
            dv = dot_n(pb, g[:, at])
            dq[:, at] = (dot_l(ds, keys) * SCALE).astype(bf16)
            dko[:, at] = dk[:tile]
            dvo[:, at] = dv[:tile]
            dfar[0, :, at] = dk[tile:].astype(bf16)
            dfar[1, :, at] = dv[tile:].astype(bf16)


def combine_kernel(near_ref, dko, dvo, left, right, dk, dv):
    place = lax.axis_index("seq")
    last = lax.axis_size("seq") - 1
    before = near_ref[0, jnp.maximum(place - 1, 0)]
    beyond = near_ref[0, jnp.minimum(place + 1, last)]
    from_left = (place > 0) & (before == place)
    from_right = (place < last) & (beyond == place)
    for which, (own, out) in enumerate(((dko, dk), (dvo, dv))):
        total = own[...] + jnp.where(from_left, left[which].astype(f32), 0.0)
        out[...] = (total + jnp.where(from_right, right[which].astype(f32), 0.0)).astype(bf16)


def product_kernel(plan, spots, *refs):
    att = refs[: plan.pairs]
    cols = refs[plan.pairs : plan.pairs + 2]
    outs = refs[plan.pairs + 2 : plan.pairs + 2 + len(spots)]
    turned = refs[plan.pairs + 2 + len(spots) :]
    for t in range(plan.pairs):
        for core in range(2):
            turned[core][:, t * HEAD_DIM : (t + 1) * HEAD_DIM] = att[t][core]
    tokens = turned[0].shape[1]
    for (i, start, size), out in zip(spots, outs, strict=True):
        rows = slice(i * HEAD_DIM, (i + 1) * HEAD_DIM)
        step = 256 if size % 256 == 0 else size
        for c in range(0, size, step):
            total = None
            for core in range(2):
                block = cols[core][:, :, start + c : start + c + step].reshape(tokens, step)
                part = dot_n(turned[core][rows, :], block)
                total = part if total is None else total + part
            out[:, c : c + step] = total.astype(out.dtype)


def gram_kernel(starts, own, *refs):
    *parts, x, gram = refs
    x[...] = own[...]
    for start, part in zip(starts, parts, strict=True):
        at = slice(start, start + part.shape[1])
        x[:, at] += part[...].astype(f32)
    gram[...] = exact(x[...], x[...], ((1,), (1,)))


def polynomial(gram):
    eye = (
        lax.broadcasted_iota(jnp.int32, gram.shape, 0)
        == lax.broadcasted_iota(jnp.int32, gram.shape, 1)
    ).astype(f32)
    square = jnp.sum(jnp.sum(gram * eye, axis=1, keepdims=True), axis=0, keepdims=True)
    inverse = 1.0 / (jnp.sqrt(square) + 1e-07)
    a = gram * inverse * inverse
    p = None
    for turn in range(NS_STEPS):
        q = coeff_a * eye + coeff_b * a + coeff_c * exact(a, a)
        p = q if p is None else exact(q, p)
        if turn + 1 < NS_STEPS:
            a = exact(exact(q, a), q)
    return p, inverse


def update_kernel(plan, factor, x, gram, gram_other, *outs):
    mine = plan.row_part(lax.axis_index("seq"))
    p, inverse = polynomial(gram[...] + gram_other[...])
    p = p * (inverse * factor)
    width = outs[0].shape[1]
    for j in range(plan.per_target):
        if width % HEAD_DIM == 0:
            block = x[:, pl.ds(pl.multiple_of((mine ^ j) * width, width), width)]
        else:
            block = jnp.zeros((HEAD_DIM, width), f32)
            for r in range(plan.per_target):
                part = x[:, r * width : (r + 1) * width]
                block = jnp.where((mine ^ j) == r, part, block)
        outs[j][...] = exact(p, block).astype(outs[j].dtype)


def place_kernel(plan, *refs):
    *parts, out = refs
    mine = plan.row_part(lax.axis_index("seq"))
    for j, part in enumerate(parts):
        at = pl.ds(pl.multiple_of((mine ^ j) * HEAD_DIM, HEAD_DIM), HEAD_DIM)
        out[at, :] = part[...].astype(f32)


def local(query_tiles, key_tiles, value_tiles, attn_grad, proj_grad, neighbour):
    tile, width = query_tiles.shape[2:]
    depth = proj_grad.shape[3]
    head_count = width // HEAD_DIM
    plan = Plan(head_count)
    n, m, per = plan.seq, plan.dp, plan.per_target
    place = lax.axis_index("seq")
    struct = jax.ShapeDtypeStruct
    query, key, value, grad = (
        a.reshape(tile, width) for a in (query_tiles, key_tiles, value_tiles, attn_grad)
    )

    to_right = [(i, i + 1) for i in range(n - 1) if i + 1 != n - 2]
    to_left = [(i + 1, i) for i in range(n - 1) if i != 1]
    key_left = lax.ppermute(key, "seq", to_right)
    key_right = lax.ppermute(key, "seq", to_left)
    value_left = lax.ppermute(value, "seq", to_right)
    value_right = lax.ppermute(value, "seq", to_left)
    beside = (key_left, value_left, key_right, value_right)

    slot = depth // n
    flat = proj_grad.reshape(tile, depth)
    mine = plan.col_part(place)
    mine_width = per * slot

    def column_part(part):
        return jnp.concatenate(
            [
                lax.dynamic_slice_in_dim(flat, (high * plan.col + part) * 2 * slot, 2 * slot, 1)
                for high in range(plan.high)
            ],
            1,
        )

    columns = [column_part(mine)] + [
        shift(after(column_part(mine ^ (t & (plan.col - 1))), key_left, key_right), "seq", t << 1)
        for t in range(1, plan.pairs)
    ]

    keep, give = pl.pallas_call(
        functools.partial(forward_kernel, plan),
        out_shape=[struct((plan.high, m * HEAD_DIM, tile), bf16)] * 2,
        in_specs=[smem()] + whole(7),
        out_specs=whole(2),
        scratch_shapes=[pltpu.VMEM((2, tile, width), bf16)],
        compiler_params=params(),
        cost_estimate=cost(8 * tile * tile * width, 16 * tile * width, 2 * tile * tile * head_count),
        name="attention_forward",
    )(neighbour, query, key, value, *beside)

    got = shift(give, "seq", 1)
    rows = [jnp.stack([keep[high], got[high]]) for high in range(plan.high)]
    pairs = [rows[0]] + [
        shift(rows[t >> plan.col_bits], "seq", t << 1) for t in range(1, plan.pairs)
    ]
    held = after(jnp.stack(columns), got)
    held_other = shift(held, "seq", 1)

    dq, dko, dvo, dfar = pl.pallas_call(
        backward_kernel,
        out_shape=[
            struct((tile, width), bf16),
            struct((tile, width), f32),
            struct((tile, width), f32),
            struct((2, tile, width), bf16),
        ],
        in_specs=[smem()] + whole(8),
        out_specs=whole(4),
        scratch_shapes=[pltpu.VMEM((2, tile, width), bf16)],
        compiler_params=params(),
        cost_estimate=cost(28 * tile * tile * width, 30 * tile * width, 2 * tile * tile * head_count),
        name="attention_backward",
    )(neighbour, query, key, value, *beside, grad)

    half = mine_width // 2
    spots = [(0, 0, mine_width), (1, 0, mine_width)]
    spots += [(i, start, half) for i in range(2, m) for start in (0, half)]
    blocks = pl.pallas_call(
        functools.partial(product_kernel, plan, spots),
        out_shape=[
            struct((HEAD_DIM, size), bf16 if i & 1 else f32) for i, start, size in spots
        ],
        in_specs=whole(plan.pairs + 2),
        out_specs=whole(len(spots)),
        scratch_shapes=[pltpu.VMEM((m * HEAD_DIM, plan.pairs * tile), bf16)] * 2,
        compiler_params=params(),
        cost_estimate=cost(
            2 * m * HEAD_DIM * n * tile * mine_width, 2 * n * tile * (mine_width + m * HEAD_DIM)
        ),
        name="gradient_product",
    )(after(pairs[0], dq), *pairs[1:], held, held_other)

    total = dict(zip([spot[:2] for spot in spots], blocks, strict=True))
    came = []
    first_step = []
    bit = 1
    while bit < m:
        for i in range(m - 1, 1, -1):
            if i & -i == bit:
                for start in (0, half):
                    part = shift(total[i, start].astype(bf16), "dp", bit)
                    if bit == 1:
                        first_step.append(part)
                    if i == bit:
                        came.append((start, part))
                    else:
                        total[i ^ bit, start] = total[i ^ bit, start] + part.astype(f32)
        bit *= 2
    came.append((0, shift(after(total[1, 0], *first_step), "dp", 1)))

    x, gram = pl.pallas_call(
        functools.partial(gram_kernel, [start for start, part in came]),
        out_shape=[struct((HEAD_DIM, mine_width), f32), struct((HEAD_DIM, HEAD_DIM), f32)],
        in_specs=whole(1 + len(came)),
        out_specs=whole(2),
        compiler_params=params(),
        cost_estimate=cost(12 * HEAD_DIM * HEAD_DIM * mine_width, 14 * HEAD_DIM * mine_width),
        name="gradient_sum",
    )(total[0, 0], *[part for start, part in came])

    gram_other = jnp.zeros_like(gram)
    for b in range(plan.col_bits):
        gram = gram + gram_other
        gram_other = shift(gram, "seq", 2 << b)

    factor = 0.2 * depth**0.5
    pieces = pl.pallas_call(
        functools.partial(update_kernel, plan, factor),
        out_shape=[struct((HEAD_DIM, slot), f32)] + [struct((HEAD_DIM, slot), bf16)] * (per - 1),
        in_specs=whole(3),
        out_specs=whole(per),
        compiler_params=params(),
        cost_estimate=cost(12 * HEAD_DIM * HEAD_DIM * mine_width, 8 * HEAD_DIM * mine_width),
        name="newton_schulz",
    )(x, gram, gram_other)
    far_right = [(i, i + 1) for i in range(n - 1) if i != 1]
    far_left = [(i + 1, i) for i in range(n - 1) if i + 1 != n - 2]
    dfar = after(dfar, total[1, 0])
    dk, dv = pl.pallas_call(
        combine_kernel,
        out_shape=[struct((tile, width), bf16)] * 2,
        in_specs=[smem()] + whole(4),
        out_specs=whole(2),
        compiler_params=params(),
        cost_estimate=cost(6 * tile * width, 20 * tile * width),
        name="key_value_sum",
    )(
        neighbour,
        dko,
        dvo,
        lax.ppermute(dfar, "seq", far_right),
        lax.ppermute(dfar, "seq", far_left),
    )

    pieces = [pieces[0]] + [
        shift(pieces[j], "seq", plan.row_mask(j)) for j in range(1, per)
    ]
    update = pl.pallas_call(
        functools.partial(place_kernel, plan),
        out_shape=struct((per * HEAD_DIM, slot), f32),
        in_specs=whole(per),
        out_specs=pl.BlockSpec(memory_space=pltpu.VMEM),
        compiler_params=params(),
        cost_estimate=cost(1, 8 * per * HEAD_DIM * slot),
        name="update_rows",
    )(after(pieces[0], dk), *pieces[1:])

    shape = query_tiles.shape
    return dq.reshape(shape), dk.reshape(shape), dv.reshape(shape), update


def solution(mesh):
    tiles = P("dp", "seq", None, None)
    return jax.shard_map(
        local,
        mesh=mesh,
        in_specs=(tiles, tiles, tiles, tiles, tiles, P("dp", None)),
        out_specs=(tiles, tiles, tiles, P("dp", "seq")),
        check_vma=False,
    )
```

```python
import functools
import math

import jax
import jax.numpy as jnp
from jax import lax
from jax.experimental import pallas as pl
from jax.experimental.pallas import tpu as pltpu
from jax.sharding import PartitionSpec as P

HEAD_DIM = 128
NS_STEPS = 5
SCALE = HEAD_DIM ** (-0.5)
LOG2E = math.log2(math.e)
GROUP = 4
coeff_a = 3.4445
coeff_b = -4.775
coeff_c = 2.0315
f32 = jnp.float32
bf16 = jnp.bfloat16
VMEM_LIMIT = 24 * 1024 * 1024


def whole(count):
    return [pl.BlockSpec(memory_space=pltpu.VMEM)] * count


def smem():
    return pl.BlockSpec(memory_space=pltpu.SMEM)


def params():
    return pltpu.CompilerParams(vmem_limit_bytes=VMEM_LIMIT)


def cost(flops, moved, exps=0):
    return pl.CostEstimate(flops=int(flops), bytes_accessed=int(moved), transcendentals=int(exps))


def dot_t(a, b):
    return lax.dot_general(a, b, (((1,), (1,)), ((), ())), preferred_element_type=f32)


def dot_n(a, b):
    return lax.dot_general(a, b, (((1,), (0,)), ((), ())), preferred_element_type=f32)


def dot_l(a, b):
    return lax.dot_general(a, b, (((0,), (0,)), ((), ())), preferred_element_type=f32)


def exact(a, b, dims=((1,), (0,))):
    return lax.dot_general(
        a, b, (dims, ((), ())), precision=lax.Precision.HIGHEST, preferred_element_type=f32
    )


class Plan:
    def __init__(self, head_count):
        self.seq = lax.axis_size("seq")
        self.dp = lax.axis_size("dp")
        self.per_target = head_count // self.dp
        self.high = self.per_target // 2
        self.col = self.seq // self.per_target
        self.col_bits = self.col.bit_length() - 1
        self.pairs = self.seq // 2

    def row_part(self, place):
        return (place >> (1 + self.col_bits)) * 2 + (place & 1)

    def row_mask(self, part):
        return ((part >> 1) << (1 + self.col_bits)) | (part & 1)

    def col_part(self, place):
        return (place >> 1) & (self.col - 1)


def after(value, *others):
    return lax.optimization_barrier((value, *others))[0]


def shift(value, axis, mask):
    return lax.ppermute(value, axis, [(i, i ^ mask) for i in range(lax.axis_size(axis))])


def head_slice(index):
    return pl.ds(pl.multiple_of(index * HEAD_DIM, HEAD_DIM), HEAD_DIM)


def softmax_keys(query, keys):
    scores = dot_t(keys, query)
    top = jnp.max(scores, axis=0, keepdims=True)
    powers = jnp.exp2((scores - top) * (SCALE * LOG2E))
    return powers * (1.0 / jnp.sum(powers, axis=0, keepdims=True))


def choose_far(near_ref, key_mate, value_mate, key_next, value_next, far):
    place = lax.axis_index("seq")
    is_mate = near_ref[0, place] == (place ^ 1)

    @pl.when(is_mate)
    def _():
        far[0] = key_mate[...]
        far[1] = value_mate[...]

    @pl.when(jnp.logical_not(is_mate))
    def _():
        far[0] = key_next[...]
        far[1] = value_next[...]


def forward_kernel(plan, near_ref, q, ko, vo, km, vm, kn, vn, out, far):
    layer = lax.axis_index("dp")
    choose_far(near_ref, km, vm, kn, vn, far)
    mine = plan.row_part(lax.axis_index("seq"))
    jobs = [(j, i) for j in range(plan.per_target) for i in range(plan.dp)]
    for first in range(0, len(jobs), GROUP):
        group = jobs[first : first + GROUP]
        spots = [head_slice((layer ^ i) * plan.per_target + (mine ^ j)) for j, i in group]
        weights = [
            softmax_keys(q[:, at], jnp.concatenate([ko[:, at], far[0, :, at]], 0)).astype(bf16)
            for at in spots
        ]
        for (j, i), at, p in zip(group, spots, weights, strict=True):
            values = jnp.concatenate([vo[:, at], far[1, :, at]], 0)
            rows = slice(i * HEAD_DIM, (i + 1) * HEAD_DIM)
            out[j >> 1, j & 1, rows, :] = dot_l(values, p).astype(bf16)


def backward_kernel(near_ref, q, ko, vo, km, vm, kn, vn, g, dq, dko, dvo, dfar, far):
    choose_far(near_ref, km, vm, kn, vn, far)
    tile = q.shape[0]
    count = q.shape[1] // HEAD_DIM
    for first in range(0, count, GROUP):
        spots = [
            slice(h * HEAD_DIM, (h + 1) * HEAD_DIM)
            for h in range(first, min(first + GROUP, count))
        ]
        weights, slopes = [], []
        for at in spots:
            values = jnp.concatenate([vo[:, at], far[1, :, at]], 0)
            keys = jnp.concatenate([ko[:, at], far[0, :, at]], 0)
            weights.append(softmax_keys(q[:, at], keys))
            slopes.append(dot_t(values, g[:, at]))
        for at, p, dp in zip(spots, weights, slopes, strict=True):
            pb = p.astype(bf16)
            delta = jnp.sum(pb.astype(f32) * dp, axis=0, keepdims=True)
            ds = (p * (dp - delta)).astype(bf16)
            keys = jnp.concatenate([ko[:, at], far[0, :, at]], 0)
            dk = dot_n(ds, q[:, at]) * SCALE
            dv = dot_n(pb, g[:, at])
            dq[:, at] = (dot_l(ds, keys) * SCALE).astype(bf16)
            dko[:, at] = dk[:tile]
            dvo[:, at] = dv[:tile]
            dfar[0, :, at] = dk[tile:].astype(bf16)
            dfar[1, :, at] = dv[tile:].astype(bf16)


def combine_kernel(near_ref, dko, dvo, mate, beyond, dk, dv):
    place = lax.axis_index("seq")
    last = lax.axis_size("seq") - 1
    other = place + 2 * (place & 1) - 1
    inside = (other >= 0) & (other <= last)
    from_mate = near_ref[0, place ^ 1] == place
    from_other = inside & (near_ref[0, jnp.clip(other, 0, last)] == place)
    for which, (own, out) in enumerate(((dko, dk), (dvo, dv))):
        total = own[...] + jnp.where(from_mate, mate[which].astype(f32), 0.0)
        out[...] = (total + jnp.where(from_other, beyond[which].astype(f32), 0.0)).astype(bf16)


def product_kernel(plan, layers, *refs):
    att = refs[: plan.pairs]
    cols, *outs, for_mate, gathered = refs[plan.pairs :]
    for t in range(plan.pairs):
        at = slice(t * HEAD_DIM, (t + 1) * HEAD_DIM)
        for core in range(2):
            for n, i in enumerate(layers):
                block = att[t][core, i * HEAD_DIM : (i + 1) * HEAD_DIM, :]
                gathered[core, n * HEAD_DIM : (n + 1) * HEAD_DIM, at] = block
    tokens, width = gathered.shape[2], cols.shape[2]
    step = 512 if width % 512 == 0 else width
    for c in range(0, width, step):
        block = cols[:, :, c : c + step].reshape(tokens, step)
        for n, out in enumerate(outs):
            rows = slice(n * HEAD_DIM, (n + 1) * HEAD_DIM)
            out[:, c : c + step] = dot_n(gathered[0, rows, :], block)
            for_mate[n, :, c : c + step] = dot_n(gathered[1, rows, :], block).astype(bf16)


def piece(ref, lead, start, size):
    at = slice(start, start + size)
    return (ref[:, at] if lead is None else ref[lead, :, at]).astype(f32)


def sum_kernel(spots, start, *refs):
    *parts, out = refs
    size = out.shape[1]
    total = None
    for (lead, first), part in zip(spots, parts, strict=True):
        value = piece(part, lead, start - first, size)
        total = value if total is None else total + value
    out[...] = total.astype(bf16)


def gram_kernel(spots, own, *refs):
    *parts, x, gram = refs
    x[...] = own[...]
    for (lead, first), part in zip(spots, parts, strict=True):
        size = part.shape[-1]
        x[:, first : first + size] += piece(part, lead, 0, size)
    gram[...] = exact(x[...], x[...], ((1,), (1,)))


def polynomial(gram):
    eye = (
        lax.broadcasted_iota(jnp.int32, gram.shape, 0)
        == lax.broadcasted_iota(jnp.int32, gram.shape, 1)
    ).astype(f32)
    square = jnp.sum(jnp.sum(gram * eye, axis=1, keepdims=True), axis=0, keepdims=True)
    inverse = 1.0 / (jnp.sqrt(square) + 1e-07)
    a = gram * inverse * inverse
    p = None
    for turn in range(NS_STEPS):
        q = coeff_a * eye + coeff_b * a + coeff_c * exact(a, a)
        p = q if p is None else exact(q, p)
        if turn + 1 < NS_STEPS:
            a = exact(exact(q, a), q)
    return p, inverse


def update_kernel(plan, factor, x, gram, gram_other, *outs):
    mine = plan.row_part(lax.axis_index("seq"))
    p, inverse = polynomial(gram[...] + gram_other[...])
    p = p * (inverse * factor)
    width = outs[0].shape[1]
    for j in range(plan.per_target):
        if width % HEAD_DIM == 0:
            block = x[:, pl.ds(pl.multiple_of((mine ^ j) * width, width), width)]
        else:
            block = jnp.zeros((HEAD_DIM, width), f32)
            for r in range(plan.per_target):
                part = x[:, r * width : (r + 1) * width]
                block = jnp.where((mine ^ j) == r, part, block)
        outs[j][...] = exact(p, block).astype(outs[j].dtype)


def place_kernel(plan, *refs):
    *parts, out = refs
    mine = plan.row_part(lax.axis_index("seq"))
    for j, part in enumerate(parts):
        at = pl.ds(pl.multiple_of((mine ^ j) * HEAD_DIM, HEAD_DIM), HEAD_DIM)
        out[at, :] = part[...].astype(f32)


def local(query_tiles, key_tiles, value_tiles, attn_grad, proj_grad, neighbour):
    tile, width = query_tiles.shape[2:]
    depth = proj_grad.shape[3]
    head_count = width // HEAD_DIM
    plan = Plan(head_count)
    n, m, per = plan.seq, plan.dp, plan.per_target
    place = lax.axis_index("seq")
    struct = jax.ShapeDtypeStruct
    query, key, value, grad = (
        a.reshape(tile, width) for a in (query_tiles, key_tiles, value_tiles, attn_grad)
    )

    steps = [(i, i + 1) for i in range(1, n - 1, 2)]
    back = [(j, i) for i, j in steps]
    takes = [(i, j) for i, j in steps if j != n - 2] + [(j, i) for j, i in back if i != 1]
    gives = [(i, j) for i, j in steps if i != 1] + [(j, i) for j, i in back if j != n - 2]
    key_next = lax.ppermute(key, "seq", takes)
    value_next = lax.ppermute(value, "seq", takes)
    key_mate = shift(key, "seq", 1)
    value_mate = shift(value, "seq", 1)
    beside = (key_mate, value_mate, key_next, value_next)

    slot = depth // n
    flat = proj_grad.reshape(tile, depth)
    mine = plan.col_part(place)
    mine_width = per * slot

    def column_part(part):
        return jnp.concatenate(
            [
                lax.dynamic_slice_in_dim(flat, (high * plan.col + part) * 2 * slot, 2 * slot, 1)
                for high in range(plan.high)
            ],
            1,
        )

    own_columns = column_part(mine)
    columns = [own_columns] + [
        shift(after(column_part(mine ^ q), key_next, key_mate), "seq", q << 1)
        for q in range(1, plan.col)
    ]
    high_columns = [
        shift(after(own_columns, key_next, key_mate), "seq", high << (1 + plan.col_bits))
        for high in range(1, plan.high)
    ]

    attended = pl.pallas_call(
        functools.partial(forward_kernel, plan),
        out_shape=struct((plan.high, 2, m * HEAD_DIM, tile), bf16),
        in_specs=[smem()] + whole(7),
        out_specs=pl.BlockSpec(memory_space=pltpu.VMEM),
        scratch_shapes=[pltpu.VMEM((2, tile, width), bf16)],
        compiler_params=params(),
        cost_estimate=cost(8 * tile * tile * width, 16 * tile * width, 2 * tile * tile * head_count),
        name="attention_forward",
    )(neighbour, query, key, value, *beside)

    pairs = [attended[0]] + [
        shift(attended[t >> plan.col_bits], "seq", t << 1) for t in range(1, plan.pairs)
    ]
    through = after(jnp.stack(columns[1:]), attended)
    held = [jnp.stack(columns)]
    for high in range(1, plan.high):
        rest = shift(through, "seq", high << (1 + plan.col_bits))
        held.append(jnp.concatenate([high_columns[high - 1][None], rest], 0))
    held = jnp.concatenate(held, 0)

    dq, dko, dvo, dfar = pl.pallas_call(
        backward_kernel,
        out_shape=[
            struct((tile, width), bf16),
            struct((tile, width), f32),
            struct((tile, width), f32),
            struct((2, tile, width), bf16),
        ],
        in_specs=[smem()] + whole(8),
        out_specs=whole(4),
        scratch_shapes=[pltpu.VMEM((2, tile, width), bf16)],
        compiler_params=params(),
        cost_estimate=cost(28 * tile * tile * width, 30 * tile * width, 2 * tile * tile * head_count),
        name="attention_backward",
    )(neighbour, query, key, value, *beside, after(grad, attended))

    def product(name, layers, *operands):
        *blocks, for_mate = pl.pallas_call(
            functools.partial(product_kernel, plan, layers),
            out_shape=[struct((HEAD_DIM, mine_width), f32)] * len(layers)
            + [struct((len(layers), HEAD_DIM, mine_width), bf16)],
            in_specs=whole(plan.pairs + 1),
            out_specs=whole(len(layers) + 1),
            scratch_shapes=[pltpu.VMEM((2, len(layers) * HEAD_DIM, plan.pairs * tile), bf16)],
            compiler_params=params(),
            cost_estimate=cost(
                2 * len(layers) * HEAD_DIM * n * tile * mine_width, n * tile * mine_width
            ),
            name=name,
        )(*operands)
        mate = shift(for_mate, "seq", 1)
        return {i: [(block, None, 0), (mate, k, 0)] for k, (i, block) in enumerate(zip(layers, blocks))}

    def added(parts, start, size):
        return pl.pallas_call(
            functools.partial(sum_kernel, [spot for _, *spot in parts], start),
            out_shape=struct((HEAD_DIM, size), bf16),
            in_specs=whole(len(parts)),
            out_specs=pl.BlockSpec(memory_space=pltpu.VMEM),
            compiler_params=params(),
            cost_estimate=cost(len(parts) * HEAD_DIM * size, 4 * len(parts) * HEAD_DIM * size),
            name="block_sum",
        )(*[array for array, *_ in parts])

    leading = [i for i in range(m - 1, 1, -1) if i & 1]
    blocks = product("product_first", leading, after(pairs[0], dq), *pairs[1:], held)
    first_block = blocks[leading[0]][0][0]
    blocks |= product(
        "product_rest",
        [i for i in range(m) if i not in leading],
        after(pairs[0], first_block),
        *pairs[1:],
        held,
    )

    half = mine_width // 2
    first_step = []
    extra = {(i, start): [] for i in range(m) for start in (0, half)}
    bit = 1
    while bit < m:
        for i in range(m - 1, 1, -1):
            if i & -i == bit:
                for start in (0, half):
                    part = shift(added(blocks[i] + extra[i, start], start, half), "dp", bit)
                    if bit == 1:
                        first_step.append(part)
                    extra[i ^ bit, start].append((part, None, start))
        bit *= 2
    near = shift(after(added(blocks[1], 0, mine_width), *first_step), "dp", 1)
    own = blocks[0][0][0]
    came = [blocks[0][1], (near, None, 0)] + extra[0, 0] + extra[0, half]

    x, gram = pl.pallas_call(
        functools.partial(gram_kernel, [spot for _, *spot in came]),
        out_shape=[struct((HEAD_DIM, mine_width), f32), struct((HEAD_DIM, HEAD_DIM), f32)],
        in_specs=whole(1 + len(came)),
        out_specs=whole(2),
        compiler_params=params(),
        cost_estimate=cost(12 * HEAD_DIM * HEAD_DIM * mine_width, 14 * HEAD_DIM * mine_width),
        name="gradient_sum",
    )(own, *[array for array, *_ in came])

    gram_other = jnp.zeros_like(gram)
    for b in range(plan.col_bits):
        gram = gram + gram_other
        gram_other = shift(gram, "seq", 2 << b)

    factor = 0.2 * depth**0.5
    pieces = pl.pallas_call(
        functools.partial(update_kernel, plan, factor),
        out_shape=[struct((HEAD_DIM, slot), f32)] + [struct((HEAD_DIM, slot), bf16)] * (per - 1),
        in_specs=whole(3),
        out_specs=whole(per),
        compiler_params=params(),
        cost_estimate=cost(12 * HEAD_DIM * HEAD_DIM * mine_width, 8 * HEAD_DIM * mine_width),
        name="newton_schulz",
    )(x, gram, gram_other)
    dfar = after(dfar, own)
    dk, dv = pl.pallas_call(
        combine_kernel,
        out_shape=[struct((tile, width), bf16)] * 2,
        in_specs=[smem()] + whole(4),
        out_specs=whole(2),
        compiler_params=params(),
        cost_estimate=cost(6 * tile * width, 20 * tile * width),
        name="key_value_sum",
    )(
        neighbour,
        dko,
        dvo,
        shift(dfar, "seq", 1),
        lax.ppermute(dfar, "seq", gives),
    )

    pieces = [pieces[0]] + [
        shift(pieces[j], "seq", plan.row_mask(j)) for j in range(1, per)
    ]
    update = pl.pallas_call(
        functools.partial(place_kernel, plan),
        out_shape=struct((per * HEAD_DIM, slot), f32),
        in_specs=whole(per),
        out_specs=pl.BlockSpec(memory_space=pltpu.VMEM),
        compiler_params=params(),
        cost_estimate=cost(1, 8 * per * HEAD_DIM * slot),
        name="update_rows",
    )(after(pieces[0], dk), *pieces[1:])

    shape = query_tiles.shape
    return dq.reshape(shape), dk.reshape(shape), dv.reshape(shape), update


def solution(mesh):
    tiles = P("dp", "seq", None, None)
    return jax.shard_map(
        local,
        mesh=mesh,
        in_specs=(tiles, tiles, tiles, tiles, tiles, P("dp", None)),
        out_specs=(tiles, tiles, tiles, P("dp", "seq")),
        check_vma=False,
    )
```

```python
import functools
import math

import jax
import jax.numpy as jnp
from jax import lax
from jax.experimental import pallas as pl
from jax.experimental.pallas import tpu as pltpu
from jax.sharding import PartitionSpec as P

HEAD_DIM = 128
NS_STEPS = 5
SCALE = HEAD_DIM ** (-0.5)
LOG2E = math.log2(math.e)
GROUP = 4
coeff_a = 3.4445
coeff_b = -4.775
coeff_c = 2.0315
f32 = jnp.float32
bf16 = jnp.bfloat16
VMEM_LIMIT = 24 * 1024 * 1024


def whole(count):
    return [pl.BlockSpec(memory_space=pltpu.VMEM)] * count


def smem():
    return pl.BlockSpec(memory_space=pltpu.SMEM)


def params():
    return pltpu.CompilerParams(vmem_limit_bytes=VMEM_LIMIT)


def cost(flops, moved, exps=0):
    return pl.CostEstimate(flops=int(flops), bytes_accessed=int(moved), transcendentals=int(exps))


def dot_t(a, b):
    return lax.dot_general(a, b, (((1,), (1,)), ((), ())), preferred_element_type=f32)


def dot_n(a, b):
    return lax.dot_general(a, b, (((1,), (0,)), ((), ())), preferred_element_type=f32)


def dot_l(a, b):
    return lax.dot_general(a, b, (((0,), (0,)), ((), ())), preferred_element_type=f32)


def exact(a, b, dims=((1,), (0,))):
    return lax.dot_general(
        a, b, (dims, ((), ())), precision=lax.Precision.HIGHEST, preferred_element_type=f32
    )


class Plan:
    def __init__(self, head_count):
        self.seq = lax.axis_size("seq")
        self.dp = lax.axis_size("dp")
        self.per_target = head_count // self.dp
        self.high = self.per_target // 2
        self.col = self.seq // self.per_target
        self.col_bits = self.col.bit_length() - 1
        self.pairs = self.seq // 2

    def row_part(self, place):
        return (place >> (1 + self.col_bits)) * 2 + (place & 1)

    def row_mask(self, part):
        return ((part >> 1) << (1 + self.col_bits)) | (part & 1)

    def col_part(self, place):
        return (place >> 1) & (self.col - 1)


def after(value, *others):
    return lax.optimization_barrier((value, *others))[0]


def shift(value, axis, mask):
    return lax.ppermute(value, axis, [(i, i ^ mask) for i in range(lax.axis_size(axis))])


def head_slice(index):
    return pl.ds(pl.multiple_of(index * HEAD_DIM, HEAD_DIM), HEAD_DIM)


def softmax_keys(query, keys):
    scores = dot_t(keys, query)
    top = jnp.max(scores, axis=0, keepdims=True)
    powers = jnp.exp2((scores - top) * (SCALE * LOG2E))
    return powers * (1.0 / jnp.sum(powers, axis=0, keepdims=True))


def choose_far(near_ref, key_mate, value_mate, key_next, value_next, far):
    place = lax.axis_index("seq")
    is_mate = near_ref[0, place] == (place ^ 1)

    @pl.when(is_mate)
    def _():
        far[0] = key_mate[...]
        far[1] = value_mate[...]

    @pl.when(jnp.logical_not(is_mate))
    def _():
        far[0] = key_next[...]
        far[1] = value_next[...]


def forward_kernel(plan, near_ref, q, ko, vo, km, vm, kn, vn, out, far):
    layer = lax.axis_index("dp")
    choose_far(near_ref, km, vm, kn, vn, far)
    mine = plan.row_part(lax.axis_index("seq"))
    jobs = [(j, i) for j in range(plan.per_target) for i in range(plan.dp)]
    for first in range(0, len(jobs), GROUP):
        group = jobs[first : first + GROUP]
        spots = [head_slice((layer ^ i) * plan.per_target + (mine ^ j)) for j, i in group]
        weights = [
            softmax_keys(q[:, at], jnp.concatenate([ko[:, at], far[0, :, at]], 0)).astype(bf16)
            for at in spots
        ]
        for (j, i), at, p in zip(group, spots, weights, strict=True):
            values = jnp.concatenate([vo[:, at], far[1, :, at]], 0)
            rows = slice(i * HEAD_DIM, (i + 1) * HEAD_DIM)
            out[j >> 1, j & 1, rows, :] = dot_l(values, p).astype(bf16)


def backward_kernel(near_ref, q, ko, vo, km, vm, kn, vn, g, dq, dko, dvo, dfar, far):
    choose_far(near_ref, km, vm, kn, vn, far)
    tile = q.shape[0]
    count = q.shape[1] // HEAD_DIM
    for first in range(0, count, GROUP):
        spots = [
            slice(h * HEAD_DIM, (h + 1) * HEAD_DIM)
            for h in range(first, min(first + GROUP, count))
        ]
        weights, slopes = [], []
        for at in spots:
            values = jnp.concatenate([vo[:, at], far[1, :, at]], 0)
            keys = jnp.concatenate([ko[:, at], far[0, :, at]], 0)
            weights.append(softmax_keys(q[:, at], keys))
            slopes.append(dot_t(values, g[:, at]))
        for at, p, dp in zip(spots, weights, slopes, strict=True):
            pb = p.astype(bf16)
            delta = jnp.sum(pb.astype(f32) * dp, axis=0, keepdims=True)
            ds = (p * (dp - delta)).astype(bf16)
            keys = jnp.concatenate([ko[:, at], far[0, :, at]], 0)
            dk = dot_n(ds, q[:, at]) * SCALE
            dv = dot_n(pb, g[:, at])
            dq[:, at] = (dot_l(ds, keys) * SCALE).astype(bf16)
            dko[:, at] = dk[:tile]
            dvo[:, at] = dv[:tile]
            dfar[0, :, at] = dk[tile:].astype(bf16)
            dfar[1, :, at] = dv[tile:].astype(bf16)


def combine_kernel(near_ref, dko, dvo, mate, beyond, dk, dv):
    place = lax.axis_index("seq")
    last = lax.axis_size("seq") - 1
    other = place + 2 * (place & 1) - 1
    inside = (other >= 0) & (other <= last)
    from_mate = near_ref[0, place ^ 1] == place
    from_other = inside & (near_ref[0, jnp.clip(other, 0, last)] == place)
    for which, (own, out) in enumerate(((dko, dk), (dvo, dv))):
        total = own[...] + jnp.where(from_mate, mate[which].astype(f32), 0.0)
        out[...] = (total + jnp.where(from_other, beyond[which].astype(f32), 0.0)).astype(bf16)


def product_kernel(plan, layers, *refs):
    att = refs[: plan.pairs]
    cols, *outs, for_mate, gathered = refs[plan.pairs :]
    for t in range(plan.pairs):
        at = slice(t * HEAD_DIM, (t + 1) * HEAD_DIM)
        for core in range(2):
            for n, i in enumerate(layers):
                block = att[t][core, i * HEAD_DIM : (i + 1) * HEAD_DIM, :]
                gathered[core, n * HEAD_DIM : (n + 1) * HEAD_DIM, at] = block
    tokens, width = gathered.shape[2], cols.shape[2]
    step = 512 if width % 512 == 0 else width
    for c in range(0, width, step):
        block = cols[:, :, c : c + step].reshape(tokens, step)
        for n, out in enumerate(outs):
            rows = slice(n * HEAD_DIM, (n + 1) * HEAD_DIM)
            out[:, c : c + step] = dot_n(gathered[0, rows, :], block)
            for_mate[n, :, c : c + step] = dot_n(gathered[1, rows, :], block).astype(bf16)


def piece(ref, lead, start, size):
    at = slice(start, start + size)
    return (ref[:, at] if lead is None else ref[lead, :, at]).astype(f32)


def sum_kernel(spots, start, *refs):
    *parts, out = refs
    size = out.shape[1]
    total = None
    for (lead, first), part in zip(spots, parts, strict=True):
        value = piece(part, lead, start - first, size)
        total = value if total is None else total + value
    out[...] = total.astype(bf16)


def gram_kernel(spots, own, *refs):
    *parts, x, gram = refs
    x[...] = own[...]
    for (lead, first), part in zip(spots, parts, strict=True):
        size = part.shape[-1]
        x[:, first : first + size] += piece(part, lead, 0, size)
    gram[...] = exact(x[...], x[...], ((1,), (1,)))


def polynomial(gram):
    eye = (
        lax.broadcasted_iota(jnp.int32, gram.shape, 0)
        == lax.broadcasted_iota(jnp.int32, gram.shape, 1)
    ).astype(f32)
    square = jnp.sum(jnp.sum(gram * eye, axis=1, keepdims=True), axis=0, keepdims=True)
    inverse = 1.0 / (jnp.sqrt(square) + 1e-07)
    a = gram * inverse * inverse
    p = None
    for turn in range(NS_STEPS):
        q = coeff_a * eye + coeff_b * a + coeff_c * exact(a, a)
        p = q if p is None else exact(q, p)
        if turn + 1 < NS_STEPS:
            a = exact(exact(q, a), q)
    return p, inverse


def update_kernel(plan, factor, x, gram, gram_other, *outs):
    mine = plan.row_part(lax.axis_index("seq"))
    p, inverse = polynomial(gram[...] + gram_other[...])
    p = p * (inverse * factor)
    width = outs[0].shape[1]
    for j in range(plan.per_target):
        if width % HEAD_DIM == 0:
            block = x[:, pl.ds(pl.multiple_of((mine ^ j) * width, width), width)]
        else:
            block = jnp.zeros((HEAD_DIM, width), f32)
            for r in range(plan.per_target):
                part = x[:, r * width : (r + 1) * width]
                block = jnp.where((mine ^ j) == r, part, block)
        outs[j][...] = exact(p, block).astype(outs[j].dtype)


def place_kernel(plan, *refs):
    *parts, out = refs
    mine = plan.row_part(lax.axis_index("seq"))
    for j, part in enumerate(parts):
        at = pl.ds(pl.multiple_of((mine ^ j) * HEAD_DIM, HEAD_DIM), HEAD_DIM)
        out[at, :] = part[...].astype(f32)


def local(query_tiles, key_tiles, value_tiles, attn_grad, proj_grad, neighbour):
    tile, width = query_tiles.shape[2:]
    depth = proj_grad.shape[3]
    head_count = width // HEAD_DIM
    plan = Plan(head_count)
    n, m, per = plan.seq, plan.dp, plan.per_target
    place = lax.axis_index("seq")
    struct = jax.ShapeDtypeStruct
    query, key, value, grad = (
        a.reshape(tile, width) for a in (query_tiles, key_tiles, value_tiles, attn_grad)
    )

    steps = [(i, i + 1) for i in range(1, n - 1, 2)]
    back = [(j, i) for i, j in steps]
    takes = [(i, j) for i, j in steps if j != n - 2] + [(j, i) for j, i in back if i != 1]
    gives = [(i, j) for i, j in steps if i != 1] + [(j, i) for j, i in back if j != n - 2]
    key_next = lax.ppermute(key, "seq", takes)
    value_next = lax.ppermute(value, "seq", takes)
    key_mate = shift(key, "seq", 1)
    value_mate = shift(value, "seq", 1)
    beside = (key_mate, value_mate, key_next, value_next)

    slot = depth // n
    flat = proj_grad.reshape(tile, depth)
    mine = plan.col_part(place)
    mine_width = per * slot

    def column_part(part):
        return jnp.concatenate(
            [
                lax.dynamic_slice_in_dim(flat, (high * plan.col + part) * 2 * slot, 2 * slot, 1)
                for high in range(plan.high)
            ],
            1,
        )

    own_columns = column_part(mine)
    columns = [own_columns] + [
        shift(column_part(mine ^ q), "seq", q << 1)
        for q in range(1, plan.col)
    ]
    high_columns = [
        shift(after(own_columns, key_next, key_mate), "seq", high << (1 + plan.col_bits))
        for high in range(1, plan.high)
    ]

    attended = pl.pallas_call(
        functools.partial(forward_kernel, plan),
        out_shape=struct((plan.high, 2, m * HEAD_DIM, tile), bf16),
        in_specs=[smem()] + whole(7),
        out_specs=pl.BlockSpec(memory_space=pltpu.VMEM),
        scratch_shapes=[pltpu.VMEM((2, tile, width), bf16)],
        compiler_params=params(),
        cost_estimate=cost(8 * tile * tile * width, 16 * tile * width, 2 * tile * tile * head_count),
        name="attention_forward",
    )(neighbour, query, key, value, *beside)

    pairs = [attended[0]] + [shift(attended[0], "seq", q << 1) for q in range(1, plan.col)]
    for high in range(1, plan.high):
        came_high = shift(attended[high], "seq", high << (1 + plan.col_bits))
        pairs.append(came_high)
        pairs += [shift(came_high, "seq", q << 1) for q in range(1, plan.col)]
    through = after(jnp.stack(columns[1:]), attended)
    held = [jnp.stack(columns)]
    for high in range(1, plan.high):
        rest = shift(through, "seq", high << (1 + plan.col_bits))
        held.append(jnp.concatenate([high_columns[high - 1][None], rest], 0))
    held = jnp.concatenate(held, 0)

    dq, dko, dvo, dfar = pl.pallas_call(
        backward_kernel,
        out_shape=[
            struct((tile, width), bf16),
            struct((tile, width), f32),
            struct((tile, width), f32),
            struct((2, tile, width), bf16),
        ],
        in_specs=[smem()] + whole(8),
        out_specs=whole(4),
        scratch_shapes=[pltpu.VMEM((2, tile, width), bf16)],
        compiler_params=params(),
        cost_estimate=cost(28 * tile * tile * width, 30 * tile * width, 2 * tile * tile * head_count),
        name="attention_backward",
    )(neighbour, query, key, value, *beside, after(grad, attended))

    def product(name, layers, *operands):
        *blocks, for_mate = pl.pallas_call(
            functools.partial(product_kernel, plan, layers),
            out_shape=[struct((HEAD_DIM, mine_width), f32)] * len(layers)
            + [struct((len(layers), HEAD_DIM, mine_width), bf16)],
            in_specs=whole(plan.pairs + 1),
            out_specs=whole(len(layers) + 1),
            scratch_shapes=[pltpu.VMEM((2, len(layers) * HEAD_DIM, plan.pairs * tile), bf16)],
            compiler_params=params(),
            cost_estimate=cost(
                2 * len(layers) * HEAD_DIM * n * tile * mine_width, n * tile * mine_width
            ),
            name=name,
        )(*operands)
        mate = shift(for_mate, "seq", 1)
        return {i: [(block, None, 0), (mate, k, 0)] for k, (i, block) in enumerate(zip(layers, blocks))}

    def added(parts, start, size):
        return pl.pallas_call(
            functools.partial(sum_kernel, [spot for _, *spot in parts], start),
            out_shape=struct((HEAD_DIM, size), bf16),
            in_specs=whole(len(parts)),
            out_specs=pl.BlockSpec(memory_space=pltpu.VMEM),
            compiler_params=params(),
            cost_estimate=cost(len(parts) * HEAD_DIM * size, 4 * len(parts) * HEAD_DIM * size),
            name="block_sum",
        )(*[array for array, *_ in parts])

    leading = [i for i in range(m - 1, 1, -1) if i & 1]
    blocks = product("product_first", leading, after(pairs[0], dq), *pairs[1:], held)
    first_block = blocks[leading[0]][0][0]
    blocks |= product(
        "product_rest",
        [i for i in range(m) if i not in leading],
        after(pairs[0], first_block),
        *pairs[1:],
        held,
    )

    extra = {i: [] for i in range(m)}
    sent = []
    bit = 1
    while bit < m:
        for i in range(m - 1, 1, -1):
            if i & -i == bit:
                sent.append(added(blocks[i] + extra[i], 0, mine_width))
                extra[i ^ bit].append((shift(sent[-1], "dp", bit), None, 0))
        bit *= 2
    near = shift(after(added(blocks[1], 0, mine_width), sent[-1]), "dp", 1)
    own = blocks[0][0][0]
    came = [blocks[0][1], (near, None, 0)] + extra[0]

    x, gram = pl.pallas_call(
        functools.partial(gram_kernel, [spot for _, *spot in came]),
        out_shape=[struct((HEAD_DIM, mine_width), f32), struct((HEAD_DIM, HEAD_DIM), f32)],
        in_specs=whole(1 + len(came)),
        out_specs=whole(2),
        compiler_params=params(),
        cost_estimate=cost(12 * HEAD_DIM * HEAD_DIM * mine_width, 14 * HEAD_DIM * mine_width),
        name="gradient_sum",
    )(own, *[array for array, *_ in came])

    gram_other = jnp.zeros_like(gram)
    for b in range(plan.col_bits):
        gram = gram + gram_other
        gram_other = shift(gram, "seq", 2 << b)

    factor = 0.2 * depth**0.5
    pieces = pl.pallas_call(
        functools.partial(update_kernel, plan, factor),
        out_shape=[struct((HEAD_DIM, slot), f32)] + [struct((HEAD_DIM, slot), bf16)] * (per - 1),
        in_specs=whole(3),
        out_specs=whole(per),
        compiler_params=params(),
        cost_estimate=cost(12 * HEAD_DIM * HEAD_DIM * mine_width, 8 * HEAD_DIM * mine_width),
        name="newton_schulz",
    )(x, gram, gram_other)
    dfar = after(dfar, own)
    dk, dv = pl.pallas_call(
        combine_kernel,
        out_shape=[struct((tile, width), bf16)] * 2,
        in_specs=[smem()] + whole(4),
        out_specs=whole(2),
        compiler_params=params(),
        cost_estimate=cost(6 * tile * width, 20 * tile * width),
        name="key_value_sum",
    )(
        neighbour,
        dko,
        dvo,
        shift(dfar, "seq", 1),
        lax.ppermute(dfar, "seq", gives),
    )

    pieces = [pieces[0]] + [
        shift(pieces[j], "seq", plan.row_mask(j)) for j in range(1, per)
    ]
    update = pl.pallas_call(
        functools.partial(place_kernel, plan),
        out_shape=struct((per * HEAD_DIM, slot), f32),
        in_specs=whole(per),
        out_specs=pl.BlockSpec(memory_space=pltpu.VMEM),
        compiler_params=params(),
        cost_estimate=cost(1, 8 * per * HEAD_DIM * slot),
        name="update_rows",
    )(after(pieces[0], dk), *pieces[1:])

    shape = query_tiles.shape
    return dq.reshape(shape), dk.reshape(shape), dv.reshape(shape), update


def solution(mesh):
    tiles = P("dp", "seq", None, None)
    return jax.shard_map(
        local,
        mesh=mesh,
        in_specs=(tiles, tiles, tiles, tiles, tiles, P("dp", None)),
        out_specs=(tiles, tiles, tiles, P("dp", "seq")),
        check_vma=False,
    )
```

```python
import functools
import math

import jax
import jax.numpy as jnp
from jax import lax
from jax.experimental import pallas as pl
from jax.experimental.pallas import tpu as pltpu
from jax.sharding import PartitionSpec as P

HEAD_DIM = 128
NS_STEPS = 5
SCALE = HEAD_DIM ** (-0.5)
LOG2E = math.log2(math.e)
GROUP = 4
coeff_a = 3.4445
coeff_b = -4.775
coeff_c = 2.0315
f32 = jnp.float32
bf16 = jnp.bfloat16
VMEM_LIMIT = 24 * 1024 * 1024


def whole(count):
    return [pl.BlockSpec(memory_space=pltpu.VMEM)] * count


def smem():
    return pl.BlockSpec(memory_space=pltpu.SMEM)


def params():
    return pltpu.CompilerParams(vmem_limit_bytes=VMEM_LIMIT)


def cost(flops, moved, exps=0):
    return pl.CostEstimate(flops=int(flops), bytes_accessed=int(moved), transcendentals=int(exps))


def dot_t(a, b):
    return lax.dot_general(a, b, (((1,), (1,)), ((), ())), preferred_element_type=f32)


def dot_n(a, b):
    return lax.dot_general(a, b, (((1,), (0,)), ((), ())), preferred_element_type=f32)


def dot_l(a, b):
    return lax.dot_general(a, b, (((0,), (0,)), ((), ())), preferred_element_type=f32)


def exact(a, b, dims=((1,), (0,))):
    return lax.dot_general(
        a, b, (dims, ((), ())), precision=lax.Precision.HIGHEST, preferred_element_type=f32
    )


class Plan:
    def __init__(self, head_count):
        self.seq = lax.axis_size("seq")
        self.dp = lax.axis_size("dp")
        self.per_target = head_count // self.dp
        self.high = self.per_target // 2
        self.col = self.seq // self.per_target
        self.col_bits = self.col.bit_length() - 1
        self.pairs = self.seq // 2

    def row_part(self, place):
        return (place >> (1 + self.col_bits)) * 2 + (place & 1)

    def row_mask(self, part):
        return ((part >> 1) << (1 + self.col_bits)) | (part & 1)

    def col_part(self, place):
        return (place >> 1) & (self.col - 1)


def after(value, *others):
    return lax.optimization_barrier((value, *others))[0]


def shift(value, axis, mask):
    return lax.ppermute(value, axis, [(i, i ^ mask) for i in range(lax.axis_size(axis))])


def head_slice(index):
    return pl.ds(pl.multiple_of(index * HEAD_DIM, HEAD_DIM), HEAD_DIM)


def softmax_keys(query, keys):
    scores = dot_t(keys, query)
    top = jnp.max(scores, axis=0, keepdims=True)
    powers = jnp.exp2((scores - top) * (SCALE * LOG2E))
    return powers * (1.0 / jnp.sum(powers, axis=0, keepdims=True))


def choose_far(near_ref, key_mate, value_mate, key_next, value_next, far):
    place = lax.axis_index("seq")
    is_mate = near_ref[0, place] == (place ^ 1)

    @pl.when(is_mate)
    def _():
        far[0] = key_mate[...]
        far[1] = value_mate[...]

    @pl.when(jnp.logical_not(is_mate))
    def _():
        far[0] = key_next[...]
        far[1] = value_next[...]


def forward_kernel(plan, near_ref, q, ko, vo, km, vm, kn, vn, out, far):
    layer = lax.axis_index("dp")
    choose_far(near_ref, km, vm, kn, vn, far)
    mine = plan.row_part(lax.axis_index("seq"))
    jobs = [(j, i) for j in range(plan.per_target) for i in range(plan.dp)]
    for first in range(0, len(jobs), GROUP):
        group = jobs[first : first + GROUP]
        spots = [head_slice((layer ^ i) * plan.per_target + (mine ^ j)) for j, i in group]
        weights = [
            softmax_keys(q[:, at], jnp.concatenate([ko[:, at], far[0, :, at]], 0)).astype(bf16)
            for at in spots
        ]
        for (j, i), at, p in zip(group, spots, weights, strict=True):
            values = jnp.concatenate([vo[:, at], far[1, :, at]], 0)
            rows = slice(i * HEAD_DIM, (i + 1) * HEAD_DIM)
            out[j >> 1, j & 1, rows, :] = dot_l(values, p).astype(bf16)


def backward_kernel(near_ref, q, ko, vo, km, vm, kn, vn, g, dq, dko, dvo, dfar, far):
    choose_far(near_ref, km, vm, kn, vn, far)
    tile = q.shape[0]
    count = q.shape[1] // HEAD_DIM
    for first in range(0, count, GROUP):
        spots = [
            slice(h * HEAD_DIM, (h + 1) * HEAD_DIM)
            for h in range(first, min(first + GROUP, count))
        ]
        weights, slopes = [], []
        for at in spots:
            values = jnp.concatenate([vo[:, at], far[1, :, at]], 0)
            keys = jnp.concatenate([ko[:, at], far[0, :, at]], 0)
            weights.append(softmax_keys(q[:, at], keys))
            slopes.append(dot_t(values, g[:, at]))
        for at, p, dp in zip(spots, weights, slopes, strict=True):
            pb = p.astype(bf16)
            delta = jnp.sum(pb.astype(f32) * dp, axis=0, keepdims=True)
            ds = (p * (dp - delta)).astype(bf16)
            keys = jnp.concatenate([ko[:, at], far[0, :, at]], 0)
            dk = dot_n(ds, q[:, at]) * SCALE
            dv = dot_n(pb, g[:, at])
            dq[:, at] = (dot_l(ds, keys) * SCALE).astype(bf16)
            dko[:, at] = dk[:tile]
            dvo[:, at] = dv[:tile]
            dfar[0, :, at] = dk[tile:].astype(bf16)
            dfar[1, :, at] = dv[tile:].astype(bf16)


def combine_kernel(near_ref, dko, dvo, mate, beyond, dk, dv):
    place = lax.axis_index("seq")
    last = lax.axis_size("seq") - 1
    other = place + 2 * (place & 1) - 1
    inside = (other >= 0) & (other <= last)
    from_mate = near_ref[0, place ^ 1] == place
    from_other = inside & (near_ref[0, jnp.clip(other, 0, last)] == place)
    for which, (own, out) in enumerate(((dko, dk), (dvo, dv))):
        total = own[...] + jnp.where(from_mate, mate[which].astype(f32), 0.0)
        out[...] = (total + jnp.where(from_other, beyond[which].astype(f32), 0.0)).astype(bf16)


def product_kernel(plan, layers, *refs):
    att = refs[: plan.pairs]
    cols, *outs, for_mate, gathered = refs[plan.pairs :]
    for t in range(plan.pairs):
        at = slice(t * HEAD_DIM, (t + 1) * HEAD_DIM)
        for core in range(2):
            for n, i in enumerate(layers):
                block = att[t][core, i * HEAD_DIM : (i + 1) * HEAD_DIM, :]
                gathered[core, n * HEAD_DIM : (n + 1) * HEAD_DIM, at] = block
    tokens, width = gathered.shape[2], cols.shape[2]
    step = 512 if width % 512 == 0 else width
    for c in range(0, width, step):
        block = cols[:, :, c : c + step].reshape(tokens, step)
        for n, out in enumerate(outs):
            rows = slice(n * HEAD_DIM, (n + 1) * HEAD_DIM)
            out[:, c : c + step] = dot_n(gathered[0, rows, :], block)
            for_mate[n, :, c : c + step] = dot_n(gathered[1, rows, :], block).astype(bf16)


def piece(ref, lead, start, size):
    at = slice(start, start + size)
    return (ref[:, at] if lead is None else ref[lead, :, at]).astype(f32)


def sum_kernel(spots, start, *refs):
    *parts, out = refs
    size = out.shape[1]
    total = None
    for (lead, first), part in zip(spots, parts, strict=True):
        value = piece(part, lead, start - first, size)
        total = value if total is None else total + value
    out[...] = total.astype(bf16)


def gram_kernel(spots, own, *refs):
    *parts, x, gram = refs
    x[...] = own[...]
    for (lead, first), part in zip(spots, parts, strict=True):
        size = part.shape[-1]
        x[:, first : first + size] += piece(part, lead, 0, size)
    gram[...] = exact(x[...], x[...], ((1,), (1,)))


def polynomial(gram):
    eye = (
        lax.broadcasted_iota(jnp.int32, gram.shape, 0)
        == lax.broadcasted_iota(jnp.int32, gram.shape, 1)
    ).astype(f32)
    square = jnp.sum(jnp.sum(gram * eye, axis=1, keepdims=True), axis=0, keepdims=True)
    inverse = 1.0 / (jnp.sqrt(square) + 1e-07)
    a = gram * inverse * inverse
    p = None
    for turn in range(NS_STEPS):
        q = coeff_a * eye + coeff_b * a + coeff_c * exact(a, a)
        p = q if p is None else exact(q, p)
        if turn + 1 < NS_STEPS:
            a = exact(exact(q, a), q)
    return p, inverse


def update_kernel(plan, factor, x, gram, gram_other, *outs):
    mine = plan.row_part(lax.axis_index("seq"))
    p, inverse = polynomial(gram[...] + gram_other[...])
    p = p * (inverse * factor)
    width = outs[0].shape[1]
    for j in range(plan.per_target):
        if width % HEAD_DIM == 0:
            block = x[:, pl.ds(pl.multiple_of((mine ^ j) * width, width), width)]
        else:
            block = jnp.zeros((HEAD_DIM, width), f32)
            for r in range(plan.per_target):
                part = x[:, r * width : (r + 1) * width]
                block = jnp.where((mine ^ j) == r, part, block)
        outs[j][...] = exact(p, block).astype(outs[j].dtype)


def place_kernel(plan, *refs):
    *parts, out = refs
    mine = plan.row_part(lax.axis_index("seq"))
    for j, part in enumerate(parts):
        at = pl.ds(pl.multiple_of((mine ^ j) * HEAD_DIM, HEAD_DIM), HEAD_DIM)
        out[at, :] = part[...].astype(f32)


def local(query_tiles, key_tiles, value_tiles, attn_grad, proj_grad, neighbour):
    tile, width = query_tiles.shape[2:]
    depth = proj_grad.shape[3]
    head_count = width // HEAD_DIM
    plan = Plan(head_count)
    n, m, per = plan.seq, plan.dp, plan.per_target
    place = lax.axis_index("seq")
    struct = jax.ShapeDtypeStruct
    query, key, value, grad = (
        a.reshape(tile, width) for a in (query_tiles, key_tiles, value_tiles, attn_grad)
    )

    steps = [(i, i + 1) for i in range(1, n - 1, 2)]
    back = [(j, i) for i, j in steps]
    takes = [(i, j) for i, j in steps if j != n - 2] + [(j, i) for j, i in back if i != 1]
    gives = [(i, j) for i, j in steps if i != 1] + [(j, i) for j, i in back if j != n - 2]
    key_next = lax.ppermute(key, "seq", takes)
    value_next = lax.ppermute(value, "seq", takes)
    key_mate = shift(key, "seq", 1)
    value_mate = shift(value, "seq", 1)
    beside = (key_mate, value_mate, key_next, value_next)

    slot = depth // n
    flat = proj_grad.reshape(tile, depth)
    mine = plan.col_part(place)
    mine_width = per * slot

    def column_part(part):
        return jnp.concatenate(
            [
                lax.dynamic_slice_in_dim(flat, (high * plan.col + part) * 2 * slot, 2 * slot, 1)
                for high in range(plan.high)
            ],
            1,
        )

    own_columns = column_part(mine)
    columns = [own_columns] + [
        shift(after(column_part(mine ^ q), key_next, value_next), "seq", q << 1)
        for q in range(1, plan.col)
    ]
    high_columns = [
        shift(after(own_columns, key_next, value_next), "seq", high << (1 + plan.col_bits))
        for high in range(1, plan.high)
    ]

    attended = pl.pallas_call(
        functools.partial(forward_kernel, plan),
        out_shape=struct((plan.high, 2, m * HEAD_DIM, tile), bf16),
        in_specs=[smem()] + whole(7),
        out_specs=pl.BlockSpec(memory_space=pltpu.VMEM),
        scratch_shapes=[pltpu.VMEM((2, tile, width), bf16)],
        compiler_params=params(),
        cost_estimate=cost(8 * tile * tile * width, 16 * tile * width, 2 * tile * tile * head_count),
        name="attention_forward",
    )(neighbour, query, key, value, *beside)

    pairs = [attended[0]] + [shift(attended[0], "seq", q << 1) for q in range(1, plan.col)]
    for high in range(1, plan.high):
        came_high = shift(attended[high], "seq", high << (1 + plan.col_bits))
        pairs.append(came_high)
        pairs += [shift(came_high, "seq", q << 1) for q in range(1, plan.col)]
    through = after(jnp.stack(columns[1:]), attended)
    held = [jnp.stack(columns)]
    for high in range(1, plan.high):
        rest = shift(through, "seq", high << (1 + plan.col_bits))
        held.append(jnp.concatenate([high_columns[high - 1][None], rest], 0))
    held = jnp.concatenate(held, 0)

    dq, dko, dvo, dfar = pl.pallas_call(
        backward_kernel,
        out_shape=[
            struct((tile, width), bf16),
            struct((tile, width), f32),
            struct((tile, width), f32),
            struct((2, tile, width), bf16),
        ],
        in_specs=[smem()] + whole(8),
        out_specs=whole(4),
        scratch_shapes=[pltpu.VMEM((2, tile, width), bf16)],
        compiler_params=params(),
        cost_estimate=cost(28 * tile * tile * width, 30 * tile * width, 2 * tile * tile * head_count),
        name="attention_backward",
    )(neighbour, query, key, value, *beside, after(grad, attended))

    def product(name, layers, *operands):
        *blocks, for_mate = pl.pallas_call(
            functools.partial(product_kernel, plan, layers),
            out_shape=[struct((HEAD_DIM, mine_width), f32)] * len(layers)
            + [struct((len(layers), HEAD_DIM, mine_width), bf16)],
            in_specs=whole(plan.pairs + 1),
            out_specs=whole(len(layers) + 1),
            scratch_shapes=[pltpu.VMEM((2, len(layers) * HEAD_DIM, plan.pairs * tile), bf16)],
            compiler_params=params(),
            cost_estimate=cost(
                2 * len(layers) * HEAD_DIM * n * tile * mine_width, n * tile * mine_width
            ),
            name=name,
        )(*operands)
        mate = shift(for_mate, "seq", 1)
        return {i: [(block, None, 0), (mate, k, 0)] for k, (i, block) in enumerate(zip(layers, blocks))}

    def added(parts, start, size):
        return pl.pallas_call(
            functools.partial(sum_kernel, [spot for _, *spot in parts], start),
            out_shape=struct((HEAD_DIM, size), bf16),
            in_specs=whole(len(parts)),
            out_specs=pl.BlockSpec(memory_space=pltpu.VMEM),
            compiler_params=params(),
            cost_estimate=cost(len(parts) * HEAD_DIM * size, 4 * len(parts) * HEAD_DIM * size),
            name="block_sum",
        )(*[array for array, *_ in parts])

    leading = [i for i in range(m - 1, 1, -1) if i & 1]
    blocks = product("product_first", leading, after(pairs[0], dq), *pairs[1:], held)
    first_block = blocks[leading[0]][0][0]
    blocks |= product(
        "product_rest",
        [i for i in range(m) if i not in leading],
        after(pairs[0], first_block),
        *pairs[1:],
        held,
    )

    extra = {i: [] for i in range(m)}
    sent = []
    bit = 1
    while bit < m:
        for i in range(m - 1, 1, -1):
            if i & -i == bit:
                sent.append(added(blocks[i] + extra[i], 0, mine_width))
                extra[i ^ bit].append((shift(sent[-1], "dp", bit), None, 0))
        bit *= 2
    near = added(blocks[1], 0, mine_width)
    dfar = after(dfar, near)
    near = shift(after(near, sent[-1]), "dp", 1)
    own = blocks[0][0][0]
    came = [blocks[0][1], (near, None, 0)] + extra[0]

    x, gram = pl.pallas_call(
        functools.partial(gram_kernel, [spot for _, *spot in came]),
        out_shape=[struct((HEAD_DIM, mine_width), f32), struct((HEAD_DIM, HEAD_DIM), f32)],
        in_specs=whole(1 + len(came)),
        out_specs=whole(2),
        compiler_params=params(),
        cost_estimate=cost(12 * HEAD_DIM * HEAD_DIM * mine_width, 14 * HEAD_DIM * mine_width),
        name="gradient_sum",
    )(own, *[array for array, *_ in came])

    gram_other = jnp.zeros_like(gram)
    for b in range(plan.col_bits):
        gram = gram + gram_other
        gram_other = shift(gram, "seq", 2 << b)

    factor = 0.2 * depth**0.5
    pieces = pl.pallas_call(
        functools.partial(update_kernel, plan, factor),
        out_shape=[struct((HEAD_DIM, slot), f32)] + [struct((HEAD_DIM, slot), bf16)] * (per - 1),
        in_specs=whole(3),
        out_specs=whole(per),
        compiler_params=params(),
        cost_estimate=cost(12 * HEAD_DIM * HEAD_DIM * mine_width, 8 * HEAD_DIM * mine_width),
        name="newton_schulz",
    )(x, gram, gram_other)
    dk, dv = pl.pallas_call(
        combine_kernel,
        out_shape=[struct((tile, width), bf16)] * 2,
        in_specs=[smem()] + whole(4),
        out_specs=whole(2),
        compiler_params=params(),
        cost_estimate=cost(6 * tile * width, 20 * tile * width),
        name="key_value_sum",
    )(
        neighbour,
        dko,
        dvo,
        shift(dfar, "seq", 1),
        lax.ppermute(dfar, "seq", gives),
    )

    pieces = [pieces[0]] + [
        shift(pieces[j], "seq", plan.row_mask(j)) for j in range(1, per)
    ]
    update = pl.pallas_call(
        functools.partial(place_kernel, plan),
        out_shape=struct((per * HEAD_DIM, slot), f32),
        in_specs=whole(per),
        out_specs=pl.BlockSpec(memory_space=pltpu.VMEM),
        compiler_params=params(),
        cost_estimate=cost(1, 8 * per * HEAD_DIM * slot),
        name="update_rows",
    )(after(pieces[0], dk), *pieces[1:])

    shape = query_tiles.shape
    return dq.reshape(shape), dk.reshape(shape), dv.reshape(shape), update


def solution(mesh):
    tiles = P("dp", "seq", None, None)
    return jax.shard_map(
        local,
        mesh=mesh,
        in_specs=(tiles, tiles, tiles, tiles, tiles, P("dp", None)),
        out_specs=(tiles, tiles, tiles, P("dp", "seq")),
        check_vma=False,
    )
```

```python
import functools
import math

import jax
import jax.numpy as jnp
from jax import lax
from jax.experimental import pallas as pl
from jax.experimental.pallas import tpu as pltpu
from jax.sharding import PartitionSpec as P

HEAD_DIM = 128
NS_STEPS = 5
SCALE = HEAD_DIM ** (-0.5)
LOG2E = math.log2(math.e)
GROUP = 4
coeff_a = 3.4445
coeff_b = -4.775
coeff_c = 2.0315
f32 = jnp.float32
bf16 = jnp.bfloat16
VMEM_LIMIT = 24 * 1024 * 1024


def whole(count):
    return [pl.BlockSpec(memory_space=pltpu.VMEM)] * count


def smem():
    return pl.BlockSpec(memory_space=pltpu.SMEM)


def params():
    return pltpu.CompilerParams(vmem_limit_bytes=VMEM_LIMIT)


def cost(flops, moved, exps=0):
    return pl.CostEstimate(flops=int(flops), bytes_accessed=int(moved), transcendentals=int(exps))


def dot_t(a, b):
    return lax.dot_general(a, b, (((1,), (1,)), ((), ())), preferred_element_type=f32)


def dot_n(a, b):
    return lax.dot_general(a, b, (((1,), (0,)), ((), ())), preferred_element_type=f32)


def dot_l(a, b):
    return lax.dot_general(a, b, (((0,), (0,)), ((), ())), preferred_element_type=f32)


def exact(a, b, dims=((1,), (0,))):
    return lax.dot_general(
        a, b, (dims, ((), ())), precision=lax.Precision.HIGHEST, preferred_element_type=f32
    )


class Plan:
    def __init__(self, head_count):
        self.seq = lax.axis_size("seq")
        self.dp = lax.axis_size("dp")
        self.per_target = head_count // self.dp
        self.high = self.per_target // 2
        self.col = self.seq // self.per_target
        self.col_bits = self.col.bit_length() - 1
        self.pairs = self.seq // 2

    def row_part(self, place):
        return (place >> (1 + self.col_bits)) * 2 + (place & 1)

    def row_mask(self, part):
        return ((part >> 1) << (1 + self.col_bits)) | (part & 1)

    def col_part(self, place):
        return (place >> 1) & (self.col - 1)


def after(value, *others):
    return lax.optimization_barrier((value, *others))[0]


def shift(value, axis, mask):
    return lax.ppermute(value, axis, [(i, i ^ mask) for i in range(lax.axis_size(axis))])


def head_slice(index):
    return pl.ds(pl.multiple_of(index * HEAD_DIM, HEAD_DIM), HEAD_DIM)


def softmax_keys(query, keys):
    scores = dot_t(keys, query)
    top = jnp.max(scores, axis=0, keepdims=True)
    powers = jnp.exp2((scores - top) * (SCALE * LOG2E))
    return powers * (1.0 / jnp.sum(powers, axis=0, keepdims=True))


def choose_far(near_ref, key_mate, value_mate, key_next, value_next, far):
    place = lax.axis_index("seq")
    is_mate = near_ref[0, place] == (place ^ 1)

    @pl.when(is_mate)
    def _():
        far[0] = key_mate[...]
        far[1] = value_mate[...]

    @pl.when(jnp.logical_not(is_mate))
    def _():
        far[0] = key_next[...]
        far[1] = value_next[...]


def forward_kernel(plan, near_ref, q, ko, vo, km, vm, kn, vn, out, far):
    layer = lax.axis_index("dp")
    choose_far(near_ref, km, vm, kn, vn, far)
    mine = plan.row_part(lax.axis_index("seq"))
    jobs = [(j, i) for j in range(plan.per_target) for i in range(plan.dp)]
    for first in range(0, len(jobs), GROUP):
        group = jobs[first : first + GROUP]
        spots = [head_slice((layer ^ i) * plan.per_target + (mine ^ j)) for j, i in group]
        weights = [
            softmax_keys(q[:, at], jnp.concatenate([ko[:, at], far[0, :, at]], 0)).astype(bf16)
            for at in spots
        ]
        for (j, i), at, p in zip(group, spots, weights, strict=True):
            values = jnp.concatenate([vo[:, at], far[1, :, at]], 0)
            rows = slice(i * HEAD_DIM, (i + 1) * HEAD_DIM)
            out[j >> 1, j & 1, rows, :] = dot_l(values, p).astype(bf16)


def backward_kernel(near_ref, q, ko, vo, km, vm, kn, vn, g, dq, dko, dvo, dfar, far):
    choose_far(near_ref, km, vm, kn, vn, far)
    tile = q.shape[0]
    count = q.shape[1] // HEAD_DIM
    for first in range(0, count, GROUP):
        spots = [
            slice(h * HEAD_DIM, (h + 1) * HEAD_DIM)
            for h in range(first, min(first + GROUP, count))
        ]
        weights, slopes = [], []
        for at in spots:
            values = jnp.concatenate([vo[:, at], far[1, :, at]], 0)
            keys = jnp.concatenate([ko[:, at], far[0, :, at]], 0)
            weights.append(softmax_keys(q[:, at], keys))
            slopes.append(dot_t(values, g[:, at]))
        for at, p, dp in zip(spots, weights, slopes, strict=True):
            pb = p.astype(bf16)
            delta = jnp.sum(pb.astype(f32) * dp, axis=0, keepdims=True)
            ds = (p * (dp - delta)).astype(bf16)
            keys = jnp.concatenate([ko[:, at], far[0, :, at]], 0)
            dk = dot_n(ds, q[:, at]) * SCALE
            dv = dot_n(pb, g[:, at])
            dq[:, at] = (dot_l(ds, keys) * SCALE).astype(bf16)
            dko[:, at] = dk[:tile]
            dvo[:, at] = dv[:tile]
            dfar[0, :, at] = dk[tile:].astype(bf16)
            dfar[1, :, at] = dv[tile:].astype(bf16)


def combine_kernel(near_ref, dko, dvo, mate, beyond, dk, dv):
    place = lax.axis_index("seq")
    last = lax.axis_size("seq") - 1
    other = place + 2 * (place & 1) - 1
    inside = (other >= 0) & (other <= last)
    from_mate = near_ref[0, place ^ 1] == place
    from_other = inside & (near_ref[0, jnp.clip(other, 0, last)] == place)
    for which, (own, out) in enumerate(((dko, dk), (dvo, dv))):
        total = own[...] + jnp.where(from_mate, mate[which].astype(f32), 0.0)
        out[...] = (total + jnp.where(from_other, beyond[which].astype(f32), 0.0)).astype(bf16)


def product_kernel(plan, layers, *refs):
    att = refs[: plan.pairs]
    cols, *outs, for_mate, gathered = refs[plan.pairs :]
    for t in range(plan.pairs):
        at = slice(t * HEAD_DIM, (t + 1) * HEAD_DIM)
        for core in range(2):
            for n, i in enumerate(layers):
                block = att[t][core, i * HEAD_DIM : (i + 1) * HEAD_DIM, :]
                gathered[core, n * HEAD_DIM : (n + 1) * HEAD_DIM, at] = block
    tokens, width = gathered.shape[2], cols.shape[2]
    step = 512 if width % 512 == 0 else width
    for c in range(0, width, step):
        block = cols[:, :, c : c + step].reshape(tokens, step)
        for n, out in enumerate(outs):
            rows = slice(n * HEAD_DIM, (n + 1) * HEAD_DIM)
            out[:, c : c + step] = dot_n(gathered[0, rows, :], block)
            for_mate[n, :, c : c + step] = dot_n(gathered[1, rows, :], block).astype(bf16)


def piece(ref, lead, start, size):
    at = slice(start, start + size)
    return (ref[:, at] if lead is None else ref[lead, :, at]).astype(f32)


def sum_kernel(spots, start, *refs):
    *parts, out = refs
    size = out.shape[1]
    total = None
    for (lead, first), part in zip(spots, parts, strict=True):
        value = piece(part, lead, start - first, size)
        total = value if total is None else total + value
    out[...] = total.astype(bf16)


def gram_kernel(spots, own, *refs):
    *parts, x, gram = refs
    x[...] = own[...]
    for (lead, first), part in zip(spots, parts, strict=True):
        size = part.shape[-1]
        x[:, first : first + size] += piece(part, lead, 0, size)
    gram[...] = exact(x[...], x[...], ((1,), (1,)))


def polynomial(gram):
    eye = (
        lax.broadcasted_iota(jnp.int32, gram.shape, 0)
        == lax.broadcasted_iota(jnp.int32, gram.shape, 1)
    ).astype(f32)
    square = jnp.sum(jnp.sum(gram * eye, axis=1, keepdims=True), axis=0, keepdims=True)
    inverse = 1.0 / (jnp.sqrt(square) + 1e-07)
    a = gram * inverse * inverse
    p = None
    for turn in range(NS_STEPS):
        q = coeff_a * eye + coeff_b * a + coeff_c * exact(a, a)
        p = q if p is None else exact(q, p)
        if turn + 1 < NS_STEPS:
            a = exact(exact(q, a), q)
    return p, inverse


def update_kernel(plan, factor, x, gram, gram_other, *outs):
    mine = plan.row_part(lax.axis_index("seq"))
    p, inverse = polynomial(gram[...] + gram_other[...])
    p = p * (inverse * factor)
    width = outs[0].shape[1]
    for j in range(plan.per_target):
        if width % HEAD_DIM == 0:
            block = x[:, pl.ds(pl.multiple_of((mine ^ j) * width, width), width)]
        else:
            block = jnp.zeros((HEAD_DIM, width), f32)
            for r in range(plan.per_target):
                part = x[:, r * width : (r + 1) * width]
                block = jnp.where((mine ^ j) == r, part, block)
        outs[j][...] = exact(p, block).astype(outs[j].dtype)


def place_kernel(plan, *refs):
    *parts, out = refs
    mine = plan.row_part(lax.axis_index("seq"))
    for j, part in enumerate(parts):
        at = pl.ds(pl.multiple_of((mine ^ j) * HEAD_DIM, HEAD_DIM), HEAD_DIM)
        out[at, :] = part[...].astype(f32)


def local(query_tiles, key_tiles, value_tiles, attn_grad, proj_grad, neighbour):
    tile, width = query_tiles.shape[2:]
    depth = proj_grad.shape[3]
    head_count = width // HEAD_DIM
    plan = Plan(head_count)
    n, m, per = plan.seq, plan.dp, plan.per_target
    place = lax.axis_index("seq")
    struct = jax.ShapeDtypeStruct
    query, key, value, grad = (
        a.reshape(tile, width) for a in (query_tiles, key_tiles, value_tiles, attn_grad)
    )

    steps = [(i, i + 1) for i in range(1, n - 1, 2)]
    back = [(j, i) for i, j in steps]
    takes = [(i, j) for i, j in steps if j != n - 2] + [(j, i) for j, i in back if i != 1]
    gives = [(i, j) for i, j in steps if i != 1] + [(j, i) for j, i in back if j != n - 2]
    key_next = lax.ppermute(key, "seq", takes)
    value_next = lax.ppermute(value, "seq", takes)
    key_mate = shift(key, "seq", 1)
    value_mate = shift(value, "seq", 1)
    beside = (key_mate, value_mate, key_next, value_next)

    slot = depth // n
    flat = proj_grad.reshape(tile, depth)
    mine = plan.col_part(place)
    mine_width = per * slot

    def column_part(part):
        return jnp.concatenate(
            [
                lax.dynamic_slice_in_dim(flat, (high * plan.col + part) * 2 * slot, 2 * slot, 1)
                for high in range(plan.high)
            ],
            1,
        )

    own_columns = column_part(mine)
    columns = [own_columns] + [
        shift(after(column_part(mine ^ q), key_next, value_next), "seq", q << 1)
        for q in range(1, plan.col)
    ]
    high_columns = [
        shift(after(own_columns, key_next, value_next), "seq", high << (1 + plan.col_bits))
        for high in range(1, plan.high)
    ]

    attended = pl.pallas_call(
        functools.partial(forward_kernel, plan),
        out_shape=struct((plan.high, 2, m * HEAD_DIM, tile), bf16),
        in_specs=[smem()] + whole(7),
        out_specs=pl.BlockSpec(memory_space=pltpu.VMEM),
        scratch_shapes=[pltpu.VMEM((2, tile, width), bf16)],
        compiler_params=params(),
        cost_estimate=cost(8 * tile * tile * width, 16 * tile * width, 2 * tile * tile * head_count),
        name="attention_forward",
    )(neighbour, query, key, value, *beside)

    pairs = [attended[0]] + [shift(attended[0], "seq", q << 1) for q in range(1, plan.col)]
    for high in range(1, plan.high):
        came_high = shift(attended[high], "seq", high << (1 + plan.col_bits))
        pairs.append(came_high)
        there = after(came_high, *pairs[1 : plan.col])
        pairs += [shift(there, "seq", q << 1) for q in range(1, plan.col)]

    through = after(jnp.stack(columns[1:]), attended)
    held = [jnp.stack(columns)]
    for high in range(1, plan.high):
        rest = jnp.concatenate(
            [shift(part, "seq", high << (1 + plan.col_bits)) for part in jnp.split(through, 2, 2)], 2
        )
        held.append(jnp.concatenate([high_columns[high - 1][None], rest], 0))
    held = jnp.concatenate(held, 0)

    def product(name, layers, *operands):
        *blocks, for_mate = pl.pallas_call(
            functools.partial(product_kernel, plan, layers),
            out_shape=[struct((HEAD_DIM, mine_width), f32)] * len(layers)
            + [struct((len(layers), HEAD_DIM, mine_width), bf16)],
            in_specs=whole(plan.pairs + 1),
            out_specs=whole(len(layers) + 1),
            scratch_shapes=[pltpu.VMEM((2, len(layers) * HEAD_DIM, plan.pairs * tile), bf16)],
            compiler_params=params(),
            cost_estimate=cost(
                2 * len(layers) * HEAD_DIM * n * tile * mine_width, n * tile * mine_width
            ),
            name=name,
        )(*operands)
        mate = shift(for_mate, "seq", 1)
        return {i: [(block, None, 0), (mate, k, 0)] for k, (i, block) in enumerate(zip(layers, blocks))}

    def added(parts, start, size):
        return pl.pallas_call(
            functools.partial(sum_kernel, [spot for _, *spot in parts], start),
            out_shape=struct((HEAD_DIM, size), bf16),
            in_specs=whole(len(parts)),
            out_specs=pl.BlockSpec(memory_space=pltpu.VMEM),
            compiler_params=params(),
            cost_estimate=cost(len(parts) * HEAD_DIM * size, 4 * len(parts) * HEAD_DIM * size),
            name="block_sum",
        )(*[array for array, *_ in parts])

    leading = [i for i in range(m - 1, 1, -1) if i & 1]
    blocks = product("product_first", leading, *pairs, held)
    first_block = blocks[leading[0]][0][0]
    blocks |= product(
        "product_rest",
        [i for i in range(m) if i not in leading],
        after(pairs[0], first_block),
        *pairs[1:],
        held,
    )

    extra = {i: [] for i in range(m)}
    sent = []
    bit = 1
    while bit < m:
        for i in range(m - 1, 1, -1):
            if i & -i == bit:
                sent.append(added(blocks[i] + extra[i], 0, mine_width))
                extra[i ^ bit].append((shift(sent[-1], "dp", bit), None, 0))
        bit *= 2
    near = shift(after(added(blocks[1], 0, mine_width), sent[-1]), "dp", 1)
    own = blocks[0][0][0]
    came = [blocks[0][1], (near, None, 0)] + extra[0]

    dq, dko, dvo, dfar = pl.pallas_call(
        backward_kernel,
        out_shape=[
            struct((tile, width), bf16),
            struct((tile, width), f32),
            struct((tile, width), f32),
            struct((2, tile, width), bf16),
        ],
        in_specs=[smem()] + whole(8),
        out_specs=whole(4),
        scratch_shapes=[pltpu.VMEM((2, tile, width), bf16)],
        compiler_params=params(),
        cost_estimate=cost(28 * tile * tile * width, 30 * tile * width, 2 * tile * tile * head_count),
        name="attention_backward",
    )(neighbour, query, key, value, *beside, after(grad, *pairs[plan.col :: plan.col]))

    x, gram = pl.pallas_call(
        functools.partial(gram_kernel, [spot for _, *spot in came]),
        out_shape=[struct((HEAD_DIM, mine_width), f32), struct((HEAD_DIM, HEAD_DIM), f32)],
        in_specs=whole(1 + len(came)),
        out_specs=whole(2),
        compiler_params=params(),
        cost_estimate=cost(12 * HEAD_DIM * HEAD_DIM * mine_width, 14 * HEAD_DIM * mine_width),
        name="gradient_sum",
    )(own, *[array for array, *_ in came])

    gram_other = jnp.zeros_like(gram)
    for b in range(plan.col_bits):
        gram = gram + gram_other
        gram_other = shift(gram, "seq", 2 << b)

    factor = 0.2 * depth**0.5
    pieces = pl.pallas_call(
        functools.partial(update_kernel, plan, factor),
        out_shape=[struct((HEAD_DIM, slot), f32)] + [struct((HEAD_DIM, slot), bf16)] * (per - 1),
        in_specs=whole(3),
        out_specs=whole(per),
        compiler_params=params(),
        cost_estimate=cost(12 * HEAD_DIM * HEAD_DIM * mine_width, 8 * HEAD_DIM * mine_width),
        name="newton_schulz",
    )(x, gram, gram_other)
    dfar = after(dfar, sent[-1])
    dk, dv = pl.pallas_call(
        combine_kernel,
        out_shape=[struct((tile, width), bf16)] * 2,
        in_specs=[smem()] + whole(4),
        out_specs=whole(2),
        compiler_params=params(),
        cost_estimate=cost(6 * tile * width, 20 * tile * width),
        name="key_value_sum",
    )(
        neighbour,
        dko,
        dvo,
        shift(dfar, "seq", 1),
        lax.ppermute(dfar, "seq", gives),
    )

    pieces = [pieces[0]] + [
        shift(pieces[j], "seq", plan.row_mask(j)) for j in range(1, per)
    ]
    update = pl.pallas_call(
        functools.partial(place_kernel, plan),
        out_shape=struct((per * HEAD_DIM, slot), f32),
        in_specs=whole(per),
        out_specs=pl.BlockSpec(memory_space=pltpu.VMEM),
        compiler_params=params(),
        cost_estimate=cost(1, 8 * per * HEAD_DIM * slot),
        name="update_rows",
    )(after(pieces[0], dk), *pieces[1:])

    shape = query_tiles.shape
    return dq.reshape(shape), dk.reshape(shape), dv.reshape(shape), update


def solution(mesh):
    tiles = P("dp", "seq", None, None)
    return jax.shard_map(
        local,
        mesh=mesh,
        in_specs=(tiles, tiles, tiles, tiles, tiles, P("dp", None)),
        out_specs=(tiles, tiles, tiles, P("dp", "seq")),
        check_vma=False,
    )
```

```python
import functools
import math

import jax
import jax.numpy as jnp
from jax import lax
from jax.experimental import pallas as pl
from jax.experimental.pallas import tpu as pltpu
from jax.sharding import PartitionSpec as P

HEAD_DIM = 128
NS_STEPS = 5
SCALE = HEAD_DIM ** (-0.5)
LOG2E = math.log2(math.e)
GROUP = 4
coeff_a = 3.4445
coeff_b = -4.775
coeff_c = 2.0315
f32 = jnp.float32
bf16 = jnp.bfloat16
VMEM_LIMIT = 24 * 1024 * 1024


def whole(count):
    return [pl.BlockSpec(memory_space=pltpu.VMEM)] * count


def smem():
    return pl.BlockSpec(memory_space=pltpu.SMEM)


def params():
    return pltpu.CompilerParams(vmem_limit_bytes=VMEM_LIMIT)


def cost(flops, moved, exps=0):
    return pl.CostEstimate(flops=int(flops), bytes_accessed=int(moved), transcendentals=int(exps))


def dot_t(a, b):
    return lax.dot_general(a, b, (((1,), (1,)), ((), ())), preferred_element_type=f32)


def dot_n(a, b):
    return lax.dot_general(a, b, (((1,), (0,)), ((), ())), preferred_element_type=f32)


def dot_l(a, b):
    return lax.dot_general(a, b, (((0,), (0,)), ((), ())), preferred_element_type=f32)


def exact(a, b, dims=((1,), (0,))):
    return lax.dot_general(
        a, b, (dims, ((), ())), precision=lax.Precision.HIGHEST, preferred_element_type=f32
    )


class Plan:
    def __init__(self, head_count):
        self.seq = lax.axis_size("seq")
        self.dp = lax.axis_size("dp")
        self.per_target = head_count // self.dp
        self.high = self.per_target // 2
        self.col = self.seq // self.per_target
        self.col_bits = self.col.bit_length() - 1
        self.pairs = self.seq // 2

    def row_part(self, place):
        return (place >> (1 + self.col_bits)) * 2 + (place & 1)

    def row_mask(self, part):
        return ((part >> 1) << (1 + self.col_bits)) | (part & 1)

    def col_part(self, place):
        return (place >> 1) & (self.col - 1)


def after(value, *others):
    return lax.optimization_barrier((value, *others))[0]


def shift(value, axis, mask):
    return lax.ppermute(value, axis, [(i, i ^ mask) for i in range(lax.axis_size(axis))])


def head_slice(index):
    return pl.ds(pl.multiple_of(index * HEAD_DIM, HEAD_DIM), HEAD_DIM)


def softmax_keys(query, keys):
    scores = dot_t(keys, query)
    top = jnp.max(scores, axis=0, keepdims=True)
    powers = jnp.exp2((scores - top) * (SCALE * LOG2E))
    return powers * (1.0 / jnp.sum(powers, axis=0, keepdims=True))


def choose_far(near_ref, key_mate, value_mate, key_next, value_next, far):
    place = lax.axis_index("seq")
    is_mate = near_ref[0, place] == (place ^ 1)

    @pl.when(is_mate)
    def _():
        far[0] = key_mate[...]
        far[1] = value_mate[...]

    @pl.when(jnp.logical_not(is_mate))
    def _():
        far[0] = key_next[...]
        far[1] = value_next[...]


def forward_kernel(plan, near_ref, q, ko, vo, km, vm, kn, vn, out, far):
    layer = lax.axis_index("dp")
    choose_far(near_ref, km, vm, kn, vn, far)
    mine = plan.row_part(lax.axis_index("seq"))
    jobs = [(j, i) for j in range(plan.per_target) for i in range(plan.dp)]
    for first in range(0, len(jobs), GROUP):
        group = jobs[first : first + GROUP]
        spots = [head_slice((layer ^ i) * plan.per_target + (mine ^ j)) for j, i in group]
        weights = [
            softmax_keys(q[:, at], jnp.concatenate([ko[:, at], far[0, :, at]], 0)).astype(bf16)
            for at in spots
        ]
        for (j, i), at, p in zip(group, spots, weights, strict=True):
            values = jnp.concatenate([vo[:, at], far[1, :, at]], 0)
            rows = slice(i * HEAD_DIM, (i + 1) * HEAD_DIM)
            out[j >> 1, j & 1, rows, :] = dot_l(values, p).astype(bf16)


def backward_kernel(near_ref, q, ko, vo, km, vm, kn, vn, g, dq, dko, dvo, dkf, dvf, dfar, far):
    choose_far(near_ref, km, vm, kn, vn, far)
    tile = q.shape[0]
    count = q.shape[1] // HEAD_DIM
    for first in range(0, count, GROUP):
        spots = [
            slice(h * HEAD_DIM, (h + 1) * HEAD_DIM)
            for h in range(first, min(first + GROUP, count))
        ]
        weights, slopes = [], []
        for at in spots:
            values = jnp.concatenate([vo[:, at], far[1, :, at]], 0)
            keys = jnp.concatenate([ko[:, at], far[0, :, at]], 0)
            weights.append(softmax_keys(q[:, at], keys))
            slopes.append(dot_t(values, g[:, at]))
        for at, p, dp in zip(spots, weights, slopes, strict=True):
            pb = p.astype(bf16)
            delta = jnp.sum(pb.astype(f32) * dp, axis=0, keepdims=True)
            ds = (p * (dp - delta)).astype(bf16)
            keys = jnp.concatenate([ko[:, at], far[0, :, at]], 0)
            dk = dot_n(ds, q[:, at]) * SCALE
            dv = dot_n(pb, g[:, at])
            dq[:, at] = (dot_l(ds, keys) * SCALE).astype(bf16)
            dko[:, at] = dk[:tile]
            dvo[:, at] = dv[:tile]
            for which, (one, term) in enumerate(((dkf, dk), (dvf, dv))):
                rounded = term[tile:].astype(bf16)
                one[:, at] = rounded
                dfar[which, :, at] = rounded


def combine_kernel(near_ref, dko, dvo, mate, kn, vn, dk, dv):
    place = lax.axis_index("seq")
    last = lax.axis_size("seq") - 1
    other = place + 2 * (place & 1) - 1
    inside = (other >= 0) & (other <= last)
    from_mate = near_ref[0, place ^ 1] == place
    from_other = inside & (near_ref[0, jnp.clip(other, 0, last)] == place)
    for which, (own, beyond, out) in enumerate(((dko, kn, dk), (dvo, vn, dv))):
        total = own[...] + jnp.where(from_mate, mate[which].astype(f32), 0.0)
        out[...] = (total + jnp.where(from_other, beyond[...].astype(f32), 0.0)).astype(bf16)


def product_kernel(plan, layers, *refs):
    att = refs[: plan.pairs]
    cols, *outs, for_mate, gathered = refs[plan.pairs :]
    for t in range(plan.pairs):
        at = slice(t * HEAD_DIM, (t + 1) * HEAD_DIM)
        for core in range(2):
            for n, i in enumerate(layers):
                block = att[t][core, i * HEAD_DIM : (i + 1) * HEAD_DIM, :]
                gathered[core, n * HEAD_DIM : (n + 1) * HEAD_DIM, at] = block
    tokens, width = gathered.shape[2], cols.shape[2]
    step = 512 if width % 512 == 0 else width
    for c in range(0, width, step):
        block = cols[:, :, c : c + step].reshape(tokens, step)
        for n, out in enumerate(outs):
            rows = slice(n * HEAD_DIM, (n + 1) * HEAD_DIM)
            out[:, c : c + step] = dot_n(gathered[0, rows, :], block)
            for_mate[n, :, c : c + step] = dot_n(gathered[1, rows, :], block).astype(bf16)


def piece(ref, lead, start, size):
    at = slice(start, start + size)
    return (ref[:, at] if lead is None else ref[lead, :, at]).astype(f32)


def sum_kernel(spots, start, *refs):
    *parts, out = refs
    size = out.shape[1]
    total = None
    for (lead, first), part in zip(spots, parts, strict=True):
        value = piece(part, lead, start - first, size)
        total = value if total is None else total + value
    out[...] = total.astype(bf16)


def gram_kernel(spots, own, *refs):
    *parts, x, gram = refs
    x[...] = own[...]
    for (lead, first), part in zip(spots, parts, strict=True):
        size = part.shape[-1]
        x[:, first : first + size] += piece(part, lead, 0, size)
    gram[...] = exact(x[...], x[...], ((1,), (1,)))


def polynomial(gram):
    eye = (
        lax.broadcasted_iota(jnp.int32, gram.shape, 0)
        == lax.broadcasted_iota(jnp.int32, gram.shape, 1)
    ).astype(f32)
    square = jnp.sum(jnp.sum(gram * eye, axis=1, keepdims=True), axis=0, keepdims=True)
    inverse = 1.0 / (jnp.sqrt(square) + 1e-07)
    a = gram * inverse * inverse
    p = None
    for turn in range(NS_STEPS):
        q = coeff_a * eye + coeff_b * a + coeff_c * exact(a, a)
        p = q if p is None else exact(q, p)
        if turn + 1 < NS_STEPS:
            a = exact(exact(q, a), q)
    return p, inverse


def update_kernel(plan, factor, x, gram, gram_other, *outs):
    mine = plan.row_part(lax.axis_index("seq"))
    p, inverse = polynomial(gram[...] + gram_other[...])
    p = p * (inverse * factor)
    width = outs[0].shape[1]
    for j in range(plan.per_target):
        if width % HEAD_DIM == 0:
            block = x[:, pl.ds(pl.multiple_of((mine ^ j) * width, width), width)]
        else:
            block = jnp.zeros((HEAD_DIM, width), f32)
            for r in range(plan.per_target):
                part = x[:, r * width : (r + 1) * width]
                block = jnp.where((mine ^ j) == r, part, block)
        outs[j][...] = exact(p, block).astype(outs[j].dtype)


def place_kernel(plan, *refs):
    *parts, out = refs
    mine = plan.row_part(lax.axis_index("seq"))
    for j, part in enumerate(parts):
        at = pl.ds(pl.multiple_of((mine ^ j) * HEAD_DIM, HEAD_DIM), HEAD_DIM)
        out[at, :] = part[...].astype(f32)


def local(query_tiles, key_tiles, value_tiles, attn_grad, proj_grad, neighbour):
    tile, width = query_tiles.shape[2:]
    depth = proj_grad.shape[3]
    head_count = width // HEAD_DIM
    plan = Plan(head_count)
    n, m, per = plan.seq, plan.dp, plan.per_target
    place = lax.axis_index("seq")
    struct = jax.ShapeDtypeStruct
    query, key, value, grad = (
        a.reshape(tile, width) for a in (query_tiles, key_tiles, value_tiles, attn_grad)
    )

    steps = [(i, i + 1) for i in range(1, n - 1, 2)]
    back = [(j, i) for i, j in steps]
    takes = [(i, j) for i, j in steps if j != n - 2] + [(j, i) for j, i in back if i != 1]
    gives = [(i, j) for i, j in steps if i != 1] + [(j, i) for j, i in back if j != n - 2]
    key_next = lax.ppermute(key, "seq", takes)
    value_next = lax.ppermute(value, "seq", takes)
    key_mate = shift(key, "seq", 1)
    value_mate = shift(value, "seq", 1)
    beside = (key_mate, value_mate, key_next, value_next)

    slot = depth // n
    flat = proj_grad.reshape(tile, depth)
    mine = plan.col_part(place)
    mine_width = per * slot

    def column_part(part):
        return jnp.concatenate(
            [
                lax.dynamic_slice_in_dim(flat, (high * plan.col + part) * 2 * slot, 2 * slot, 1)
                for high in range(plan.high)
            ],
            1,
        )

    own_columns = column_part(mine)
    columns = [own_columns] + [
        shift(after(column_part(mine ^ q), key_next, value_next), "seq", q << 1)
        for q in range(1, plan.col)
    ]
    high_columns = [
        shift(after(own_columns, key_next, value_next), "seq", high << (1 + plan.col_bits))
        for high in range(1, plan.high)
    ]

    attended = pl.pallas_call(
        functools.partial(forward_kernel, plan),
        out_shape=struct((plan.high, 2, m * HEAD_DIM, tile), bf16),
        in_specs=[smem()] + whole(7),
        out_specs=pl.BlockSpec(memory_space=pltpu.VMEM),
        scratch_shapes=[pltpu.VMEM((2, tile, width), bf16)],
        compiler_params=params(),
        cost_estimate=cost(8 * tile * tile * width, 16 * tile * width, 2 * tile * tile * head_count),
        name="attention_forward",
    )(neighbour, query, key, value, *beside)

    pairs = [attended[0]] + [shift(attended[0], "seq", q << 1) for q in range(1, plan.col)]
    for high in range(1, plan.high):
        came_high = shift(attended[high], "seq", high << (1 + plan.col_bits))
        pairs.append(came_high)
        there = after(came_high, *pairs[1 : plan.col])
        pairs += [shift(there, "seq", q << 1) for q in range(1, plan.col)]

    through = after(jnp.stack(columns[1:]), attended)
    held = [jnp.stack(columns)]
    for high in range(1, plan.high):
        rest = jnp.concatenate(
            [shift(part, "seq", high << (1 + plan.col_bits)) for part in jnp.split(through, 2, 2)], 2
        )
        held.append(jnp.concatenate([high_columns[high - 1][None], rest], 0))
    held = jnp.concatenate(held, 0)

    def product(name, layers, *operands):
        *blocks, for_mate = pl.pallas_call(
            functools.partial(product_kernel, plan, layers),
            out_shape=[struct((HEAD_DIM, mine_width), f32)] * len(layers)
            + [struct((len(layers), HEAD_DIM, mine_width), bf16)],
            in_specs=whole(plan.pairs + 1),
            out_specs=whole(len(layers) + 1),
            scratch_shapes=[pltpu.VMEM((2, len(layers) * HEAD_DIM, plan.pairs * tile), bf16)],
            compiler_params=params(),
            cost_estimate=cost(
                2 * len(layers) * HEAD_DIM * n * tile * mine_width, n * tile * mine_width
            ),
            name=name,
        )(*operands)
        mate = shift(for_mate, "seq", 1)
        return {i: [(block, None, 0), (mate, k, 0)] for k, (i, block) in enumerate(zip(layers, blocks))}

    def added(parts, start, size):
        return pl.pallas_call(
            functools.partial(sum_kernel, [spot for _, *spot in parts], start),
            out_shape=struct((HEAD_DIM, size), bf16),
            in_specs=whole(len(parts)),
            out_specs=pl.BlockSpec(memory_space=pltpu.VMEM),
            compiler_params=params(),
            cost_estimate=cost(len(parts) * HEAD_DIM * size, 4 * len(parts) * HEAD_DIM * size),
            name="block_sum",
        )(*[array for array, *_ in parts])

    first = [i for i in range(m - 1, 1, -1) if i & 1]
    middle = [i for i in range(m - 1, 1, -1) if not i & 1]
    blocks = product("product_first", first, *pairs, held)
    going = {i: added(blocks[i], 0, mine_width) for i in first}
    blocks |= product("product_middle", middle, after(pairs[0], *going.values()), *pairs[1:], held)

    dq, dko, dvo, dkf, dvf, dfar = pl.pallas_call(
        backward_kernel,
        out_shape=[
            struct((tile, width), bf16),
            struct((tile, width), f32),
            struct((tile, width), f32),
            struct((tile, width), bf16),
            struct((tile, width), bf16),
            struct((2, tile, width), bf16),
        ],
        in_specs=[smem()] + whole(8),
        out_specs=whole(6),
        scratch_shapes=[pltpu.VMEM((2, tile, width), bf16)],
        compiler_params=params(),
        cost_estimate=cost(28 * tile * tile * width, 30 * tile * width, 2 * tile * tile * head_count),
        name="attention_backward",
    )(neighbour, query, key, value, *beside, after(grad, *going.values()))

    blocks |= product("product_last", [1, 0], after(pairs[0], dq), *pairs[1:], held)

    extra = {i: [] for i in range(m)}
    sent = []
    bit = 1
    while bit < m:
        for i in range(m - 1, 1, -1):
            if i & -i == bit:
                if bit == 1:
                    sent.append(going[i])
                else:
                    (block, *where), *others = blocks[i] + extra[i]
                    sent.append(added([(after(block, dq), *where)] + others, 0, mine_width))
                extra[i ^ bit].append((shift(sent[-1], "dp", bit), None, 0))
        bit *= 2
    near = shift(after(added(blocks[1], 0, mine_width), sent[-1]), "dp", 1)
    own = blocks[0][0][0]
    came = [blocks[0][1], (near, None, 0)] + extra[0]

    x, gram = pl.pallas_call(
        functools.partial(gram_kernel, [spot for _, *spot in came]),
        out_shape=[struct((HEAD_DIM, mine_width), f32), struct((HEAD_DIM, HEAD_DIM), f32)],
        in_specs=whole(1 + len(came)),
        out_specs=whole(2),
        compiler_params=params(),
        cost_estimate=cost(12 * HEAD_DIM * HEAD_DIM * mine_width, 14 * HEAD_DIM * mine_width),
        name="gradient_sum",
    )(own, *[array for array, *_ in came])

    gram_other = jnp.zeros_like(gram)
    for b in range(plan.col_bits):
        gram = gram + gram_other
        gram_other = shift(gram, "seq", 2 << b)

    factor = 0.2 * depth**0.5
    pieces = pl.pallas_call(
        functools.partial(update_kernel, plan, factor),
        out_shape=[struct((HEAD_DIM, slot), f32)] + [struct((HEAD_DIM, slot), bf16)] * (per - 1),
        in_specs=whole(3),
        out_specs=whole(per),
        compiler_params=params(),
        cost_estimate=cost(12 * HEAD_DIM * HEAD_DIM * mine_width, 8 * HEAD_DIM * mine_width),
        name="newton_schulz",
    )(x, gram, gram_other)
    dkf, dvf, dfar = (after(part, sent[-1]) for part in (dkf, dvf, dfar))
    dk, dv = pl.pallas_call(
        combine_kernel,
        out_shape=[struct((tile, width), bf16)] * 2,
        in_specs=[smem()] + whole(5),
        out_specs=whole(2),
        compiler_params=params(),
        cost_estimate=cost(6 * tile * width, 20 * tile * width),
        name="key_value_sum",
    )(
        neighbour,
        dko,
        dvo,
        shift(dfar, "seq", 1),
        lax.ppermute(dkf, "seq", gives),
        lax.ppermute(dvf, "seq", gives),
    )

    pieces = [pieces[0]] + [
        shift(pieces[j], "seq", plan.row_mask(j)) for j in range(1, per)
    ]
    update = pl.pallas_call(
        functools.partial(place_kernel, plan),
        out_shape=struct((per * HEAD_DIM, slot), f32),
        in_specs=whole(per),
        out_specs=pl.BlockSpec(memory_space=pltpu.VMEM),
        compiler_params=params(),
        cost_estimate=cost(1, 8 * per * HEAD_DIM * slot),
        name="update_rows",
    )(after(pieces[0], dk), *pieces[1:])

    shape = query_tiles.shape
    return dq.reshape(shape), dk.reshape(shape), dv.reshape(shape), update


def solution(mesh):
    tiles = P("dp", "seq", None, None)
    return jax.shard_map(
        local,
        mesh=mesh,
        in_specs=(tiles, tiles, tiles, tiles, tiles, P("dp", None)),
        out_specs=(tiles, tiles, tiles, P("dp", "seq")),
        check_vma=False,
    )
```

```python
import functools
import math

import jax
import jax.numpy as jnp
from jax import lax
from jax.experimental import pallas as pl
from jax.experimental.pallas import tpu as pltpu
from jax.sharding import PartitionSpec as P

HEAD_DIM = 128
NS_STEPS = 5
SCALE = HEAD_DIM ** (-0.5)
LOG2E = math.log2(math.e)
GROUP = 4
coeff_a = 3.4445
coeff_b = -4.775
coeff_c = 2.0315
f32 = jnp.float32
bf16 = jnp.bfloat16
VMEM_LIMIT = 24 * 1024 * 1024


def whole(count):
    return [pl.BlockSpec(memory_space=pltpu.VMEM)] * count


def smem():
    return pl.BlockSpec(memory_space=pltpu.SMEM)


def params():
    return pltpu.CompilerParams(vmem_limit_bytes=VMEM_LIMIT)


def cost(flops, moved, exps=0):
    return pl.CostEstimate(flops=int(flops), bytes_accessed=int(moved), transcendentals=int(exps))


def dot_t(a, b):
    return lax.dot_general(a, b, (((1,), (1,)), ((), ())), preferred_element_type=f32)


def dot_n(a, b):
    return lax.dot_general(a, b, (((1,), (0,)), ((), ())), preferred_element_type=f32)


def dot_l(a, b):
    return lax.dot_general(a, b, (((0,), (0,)), ((), ())), preferred_element_type=f32)


def exact(a, b, dims=((1,), (0,))):
    return lax.dot_general(
        a, b, (dims, ((), ())), precision=lax.Precision.HIGHEST, preferred_element_type=f32
    )


class Plan:
    def __init__(self, head_count):
        self.seq = lax.axis_size("seq")
        self.dp = lax.axis_size("dp")
        self.per_target = head_count // self.dp
        self.high = self.per_target // 2
        self.col = self.seq // self.per_target
        self.col_bits = self.col.bit_length() - 1
        self.pairs = self.seq // 2

    def row_part(self, place):
        return (place >> (1 + self.col_bits)) * 2 + (place & 1)

    def row_mask(self, part):
        return ((part >> 1) << (1 + self.col_bits)) | (part & 1)

    def col_part(self, place):
        return (place >> 1) & (self.col - 1)


def after(value, *others):
    return lax.optimization_barrier((value, *others))[0]


def shift(value, axis, mask):
    return lax.ppermute(value, axis, [(i, i ^ mask) for i in range(lax.axis_size(axis))])


def head_slice(index):
    return pl.ds(pl.multiple_of(index * HEAD_DIM, HEAD_DIM), HEAD_DIM)


def softmax_keys(query, keys):
    scores = dot_t(keys, query)
    top = jnp.max(scores, axis=0, keepdims=True)
    powers = jnp.exp2((scores - top) * (SCALE * LOG2E))
    return powers * (1.0 / jnp.sum(powers, axis=0, keepdims=True))


def choose_far(near_ref, key_mate, value_mate, key_next, value_next, far):
    place = lax.axis_index("seq")
    is_mate = near_ref[0, place] == (place ^ 1)

    @pl.when(is_mate)
    def _():
        far[0] = key_mate[...]
        far[1] = value_mate[...]

    @pl.when(jnp.logical_not(is_mate))
    def _():
        far[0] = key_next[...]
        far[1] = value_next[...]


def forward_kernel(plan, near_ref, q, ko, vo, km, vm, kn, vn, out, far):
    layer = lax.axis_index("dp")
    choose_far(near_ref, km, vm, kn, vn, far)
    mine = plan.row_part(lax.axis_index("seq"))
    jobs = [(j, i) for j in range(plan.per_target) for i in range(plan.dp)]
    for first in range(0, len(jobs), GROUP):
        group = jobs[first : first + GROUP]
        spots = [head_slice((layer ^ i) * plan.per_target + (mine ^ j)) for j, i in group]
        weights = [
            softmax_keys(q[:, at], jnp.concatenate([ko[:, at], far[0, :, at]], 0)).astype(bf16)
            for at in spots
        ]
        for (j, i), at, p in zip(group, spots, weights, strict=True):
            values = jnp.concatenate([vo[:, at], far[1, :, at]], 0)
            rows = slice(i * HEAD_DIM, (i + 1) * HEAD_DIM)
            out[j >> 1, j & 1, rows, :] = dot_l(values, p).astype(bf16)


def backward_kernel(near_ref, q, ko, vo, km, vm, kn, vn, g, dq, dko, dvo, dkf, dvf, dfar, far):
    choose_far(near_ref, km, vm, kn, vn, far)
    tile = q.shape[0]
    count = q.shape[1] // HEAD_DIM
    for first in range(0, count, GROUP):
        spots = [
            slice(h * HEAD_DIM, (h + 1) * HEAD_DIM)
            for h in range(first, min(first + GROUP, count))
        ]
        weights, slopes = [], []
        for at in spots:
            values = jnp.concatenate([vo[:, at], far[1, :, at]], 0)
            keys = jnp.concatenate([ko[:, at], far[0, :, at]], 0)
            weights.append(softmax_keys(q[:, at], keys))
            slopes.append(dot_t(values, g[:, at]))
        for at, p, dp in zip(spots, weights, slopes, strict=True):
            pb = p.astype(bf16)
            delta = jnp.sum(pb.astype(f32) * dp, axis=0, keepdims=True)
            ds = (p * (dp - delta)).astype(bf16)
            keys = jnp.concatenate([ko[:, at], far[0, :, at]], 0)
            dk = dot_n(ds, q[:, at]) * SCALE
            dv = dot_n(pb, g[:, at])
            dq[:, at] = (dot_l(ds, keys) * SCALE).astype(bf16)
            dko[:, at] = dk[:tile]
            dvo[:, at] = dv[:tile]
            for which, (one, term) in enumerate(((dkf, dk), (dvf, dv))):
                rounded = term[tile:].astype(bf16)
                one[:, at] = rounded
                dfar[which, :, at] = rounded


def combine_kernel(near_ref, dko, dvo, mate, kn, vn, dk, dv):
    place = lax.axis_index("seq")
    last = lax.axis_size("seq") - 1
    other = place + 2 * (place & 1) - 1
    inside = (other >= 0) & (other <= last)
    from_mate = near_ref[0, place ^ 1] == place
    from_other = inside & (near_ref[0, jnp.clip(other, 0, last)] == place)
    for which, (own, beyond, out) in enumerate(((dko, kn, dk), (dvo, vn, dv))):
        total = own[...] + jnp.where(from_mate, mate[which].astype(f32), 0.0)
        out[...] = (total + jnp.where(from_other, beyond[...].astype(f32), 0.0)).astype(bf16)


def product_kernel(plan, layers, *refs):
    att = refs[: plan.pairs]
    cols, *outs, for_mate, gathered = refs[plan.pairs :]
    for t in range(plan.pairs):
        at = slice(t * HEAD_DIM, (t + 1) * HEAD_DIM)
        for core in range(2):
            for n, i in enumerate(layers):
                block = att[t][core, i * HEAD_DIM : (i + 1) * HEAD_DIM, :]
                gathered[core, n * HEAD_DIM : (n + 1) * HEAD_DIM, at] = block
    tokens, width = gathered.shape[2], cols.shape[2]
    step = 512 if width % 512 == 0 else width
    for c in range(0, width, step):
        block = cols[:, :, c : c + step].reshape(tokens, step)
        for n, out in enumerate(outs):
            rows = slice(n * HEAD_DIM, (n + 1) * HEAD_DIM)
            out[:, c : c + step] = dot_n(gathered[0, rows, :], block)
            for_mate[n, :, c : c + step] = dot_n(gathered[1, rows, :], block).astype(bf16)


def piece(ref, lead, start, size):
    at = slice(start, start + size)
    return (ref[:, at] if lead is None else ref[lead, :, at]).astype(f32)


def sum_kernel(spots, start, *refs):
    *parts, out = refs
    size = out.shape[1]
    total = None
    for (lead, first), part in zip(spots, parts, strict=True):
        value = piece(part, lead, start - first, size)
        total = value if total is None else total + value
    out[...] = total.astype(bf16)


def gram_kernel(spots, own, *refs):
    *parts, x, gram = refs
    x[...] = own[...]
    for (lead, first), part in zip(spots, parts, strict=True):
        size = part.shape[-1]
        x[:, first : first + size] += piece(part, lead, 0, size)
    gram[...] = exact(x[...], x[...], ((1,), (1,)))


def polynomial(gram):
    eye = (
        lax.broadcasted_iota(jnp.int32, gram.shape, 0)
        == lax.broadcasted_iota(jnp.int32, gram.shape, 1)
    ).astype(f32)
    square = jnp.sum(jnp.sum(gram * eye, axis=1, keepdims=True), axis=0, keepdims=True)
    inverse = 1.0 / (jnp.sqrt(square) + 1e-07)
    a = gram * inverse * inverse
    p = None
    for turn in range(NS_STEPS):
        q = coeff_a * eye + coeff_b * a + coeff_c * exact(a, a)
        p = q if p is None else exact(q, p)
        if turn + 1 < NS_STEPS:
            a = exact(exact(q, a), q)
    return p, inverse


def update_kernel(plan, factor, x, gram, gram_other, *outs):
    mine = plan.row_part(lax.axis_index("seq"))
    p, inverse = polynomial(gram[...] + gram_other[...])
    p = p * (inverse * factor)
    width = outs[0].shape[1]
    for j in range(plan.per_target):
        if width % HEAD_DIM == 0:
            block = x[:, pl.ds(pl.multiple_of((mine ^ j) * width, width), width)]
        else:
            block = jnp.zeros((HEAD_DIM, width), f32)
            for r in range(plan.per_target):
                part = x[:, r * width : (r + 1) * width]
                block = jnp.where((mine ^ j) == r, part, block)
        outs[j][...] = exact(p, block).astype(outs[j].dtype)


def place_kernel(plan, *refs):
    *parts, out = refs
    mine = plan.row_part(lax.axis_index("seq"))
    for j, part in enumerate(parts):
        at = pl.ds(pl.multiple_of((mine ^ j) * HEAD_DIM, HEAD_DIM), HEAD_DIM)
        out[at, :] = part[...].astype(f32)


def local(query_tiles, key_tiles, value_tiles, attn_grad, proj_grad, neighbour):
    tile, width = query_tiles.shape[2:]
    depth = proj_grad.shape[3]
    head_count = width // HEAD_DIM
    plan = Plan(head_count)
    n, m, per = plan.seq, plan.dp, plan.per_target
    place = lax.axis_index("seq")
    struct = jax.ShapeDtypeStruct
    query, key, value, grad = (
        a.reshape(tile, width) for a in (query_tiles, key_tiles, value_tiles, attn_grad)
    )

    steps = [(i, i + 1) for i in range(1, n - 1, 2)]
    back = [(j, i) for i, j in steps]
    takes = [(i, j) for i, j in steps if j != n - 2] + [(j, i) for j, i in back if i != 1]
    gives = [(i, j) for i, j in steps if i != 1] + [(j, i) for j, i in back if j != n - 2]
    key_next = lax.ppermute(key, "seq", takes)
    value_next = lax.ppermute(value, "seq", takes)
    key_mate = shift(key, "seq", 1)
    value_mate = shift(value, "seq", 1)
    beside = (key_mate, value_mate, key_next, value_next)

    slot = depth // n
    flat = proj_grad.reshape(tile, depth)
    mine = plan.col_part(place)
    mine_width = per * slot

    def column_part(part):
        return jnp.concatenate(
            [
                lax.dynamic_slice_in_dim(flat, (high * plan.col + part) * 2 * slot, 2 * slot, 1)
                for high in range(plan.high)
            ],
            1,
        )

    own_columns = column_part(mine)
    columns = [own_columns] + [
        shift(after(column_part(mine ^ q), key_next, value_next), "seq", q << 1)
        for q in range(1, plan.col)
    ]
    high_columns = [
        shift(after(own_columns, key_next, value_next), "seq", high << (1 + plan.col_bits))
        for high in range(1, plan.high)
    ]

    attended = pl.pallas_call(
        functools.partial(forward_kernel, plan),
        out_shape=struct((plan.high, 2, m * HEAD_DIM, tile), bf16),
        in_specs=[smem()] + whole(7),
        out_specs=pl.BlockSpec(memory_space=pltpu.VMEM),
        scratch_shapes=[pltpu.VMEM((2, tile, width), bf16)],
        compiler_params=params(),
        cost_estimate=cost(8 * tile * tile * width, 16 * tile * width, 2 * tile * tile * head_count),
        name="attention_forward",
    )(neighbour, query, key, value, *beside)

    pairs = [attended[0]] + [shift(attended[0], "seq", q << 1) for q in range(1, plan.col)]
    for high in range(1, plan.high):
        came_high = shift(attended[high], "seq", high << (1 + plan.col_bits))
        pairs.append(came_high)
        there = after(came_high, *pairs[1 : plan.col])
        pairs += [shift(there, "seq", q << 1) for q in range(1, plan.col)]

    through = after(jnp.stack(columns[1:]), attended, *high_columns)
    held = [jnp.stack(columns)]
    for high in range(1, plan.high):
        rest = jnp.concatenate(
            [shift(part, "seq", high << (1 + plan.col_bits)) for part in jnp.split(through, 2, 2)], 2
        )
        held.append(jnp.concatenate([high_columns[high - 1][None], rest], 0))
    held = jnp.concatenate(held, 0)

    def product(name, layers, *operands):
        *blocks, for_mate = pl.pallas_call(
            functools.partial(product_kernel, plan, layers),
            out_shape=[struct((HEAD_DIM, mine_width), f32)] * len(layers)
            + [struct((len(layers), HEAD_DIM, mine_width), bf16)],
            in_specs=whole(plan.pairs + 1),
            out_specs=whole(len(layers) + 1),
            scratch_shapes=[pltpu.VMEM((2, len(layers) * HEAD_DIM, plan.pairs * tile), bf16)],
            compiler_params=params(),
            cost_estimate=cost(
                2 * len(layers) * HEAD_DIM * n * tile * mine_width, n * tile * mine_width
            ),
            name=name,
        )(*operands)
        mate = shift(for_mate, "seq", 1)
        return {i: [(block, None, 0), (mate, k, 0)] for k, (i, block) in enumerate(zip(layers, blocks))}

    def added(parts, start, size):
        return pl.pallas_call(
            functools.partial(sum_kernel, [spot for _, *spot in parts], start),
            out_shape=struct((HEAD_DIM, size), bf16),
            in_specs=whole(len(parts)),
            out_specs=pl.BlockSpec(memory_space=pltpu.VMEM),
            compiler_params=params(),
            cost_estimate=cost(len(parts) * HEAD_DIM * size, 4 * len(parts) * HEAD_DIM * size),
            name="block_sum",
        )(*[array for array, *_ in parts])

    first = [i for i in range(m - 1, 1, -1) if i & 1]
    middle = [i for i in range(m - 1, 1, -1) if not i & 1]
    blocks = product("product_first", first, *pairs, held)
    going = {i: added(blocks[i], 0, mine_width) for i in first}
    blocks |= product("product_middle", middle, after(pairs[0], *going.values()), *pairs[1:], held)

    dq, dko, dvo, dkf, dvf, dfar = pl.pallas_call(
        backward_kernel,
        out_shape=[
            struct((tile, width), bf16),
            struct((tile, width), f32),
            struct((tile, width), f32),
            struct((tile, width), bf16),
            struct((tile, width), bf16),
            struct((2, tile, width), bf16),
        ],
        in_specs=[smem()] + whole(8),
        out_specs=whole(6),
        scratch_shapes=[pltpu.VMEM((2, tile, width), bf16)],
        compiler_params=params(),
        cost_estimate=cost(28 * tile * tile * width, 30 * tile * width, 2 * tile * tile * head_count),
        name="attention_backward",
    )(neighbour, query, key, value, *beside, after(grad, *going.values()))

    blocks |= product("product_near", [1], after(pairs[0], dq), *pairs[1:], held)
    blocks |= product("product_own", [0], after(pairs[0], dq), *pairs[1:], held)

    extra = {i: [] for i in range(m)}
    sent = []
    bit = 1
    while bit < m:
        for i in range(m - 1, 1, -1):
            if i & -i == bit:
                if bit == 1:
                    sent.append(going[i])
                else:
                    (block, *where), *others = blocks[i] + extra[i]
                    sent.append(added([(after(block, dq), *where)] + others, 0, mine_width))
                extra[i ^ bit].append((shift(sent[-1], "dp", bit), None, 0))
        bit *= 2
    near = shift(after(added(blocks[1], 0, mine_width), sent[-1], blocks[0][1][0]), "dp", 1)
    own = blocks[0][0][0]
    came = [blocks[0][1], (near, None, 0)] + extra[0]

    x, gram = pl.pallas_call(
        functools.partial(gram_kernel, [spot for _, *spot in came]),
        out_shape=[struct((HEAD_DIM, mine_width), f32), struct((HEAD_DIM, HEAD_DIM), f32)],
        in_specs=whole(1 + len(came)),
        out_specs=whole(2),
        compiler_params=params(),
        cost_estimate=cost(12 * HEAD_DIM * HEAD_DIM * mine_width, 14 * HEAD_DIM * mine_width),
        name="gradient_sum",
    )(own, *[array for array, *_ in came])

    gram_other = jnp.zeros_like(gram)
    for b in range(plan.col_bits):
        gram = gram + gram_other
        gram_other = shift(gram, "seq", 2 << b)

    factor = 0.2 * depth**0.5
    pieces = pl.pallas_call(
        functools.partial(update_kernel, plan, factor),
        out_shape=[struct((HEAD_DIM, slot), f32)] + [struct((HEAD_DIM, slot), bf16)] * (per - 1),
        in_specs=whole(3),
        out_specs=whole(per),
        compiler_params=params(),
        cost_estimate=cost(12 * HEAD_DIM * HEAD_DIM * mine_width, 8 * HEAD_DIM * mine_width),
        name="newton_schulz",
    )(x, gram, gram_other)
    dkf, dvf, dfar = (after(part, sent[-1]) for part in (dkf, dvf, dfar))
    dk, dv = pl.pallas_call(
        combine_kernel,
        out_shape=[struct((tile, width), bf16)] * 2,
        in_specs=[smem()] + whole(5),
        out_specs=whole(2),
        compiler_params=params(),
        cost_estimate=cost(6 * tile * width, 20 * tile * width),
        name="key_value_sum",
    )(
        neighbour,
        dko,
        dvo,
        shift(dfar, "seq", 1),
        lax.ppermute(dkf, "seq", gives),
        lax.ppermute(dvf, "seq", gives),
    )

    pieces = [pieces[0]] + [
        shift(pieces[j], "seq", plan.row_mask(j)) for j in range(1, per)
    ]
    update = pl.pallas_call(
        functools.partial(place_kernel, plan),
        out_shape=struct((per * HEAD_DIM, slot), f32),
        in_specs=whole(per),
        out_specs=pl.BlockSpec(memory_space=pltpu.VMEM),
        compiler_params=params(),
        cost_estimate=cost(1, 8 * per * HEAD_DIM * slot),
        name="update_rows",
    )(*pieces)

    shape = query_tiles.shape
    return dq.reshape(shape), dk.reshape(shape), dv.reshape(shape), update


def solution(mesh):
    tiles = P("dp", "seq", None, None)
    return jax.shard_map(
        local,
        mesh=mesh,
        in_specs=(tiles, tiles, tiles, tiles, tiles, P("dp", None)),
        out_specs=(tiles, tiles, tiles, P("dp", "seq")),
        check_vma=False,
    )
```

```python
import functools
import math

import jax
import jax.numpy as jnp
from jax import lax
from jax.experimental import pallas as pl
from jax.experimental.pallas import tpu as pltpu
from jax.sharding import PartitionSpec as P

HEAD_DIM = 128
NS_STEPS = 5
SCALE = HEAD_DIM ** (-0.5)
LOG2E = math.log2(math.e)
GROUP = 4
coeff_a = 3.4445
coeff_b = -4.775
coeff_c = 2.0315
f32 = jnp.float32
bf16 = jnp.bfloat16
VMEM_LIMIT = 24 * 1024 * 1024


def whole(count):
    return [pl.BlockSpec(memory_space=pltpu.VMEM)] * count


def smem():
    return pl.BlockSpec(memory_space=pltpu.SMEM)


def params():
    return pltpu.CompilerParams(vmem_limit_bytes=VMEM_LIMIT)


def cost(flops, moved, exps=0):
    return pl.CostEstimate(flops=int(flops), bytes_accessed=int(moved), transcendentals=int(exps))


def dot_t(a, b):
    return lax.dot_general(a, b, (((1,), (1,)), ((), ())), preferred_element_type=f32)


def dot_n(a, b):
    return lax.dot_general(a, b, (((1,), (0,)), ((), ())), preferred_element_type=f32)


def dot_l(a, b):
    return lax.dot_general(a, b, (((0,), (0,)), ((), ())), preferred_element_type=f32)


def exact(a, b, dims=((1,), (0,))):
    return lax.dot_general(
        a, b, (dims, ((), ())), precision=lax.Precision.HIGHEST, preferred_element_type=f32
    )


class Plan:
    def __init__(self, head_count):
        self.seq = lax.axis_size("seq")
        self.dp = lax.axis_size("dp")
        self.per_target = head_count // self.dp
        self.high = self.per_target // 2
        self.col = self.seq // self.per_target
        self.col_bits = self.col.bit_length() - 1
        self.pairs = self.seq // 2

    def row_part(self, place):
        return (place >> (1 + self.col_bits)) * 2 + (place & 1)

    def row_mask(self, part):
        return ((part >> 1) << (1 + self.col_bits)) | (part & 1)

    def col_part(self, place):
        return (place >> 1) & (self.col - 1)


def after(value, *others):
    return lax.optimization_barrier((value, *others))[0]


def shift(value, axis, mask):
    return lax.ppermute(value, axis, [(i, i ^ mask) for i in range(lax.axis_size(axis))])


def head_slice(index):
    return pl.ds(pl.multiple_of(index * HEAD_DIM, HEAD_DIM), HEAD_DIM)


def softmax_keys(query, keys):
    scores = dot_t(keys, query)
    top = jnp.max(scores, axis=0, keepdims=True)
    powers = jnp.exp2((scores - top) * (SCALE * LOG2E))
    return powers * (1.0 / jnp.sum(powers, axis=0, keepdims=True))


def choose_far(near_ref, key_mate, value_mate, key_next, value_next, far):
    place = lax.axis_index("seq")
    is_mate = near_ref[0, place] == (place ^ 1)

    @pl.when(is_mate)
    def _():
        far[0] = key_mate[...]
        far[1] = value_mate[...]

    @pl.when(jnp.logical_not(is_mate))
    def _():
        far[0] = key_next[...]
        far[1] = value_next[...]


def forward_kernel(plan, near_ref, q, ko, vo, km, vm, kn, vn, out, far):
    layer = lax.axis_index("dp")
    choose_far(near_ref, km, vm, kn, vn, far)
    mine = plan.row_part(lax.axis_index("seq"))
    jobs = [(j, i) for j in range(plan.per_target) for i in range(plan.dp)]
    for first in range(0, len(jobs), GROUP):
        group = jobs[first : first + GROUP]
        spots = [head_slice((layer ^ i) * plan.per_target + (mine ^ j)) for j, i in group]
        weights = [
            softmax_keys(q[:, at], jnp.concatenate([ko[:, at], far[0, :, at]], 0)).astype(bf16)
            for at in spots
        ]
        for (j, i), at, p in zip(group, spots, weights, strict=True):
            values = jnp.concatenate([vo[:, at], far[1, :, at]], 0)
            rows = slice(i * HEAD_DIM, (i + 1) * HEAD_DIM)
            out[j >> 1, j & 1, rows, :] = dot_l(values, p).astype(bf16)


def backward_kernel(near_ref, q, ko, vo, km, vm, kn, vn, g, dq, dko, dvo, dkf, dvf, dfar, far):
    choose_far(near_ref, km, vm, kn, vn, far)
    tile = q.shape[0]
    count = q.shape[1] // HEAD_DIM
    for first in range(0, count, GROUP):
        spots = [
            slice(h * HEAD_DIM, (h + 1) * HEAD_DIM)
            for h in range(first, min(first + GROUP, count))
        ]
        weights, slopes = [], []
        for at in spots:
            values = jnp.concatenate([vo[:, at], far[1, :, at]], 0)
            keys = jnp.concatenate([ko[:, at], far[0, :, at]], 0)
            weights.append(softmax_keys(q[:, at], keys))
            slopes.append(dot_t(values, g[:, at]))
        for at, p, dp in zip(spots, weights, slopes, strict=True):
            pb = p.astype(bf16)
            delta = jnp.sum(pb.astype(f32) * dp, axis=0, keepdims=True)
            ds = (p * (dp - delta)).astype(bf16)
            keys = jnp.concatenate([ko[:, at], far[0, :, at]], 0)
            dk = dot_n(ds, q[:, at]) * SCALE
            dv = dot_n(pb, g[:, at])
            dq[:, at] = (dot_l(ds, keys) * SCALE).astype(bf16)
            dko[:, at] = dk[:tile]
            dvo[:, at] = dv[:tile]
            for which, (one, term) in enumerate(((dkf, dk), (dvf, dv))):
                rounded = term[tile:].astype(bf16)
                one[:, at] = rounded
                dfar[which, :, at] = rounded


def combine_kernel(near_ref, dko, dvo, mate, kn, vn, dk, dv):
    place = lax.axis_index("seq")
    last = lax.axis_size("seq") - 1
    other = place + 2 * (place & 1) - 1
    inside = (other >= 0) & (other <= last)
    from_mate = near_ref[0, place ^ 1] == place
    from_other = inside & (near_ref[0, jnp.clip(other, 0, last)] == place)
    for which, (own, beyond, out) in enumerate(((dko, kn, dk), (dvo, vn, dv))):
        total = own[...] + jnp.where(from_mate, mate[which].astype(f32), 0.0)
        out[...] = (total + jnp.where(from_other, beyond[...].astype(f32), 0.0)).astype(bf16)


def product_kernel(plan, layers, *refs):
    att = refs[: plan.pairs]
    cols, *outs, for_mate, gathered = refs[plan.pairs :]
    for t in range(plan.pairs):
        at = slice(t * HEAD_DIM, (t + 1) * HEAD_DIM)
        for core in range(2):
            for n, i in enumerate(layers):
                block = att[t][core, i * HEAD_DIM : (i + 1) * HEAD_DIM, :]
                gathered[core, n * HEAD_DIM : (n + 1) * HEAD_DIM, at] = block
    tokens, width = gathered.shape[2], cols.shape[2]
    step = 512 if width % 512 == 0 else width
    for c in range(0, width, step):
        block = cols[:, :, c : c + step].reshape(tokens, step)
        for n, out in enumerate(outs):
            rows = slice(n * HEAD_DIM, (n + 1) * HEAD_DIM)
            out[:, c : c + step] = dot_n(gathered[0, rows, :], block)
            for_mate[n, :, c : c + step] = dot_n(gathered[1, rows, :], block).astype(bf16)


def piece(ref, lead, start, size):
    at = slice(start, start + size)
    return (ref[:, at] if lead is None else ref[lead, :, at]).astype(f32)


def sum_kernel(spots, start, *refs):
    *parts, out = refs
    size = out.shape[1]
    total = None
    for (lead, first), part in zip(spots, parts, strict=True):
        value = piece(part, lead, start - first, size)
        total = value if total is None else total + value
    out[...] = total.astype(bf16)


def gram_kernel(spots, own, *refs):
    *parts, x, gram = refs
    x[...] = own[...]
    for (lead, first), part in zip(spots, parts, strict=True):
        size = part.shape[-1]
        x[:, first : first + size] += piece(part, lead, 0, size)
    gram[...] = exact(x[...], x[...], ((1,), (1,)))


def polynomial(gram):
    eye = (
        lax.broadcasted_iota(jnp.int32, gram.shape, 0)
        == lax.broadcasted_iota(jnp.int32, gram.shape, 1)
    ).astype(f32)
    square = jnp.sum(jnp.sum(gram * eye, axis=1, keepdims=True), axis=0, keepdims=True)
    inverse = 1.0 / (jnp.sqrt(square) + 1e-07)
    a = gram * inverse * inverse
    p = None
    for turn in range(NS_STEPS):
        q = coeff_a * eye + coeff_b * a + coeff_c * exact(a, a)
        p = q if p is None else exact(q, p)
        if turn + 1 < NS_STEPS:
            a = exact(exact(q, a), q)
    return p, inverse


def update_kernel(plan, factor, x, gram, gram_other, *outs):
    mine = plan.row_part(lax.axis_index("seq"))
    p, inverse = polynomial(gram[...] + gram_other[...])
    p = p * (inverse * factor)
    width = outs[0].shape[1]
    for j in range(plan.per_target):
        if width % HEAD_DIM == 0:
            block = x[:, pl.ds(pl.multiple_of((mine ^ j) * width, width), width)]
        else:
            block = jnp.zeros((HEAD_DIM, width), f32)
            for r in range(plan.per_target):
                part = x[:, r * width : (r + 1) * width]
                block = jnp.where((mine ^ j) == r, part, block)
        outs[j][...] = exact(p, block).astype(outs[j].dtype)


def place_kernel(plan, *refs):
    *parts, out = refs
    mine = plan.row_part(lax.axis_index("seq"))
    for j, part in enumerate(parts):
        at = pl.ds(pl.multiple_of((mine ^ j) * HEAD_DIM, HEAD_DIM), HEAD_DIM)
        out[at, :] = part[...].astype(f32)


def local(query_tiles, key_tiles, value_tiles, attn_grad, proj_grad, neighbour):
    tile, width = query_tiles.shape[2:]
    depth = proj_grad.shape[3]
    head_count = width // HEAD_DIM
    plan = Plan(head_count)
    n, m, per = plan.seq, plan.dp, plan.per_target
    place = lax.axis_index("seq")
    struct = jax.ShapeDtypeStruct
    query, key, value, grad = (
        a.reshape(tile, width) for a in (query_tiles, key_tiles, value_tiles, attn_grad)
    )

    steps = [(i, i + 1) for i in range(1, n - 1, 2)]
    back = [(j, i) for i, j in steps]
    takes = [(i, j) for i, j in steps if j != n - 2] + [(j, i) for j, i in back if i != 1]
    gives = [(i, j) for i, j in steps if i != 1] + [(j, i) for j, i in back if j != n - 2]
    key_next = lax.ppermute(key, "seq", takes)
    value_next = lax.ppermute(value, "seq", takes)
    key_mate = shift(key, "seq", 1)
    value_mate = shift(value, "seq", 1)
    beside = (key_mate, value_mate, key_next, value_next)

    slot = depth // n
    flat = proj_grad.reshape(tile, depth)
    mine = plan.col_part(place)
    mine_width = per * slot

    def column_part(part):
        return jnp.concatenate(
            [
                lax.dynamic_slice_in_dim(flat, (high * plan.col + part) * 2 * slot, 2 * slot, 1)
                for high in range(plan.high)
            ],
            1,
        )

    own_columns = column_part(mine)
    columns = [own_columns] + [
        shift(after(column_part(mine ^ q), key_next, value_next), "seq", q << 1)
        for q in range(1, plan.col)
    ]
    high_columns = [
        shift(after(own_columns, key_next, value_next), "seq", high << (1 + plan.col_bits))
        for high in range(1, plan.high)
    ]

    attended = pl.pallas_call(
        functools.partial(forward_kernel, plan),
        out_shape=struct((plan.high, 2, m * HEAD_DIM, tile), bf16),
        in_specs=[smem()] + whole(7),
        out_specs=pl.BlockSpec(memory_space=pltpu.VMEM),
        scratch_shapes=[pltpu.VMEM((2, tile, width), bf16)],
        compiler_params=params(),
        cost_estimate=cost(8 * tile * tile * width, 16 * tile * width, 2 * tile * tile * head_count),
        name="attention_forward",
    )(neighbour, query, key, value, *beside)

    pairs = [attended[0]] + [shift(attended[0], "seq", q << 1) for q in range(1, plan.col)]
    for high in range(1, plan.high):
        came_high = shift(attended[high], "seq", high << (1 + plan.col_bits))
        pairs.append(came_high)
        there = after(came_high, *pairs[1 : plan.col])
        pairs += [shift(there, "seq", q << 1) for q in range(1, plan.col)]

    through = after(jnp.stack(columns[1:]), attended, *high_columns)
    held = [jnp.stack(columns)]
    late = []
    for high in range(1, plan.high):
        halves = [shift(part, "seq", high << (1 + plan.col_bits)) for part in jnp.split(through, 2, 2)]
        late.append(halves[0])
        rest = jnp.concatenate(halves, 2)
        held.append(jnp.concatenate([high_columns[high - 1][None], rest], 0))
    held = jnp.concatenate(held, 0)

    dq, dko, dvo, dkf, dvf, dfar = pl.pallas_call(
        backward_kernel,
        out_shape=[
            struct((tile, width), bf16),
            struct((tile, width), f32),
            struct((tile, width), f32),
            struct((tile, width), bf16),
            struct((tile, width), bf16),
            struct((2, tile, width), bf16),
        ],
        in_specs=[smem()] + whole(8),
        out_specs=whole(6),
        scratch_shapes=[pltpu.VMEM((2, tile, width), bf16)],
        compiler_params=params(),
        cost_estimate=cost(28 * tile * tile * width, 30 * tile * width, 2 * tile * tile * head_count),
        name="attention_backward",
    )(neighbour, query, key, value, *beside, after(grad, *late))

    def product(name, layers, *operands):
        *blocks, for_mate = pl.pallas_call(
            functools.partial(product_kernel, plan, layers),
            out_shape=[struct((HEAD_DIM, mine_width), f32)] * len(layers)
            + [struct((len(layers), HEAD_DIM, mine_width), bf16)],
            in_specs=whole(plan.pairs + 1),
            out_specs=whole(len(layers) + 1),
            scratch_shapes=[pltpu.VMEM((2, len(layers) * HEAD_DIM, plan.pairs * tile), bf16)],
            compiler_params=params(),
            cost_estimate=cost(
                2 * len(layers) * HEAD_DIM * n * tile * mine_width, n * tile * mine_width
            ),
            name=name,
        )(*operands)
        mate = shift(for_mate, "seq", 1)
        return {i: [(block, None, 0), (mate, k, 0)] for k, (i, block) in enumerate(zip(layers, blocks))}

    def added(parts, start, size):
        return pl.pallas_call(
            functools.partial(sum_kernel, [spot for _, *spot in parts], start),
            out_shape=struct((HEAD_DIM, size), bf16),
            in_specs=whole(len(parts)),
            out_specs=pl.BlockSpec(memory_space=pltpu.VMEM),
            compiler_params=params(),
            cost_estimate=cost(len(parts) * HEAD_DIM * size, 4 * len(parts) * HEAD_DIM * size),
            name="block_sum",
        )(*[array for array, *_ in parts])

    first = [i for i in range(m - 1, 1, -1) if i & 1]
    middle = [i for i in range(m - 1, 1, -1) if not i & 1]
    blocks = product("product_first", first, after(pairs[0], dq), *pairs[1:], held)
    going = {i: added(blocks[i], 0, mine_width) for i in first}
    blocks |= product("product_middle", middle, after(pairs[0], *going.values()), *pairs[1:], held)

    blocks |= product("product_near", [1], after(pairs[0], dq), *pairs[1:], held)
    blocks |= product("product_own", [0], after(pairs[0], dq), *pairs[1:], held)

    extra = {i: [] for i in range(m)}
    sent = []
    bit = 1
    while bit < m:
        for i in range(m - 1, 1, -1):
            if i & -i == bit:
                if bit == 1:
                    sent.append(going[i])
                else:
                    (block, *where), *others = blocks[i] + extra[i]
                    sent.append(added([(after(block, dq), *where)] + others, 0, mine_width))
                extra[i ^ bit].append((shift(sent[-1], "dp", bit), None, 0))
        bit *= 2
    near = shift(after(added(blocks[1], 0, mine_width), sent[-1], blocks[0][1][0]), "dp", 1)
    own = blocks[0][0][0]
    came = [blocks[0][1], (near, None, 0)] + extra[0]

    far = [
        shift(after(dfar, dq), "seq", 1),
        lax.ppermute(after(dkf, dq), "seq", gives),
        lax.ppermute(after(dvf, dq), "seq", gives),
    ]
    dk, dv = pl.pallas_call(
        combine_kernel,
        out_shape=[struct((tile, width), bf16)] * 2,
        in_specs=[smem()] + whole(5),
        out_specs=whole(2),
        compiler_params=params(),
        cost_estimate=cost(6 * tile * width, 20 * tile * width),
        name="key_value_sum",
    )(
        neighbour,
        dko,
        dvo,
        *far,
    )

    x, gram = pl.pallas_call(
        functools.partial(gram_kernel, [spot for _, *spot in came]),
        out_shape=[struct((HEAD_DIM, mine_width), f32), struct((HEAD_DIM, HEAD_DIM), f32)],
        in_specs=whole(1 + len(came)),
        out_specs=whole(2),
        compiler_params=params(),
        cost_estimate=cost(12 * HEAD_DIM * HEAD_DIM * mine_width, 14 * HEAD_DIM * mine_width),
        name="gradient_sum",
    )(own, *[array for array, *_ in came])

    gram_other = jnp.zeros_like(gram)
    for b in range(plan.col_bits):
        gram = gram + gram_other
        gram_other = shift(gram, "seq", 2 << b)

    factor = 0.2 * depth**0.5
    pieces = pl.pallas_call(
        functools.partial(update_kernel, plan, factor),
        out_shape=[struct((HEAD_DIM, slot), f32)] + [struct((HEAD_DIM, slot), bf16)] * (per - 1),
        in_specs=whole(3),
        out_specs=whole(per),
        compiler_params=params(),
        cost_estimate=cost(12 * HEAD_DIM * HEAD_DIM * mine_width, 8 * HEAD_DIM * mine_width),
        name="newton_schulz",
    )(after(x, dk), gram, gram_other)
    pieces = [pieces[0]] + [
        shift(pieces[j], "seq", plan.row_mask(j)) for j in range(1, per)
    ]
    update = pl.pallas_call(
        functools.partial(place_kernel, plan),
        out_shape=struct((per * HEAD_DIM, slot), f32),
        in_specs=whole(per),
        out_specs=pl.BlockSpec(memory_space=pltpu.VMEM),
        compiler_params=params(),
        cost_estimate=cost(1, 8 * per * HEAD_DIM * slot),
        name="update_rows",
    )(*pieces)

    shape = query_tiles.shape
    return dq.reshape(shape), dk.reshape(shape), dv.reshape(shape), update


def solution(mesh):
    tiles = P("dp", "seq", None, None)
    return jax.shard_map(
        local,
        mesh=mesh,
        in_specs=(tiles, tiles, tiles, tiles, tiles, P("dp", None)),
        out_specs=(tiles, tiles, tiles, P("dp", "seq")),
        check_vma=False,
    )
```

```python
import functools
import math

import jax
import jax.numpy as jnp
from jax import lax
from jax.experimental import pallas as pl
from jax.experimental.pallas import tpu as pltpu
from jax.sharding import PartitionSpec as P

HEAD_DIM = 128
NS_STEPS = 5
SCALE = HEAD_DIM ** (-0.5)
LOG2E = math.log2(math.e)
GROUP = 4
coeff_a = 3.4445
coeff_b = -4.775
coeff_c = 2.0315
f32 = jnp.float32
bf16 = jnp.bfloat16
VMEM_LIMIT = 24 * 1024 * 1024


def whole(count):
    return [pl.BlockSpec(memory_space=pltpu.VMEM)] * count


def smem():
    return pl.BlockSpec(memory_space=pltpu.SMEM)


def params():
    return pltpu.CompilerParams(vmem_limit_bytes=VMEM_LIMIT)


def cost(flops, moved, exps=0):
    return pl.CostEstimate(flops=int(flops), bytes_accessed=int(moved), transcendentals=int(exps))


def dot_t(a, b):
    return lax.dot_general(a, b, (((1,), (1,)), ((), ())), preferred_element_type=f32)


def dot_n(a, b):
    return lax.dot_general(a, b, (((1,), (0,)), ((), ())), preferred_element_type=f32)


def dot_l(a, b):
    return lax.dot_general(a, b, (((0,), (0,)), ((), ())), preferred_element_type=f32)


def exact(a, b, dims=((1,), (0,))):
    return lax.dot_general(
        a, b, (dims, ((), ())), precision=lax.Precision.HIGHEST, preferred_element_type=f32
    )


class Plan:
    def __init__(self, head_count):
        self.seq = lax.axis_size("seq")
        self.dp = lax.axis_size("dp")
        self.per_target = head_count // self.dp
        self.high = self.per_target // 2
        self.col = self.seq // self.per_target
        self.col_bits = self.col.bit_length() - 1
        self.pairs = self.seq // 2

    def row_part(self, place):
        return (place >> (1 + self.col_bits)) * 2 + (place & 1)

    def row_mask(self, part):
        return ((part >> 1) << (1 + self.col_bits)) | (part & 1)

    def col_part(self, place):
        return (place >> 1) & (self.col - 1)


def after(value, *others):
    return lax.optimization_barrier((value, *others))[0]


def shift(value, axis, mask):
    return lax.ppermute(value, axis, [(i, i ^ mask) for i in range(lax.axis_size(axis))])


def head_slice(index):
    return pl.ds(pl.multiple_of(index * HEAD_DIM, HEAD_DIM), HEAD_DIM)


def softmax_keys(query, keys):
    scores = dot_t(keys, query)
    top = jnp.max(scores, axis=0, keepdims=True)
    powers = jnp.exp2((scores - top) * (SCALE * LOG2E))
    return powers * (1.0 / jnp.sum(powers, axis=0, keepdims=True))


def choose_far(near_ref, key_mate, value_mate, key_next, value_next, far):
    place = lax.axis_index("seq")
    is_mate = near_ref[0, place] == (place ^ 1)

    @pl.when(is_mate)
    def _():
        far[0] = key_mate[...]
        far[1] = value_mate[...]

    @pl.when(jnp.logical_not(is_mate))
    def _():
        far[0] = key_next[...]
        far[1] = value_next[...]


def forward_kernel(plan, near_ref, q, ko, vo, km, vm, kn, vn, out, far):
    layer = lax.axis_index("dp")
    choose_far(near_ref, km, vm, kn, vn, far)
    mine = plan.row_part(lax.axis_index("seq"))
    jobs = [(j, i) for j in range(plan.per_target) for i in range(plan.dp)]
    for first in range(0, len(jobs), GROUP):
        group = jobs[first : first + GROUP]
        spots = [head_slice((layer ^ i) * plan.per_target + (mine ^ j)) for j, i in group]
        weights = [
            softmax_keys(q[:, at], jnp.concatenate([ko[:, at], far[0, :, at]], 0)).astype(bf16)
            for at in spots
        ]
        for (j, i), at, p in zip(group, spots, weights, strict=True):
            values = jnp.concatenate([vo[:, at], far[1, :, at]], 0)
            rows = slice(i * HEAD_DIM, (i + 1) * HEAD_DIM)
            out[j >> 1, j & 1, rows, :] = dot_l(values, p).astype(bf16)


def backward_kernel(near_ref, q, ko, vo, km, vm, kn, vn, g, dq, dko, dvo, dkf, dvf, dfar, far):
    choose_far(near_ref, km, vm, kn, vn, far)
    tile = q.shape[0]
    count = q.shape[1] // HEAD_DIM
    for first in range(0, count, GROUP):
        spots = [
            slice(h * HEAD_DIM, (h + 1) * HEAD_DIM)
            for h in range(first, min(first + GROUP, count))
        ]
        weights, slopes = [], []
        for at in spots:
            values = jnp.concatenate([vo[:, at], far[1, :, at]], 0)
            keys = jnp.concatenate([ko[:, at], far[0, :, at]], 0)
            weights.append(softmax_keys(q[:, at], keys))
            slopes.append(dot_t(values, g[:, at]))
        for at, p, dp in zip(spots, weights, slopes, strict=True):
            pb = p.astype(bf16)
            delta = jnp.sum(pb.astype(f32) * dp, axis=0, keepdims=True)
            ds = (p * (dp - delta)).astype(bf16)
            keys = jnp.concatenate([ko[:, at], far[0, :, at]], 0)
            dk = dot_n(ds, q[:, at]) * SCALE
            dv = dot_n(pb, g[:, at])
            dq[:, at] = (dot_l(ds, keys) * SCALE).astype(bf16)
            dko[:, at] = dk[:tile]
            dvo[:, at] = dv[:tile]
            for which, (one, term) in enumerate(((dkf, dk), (dvf, dv))):
                rounded = term[tile:].astype(bf16)
                one[:, at] = rounded
                dfar[which, :, at] = rounded


def combine_kernel(near_ref, dko, dvo, mate, kn, vn, dk, dv):
    place = lax.axis_index("seq")
    last = lax.axis_size("seq") - 1
    other = place + 2 * (place & 1) - 1
    inside = (other >= 0) & (other <= last)
    from_mate = near_ref[0, place ^ 1] == place
    from_other = inside & (near_ref[0, jnp.clip(other, 0, last)] == place)
    for which, (own, beyond, out) in enumerate(((dko, kn, dk), (dvo, vn, dv))):
        total = own[...] + jnp.where(from_mate, mate[which].astype(f32), 0.0)
        out[...] = (total + jnp.where(from_other, beyond[...].astype(f32), 0.0)).astype(bf16)


def product_kernel(plan, layers, *refs):
    att = refs[: plan.pairs]
    cols, *outs, for_mate, gathered = refs[plan.pairs :]
    for t in range(plan.pairs):
        at = slice(t * HEAD_DIM, (t + 1) * HEAD_DIM)
        for core in range(2):
            for n, i in enumerate(layers):
                block = att[t][core, i * HEAD_DIM : (i + 1) * HEAD_DIM, :]
                gathered[core, n * HEAD_DIM : (n + 1) * HEAD_DIM, at] = block
    tokens, width = gathered.shape[2], cols.shape[2]
    step = 512 if width % 512 == 0 else width
    for c in range(0, width, step):
        block = cols[:, :, c : c + step].reshape(tokens, step)
        for n, out in enumerate(outs):
            rows = slice(n * HEAD_DIM, (n + 1) * HEAD_DIM)
            out[:, c : c + step] = dot_n(gathered[0, rows, :], block)
            for_mate[n, :, c : c + step] = dot_n(gathered[1, rows, :], block).astype(bf16)


def piece(ref, lead, start, size):
    at = slice(start, start + size)
    return (ref[:, at] if lead is None else ref[lead, :, at]).astype(f32)


def sum_kernel(spots, start, *refs):
    *parts, out = refs
    size = out.shape[1]
    total = None
    for (lead, first), part in zip(spots, parts, strict=True):
        value = piece(part, lead, start - first, size)
        total = value if total is None else total + value
    out[...] = total.astype(bf16)


def gram_kernel(spots, own, *refs):
    *parts, x, gram = refs
    x[...] = own[...]
    for (lead, first), part in zip(spots, parts, strict=True):
        size = part.shape[-1]
        x[:, first : first + size] += piece(part, lead, 0, size)
    gram[...] = exact(x[...], x[...], ((1,), (1,)))


def polynomial(gram):
    eye = (
        lax.broadcasted_iota(jnp.int32, gram.shape, 0)
        == lax.broadcasted_iota(jnp.int32, gram.shape, 1)
    ).astype(f32)
    square = jnp.sum(jnp.sum(gram * eye, axis=1, keepdims=True), axis=0, keepdims=True)
    inverse = 1.0 / (jnp.sqrt(square) + 1e-07)
    a = gram * inverse * inverse
    p = None
    for turn in range(NS_STEPS):
        q = coeff_a * eye + coeff_b * a + coeff_c * exact(a, a)
        p = q if p is None else exact(q, p)
        if turn + 1 < NS_STEPS:
            a = exact(exact(q, a), q)
    return p, inverse


def update_kernel(plan, factor, x, gram, gram_other, *outs):
    mine = plan.row_part(lax.axis_index("seq"))
    p, inverse = polynomial(gram[...] + gram_other[...])
    p = p * (inverse * factor)
    width = outs[0].shape[1]
    for j in range(plan.per_target):
        if width % HEAD_DIM == 0:
            block = x[:, pl.ds(pl.multiple_of((mine ^ j) * width, width), width)]
        else:
            block = jnp.zeros((HEAD_DIM, width), f32)
            for r in range(plan.per_target):
                part = x[:, r * width : (r + 1) * width]
                block = jnp.where((mine ^ j) == r, part, block)
        outs[j][...] = exact(p, block).astype(outs[j].dtype)


def place_kernel(plan, *refs):
    *parts, out = refs
    mine = plan.row_part(lax.axis_index("seq"))
    for j, part in enumerate(parts):
        at = pl.ds(pl.multiple_of((mine ^ j) * HEAD_DIM, HEAD_DIM), HEAD_DIM)
        out[at, :] = part[...].astype(f32)


def local(query_tiles, key_tiles, value_tiles, attn_grad, proj_grad, neighbour):
    tile, width = query_tiles.shape[2:]
    depth = proj_grad.shape[3]
    head_count = width // HEAD_DIM
    plan = Plan(head_count)
    n, m, per = plan.seq, plan.dp, plan.per_target
    place = lax.axis_index("seq")
    struct = jax.ShapeDtypeStruct
    query, key, value, grad = (
        a.reshape(tile, width) for a in (query_tiles, key_tiles, value_tiles, attn_grad)
    )

    steps = [(i, i + 1) for i in range(1, n - 1, 2)]
    back = [(j, i) for i, j in steps]
    takes = [(i, j) for i, j in steps if j != n - 2] + [(j, i) for j, i in back if i != 1]
    gives = [(i, j) for i, j in steps if i != 1] + [(j, i) for j, i in back if j != n - 2]
    key_next = lax.ppermute(key, "seq", takes)
    value_next = lax.ppermute(value, "seq", takes)
    key_mate = shift(key, "seq", 1)
    value_mate = shift(value, "seq", 1)
    beside = (key_mate, value_mate, key_next, value_next)

    slot = depth // n
    flat = proj_grad.reshape(tile, depth)
    mine = plan.col_part(place)
    mine_width = per * slot

    def column_part(part):
        return jnp.concatenate(
            [
                lax.dynamic_slice_in_dim(flat, (high * plan.col + part) * 2 * slot, 2 * slot, 1)
                for high in range(plan.high)
            ],
            1,
        )

    own_columns = column_part(mine)
    columns = [own_columns] + [
        shift(after(column_part(mine ^ q), key_next, value_next), "seq", q << 1)
        for q in range(1, plan.col)
    ]
    high_columns = [
        shift(after(own_columns, key_next, value_next), "seq", high << (1 + plan.col_bits))
        for high in range(1, plan.high)
    ]

    attended = pl.pallas_call(
        functools.partial(forward_kernel, plan),
        out_shape=struct((plan.high, 2, m * HEAD_DIM, tile), bf16),
        in_specs=[smem()] + whole(7),
        out_specs=pl.BlockSpec(memory_space=pltpu.VMEM),
        scratch_shapes=[pltpu.VMEM((2, tile, width), bf16)],
        compiler_params=params(),
        cost_estimate=cost(8 * tile * tile * width, 16 * tile * width, 2 * tile * tile * head_count),
        name="attention_forward",
    )(neighbour, query, key, value, *beside)

    by_high = [attended[0]] + [
        shift(attended[high], "seq", high << (1 + plan.col_bits)) for high in range(1, plan.high)
    ]
    pairs = [attended[0]] + [shift(attended[0], "seq", q << 1) for q in range(1, plan.col)]
    for came_high in by_high[1:]:
        there = after(came_high, *pairs[1 : plan.col])
        pairs += [came_high] + [shift(there, "seq", q << 1) for q in range(1, plan.col)]

    through = lax.optimization_barrier((attended, *high_columns, jnp.stack(columns[1:])))[-1]
    held = [jnp.stack(columns)]
    late = []
    for high in range(1, plan.high):
        halves = [shift(part, "seq", high << (1 + plan.col_bits)) for part in jnp.split(through, 2, 2)]
        late.append(halves[0])
        rest = jnp.concatenate(halves, 2)
        held.append(jnp.concatenate([high_columns[high - 1][None], rest], 0))
    held = jnp.concatenate(held, 0)

    dq, dko, dvo, dkf, dvf, dfar = pl.pallas_call(
        backward_kernel,
        out_shape=[
            struct((tile, width), bf16),
            struct((tile, width), f32),
            struct((tile, width), f32),
            struct((tile, width), bf16),
            struct((tile, width), bf16),
            struct((2, tile, width), bf16),
        ],
        in_specs=[smem()] + whole(8),
        out_specs=whole(6),
        scratch_shapes=[pltpu.VMEM((2, tile, width), bf16)],
        compiler_params=params(),
        cost_estimate=cost(28 * tile * tile * width, 30 * tile * width, 2 * tile * tile * head_count),
        name="attention_backward",
    )(neighbour, query, key, value, *beside, after(grad, *late))

    def product(name, layers, *operands):
        *blocks, for_mate = pl.pallas_call(
            functools.partial(product_kernel, plan, layers),
            out_shape=[struct((HEAD_DIM, mine_width), f32)] * len(layers)
            + [struct((len(layers), HEAD_DIM, mine_width), bf16)],
            in_specs=whole(plan.pairs + 1),
            out_specs=whole(len(layers) + 1),
            scratch_shapes=[pltpu.VMEM((2, len(layers) * HEAD_DIM, plan.pairs * tile), bf16)],
            compiler_params=params(),
            cost_estimate=cost(
                2 * len(layers) * HEAD_DIM * n * tile * mine_width, n * tile * mine_width
            ),
            name=name,
        )(*operands)
        mate = shift(for_mate, "seq", 1)
        return {i: [(block, None, 0), (mate, k, 0)] for k, (i, block) in enumerate(zip(layers, blocks))}

    def added(parts, start, size):
        return pl.pallas_call(
            functools.partial(sum_kernel, [spot for _, *spot in parts], start),
            out_shape=struct((HEAD_DIM, size), bf16),
            in_specs=whole(len(parts)),
            out_specs=pl.BlockSpec(memory_space=pltpu.VMEM),
            compiler_params=params(),
            cost_estimate=cost(len(parts) * HEAD_DIM * size, 4 * len(parts) * HEAD_DIM * size),
            name="block_sum",
        )(*[array for array, *_ in parts])

    first = [i for i in range(m - 1, 1, -1) if i & 1]
    middle = [i for i in range(m - 1, 1, -1) if not i & 1]
    blocks = product("product_first", first, after(pairs[0], dq), *pairs[1:], held)
    going = {i: added(blocks[i], 0, mine_width) for i in first}
    blocks |= product("product_middle", middle, after(pairs[0], *going.values()), *pairs[1:], held)

    blocks |= product("product_near", [1], after(pairs[0], dq), *pairs[1:], held)
    blocks |= product("product_own", [0], after(pairs[0], dq), *pairs[1:], held)

    extra = {i: [] for i in range(m)}
    sent = []
    bit = 1
    while bit < m:
        for i in range(m - 1, 1, -1):
            if i & -i == bit:
                if bit == 1:
                    sent.append(going[i])
                else:
                    (block, *where), *others = blocks[i] + extra[i]
                    sent.append(added([(after(block, dq), *where)] + others, 0, mine_width))
                extra[i ^ bit].append((shift(sent[-1], "dp", bit), None, 0))
        bit *= 2
    far = [
        shift(after(dfar, dq), "seq", 1),
        lax.ppermute(after(dkf, dq), "seq", gives),
        lax.ppermute(after(dvf, dq), "seq", gives),
    ]
    own = blocks[0][0][0]
    came = [blocks[0][1]] + extra[0]
    parts = 1
    size = mine_width // parts
    for start in range(0, mine_width, size):
        near = after(added(blocks[1], start, size), sent[-1], blocks[0][1][0], far[0])
        came.append((shift(near, "dp", 1), None, start))
    dk, dv = pl.pallas_call(
        combine_kernel,
        out_shape=[struct((tile, width), bf16)] * 2,
        in_specs=[smem()] + whole(5),
        out_specs=whole(2),
        compiler_params=params(),
        cost_estimate=cost(6 * tile * width, 20 * tile * width),
        name="key_value_sum",
    )(
        neighbour,
        dko,
        dvo,
        *far,
    )

    x, gram = pl.pallas_call(
        functools.partial(gram_kernel, [spot for _, *spot in came]),
        out_shape=[struct((HEAD_DIM, mine_width), f32), struct((HEAD_DIM, HEAD_DIM), f32)],
        in_specs=whole(1 + len(came)),
        out_specs=whole(2),
        compiler_params=params(),
        cost_estimate=cost(12 * HEAD_DIM * HEAD_DIM * mine_width, 14 * HEAD_DIM * mine_width),
        name="gradient_sum",
    )(own, *[array for array, *_ in came])

    gram_other = jnp.zeros_like(gram)
    for b in range(plan.col_bits):
        gram = gram + gram_other
        gram_other = shift(gram, "seq", 2 << b)

    factor = 0.2 * depth**0.5
    pieces = pl.pallas_call(
        functools.partial(update_kernel, plan, factor),
        out_shape=[struct((HEAD_DIM, slot), f32)] + [struct((HEAD_DIM, slot), bf16)] * (per - 1),
        in_specs=whole(3),
        out_specs=whole(per),
        compiler_params=params(),
        cost_estimate=cost(12 * HEAD_DIM * HEAD_DIM * mine_width, 8 * HEAD_DIM * mine_width),
        name="newton_schulz",
    )(after(x, dk), gram, gram_other)
    pieces = [pieces[0]] + [
        shift(pieces[j], "seq", plan.row_mask(j)) for j in range(1, per)
    ]
    update = pl.pallas_call(
        functools.partial(place_kernel, plan),
        out_shape=struct((per * HEAD_DIM, slot), f32),
        in_specs=whole(per),
        out_specs=pl.BlockSpec(memory_space=pltpu.VMEM),
        compiler_params=params(),
        cost_estimate=cost(1, 8 * per * HEAD_DIM * slot),
        name="update_rows",
    )(*pieces)

    shape = query_tiles.shape
    return dq.reshape(shape), dk.reshape(shape), dv.reshape(shape), update


def solution(mesh):
    tiles = P("dp", "seq", None, None)
    return jax.shard_map(
        local,
        mesh=mesh,
        in_specs=(tiles, tiles, tiles, tiles, tiles, P("dp", None)),
        out_specs=(tiles, tiles, tiles, P("dp", "seq")),
        check_vma=False,
    )
```

```python
import functools
import math

import jax
import jax.numpy as jnp
from jax import lax
from jax.experimental import pallas as pl
from jax.experimental.pallas import tpu as pltpu
from jax.sharding import PartitionSpec as P

HEAD_DIM = 128
NS_STEPS = 5
SCALE = HEAD_DIM ** (-0.5)
LOG2E = math.log2(math.e)
GROUP = 4
coeff_a = 3.4445
coeff_b = -4.775
coeff_c = 2.0315
f32 = jnp.float32
bf16 = jnp.bfloat16
VMEM_LIMIT = 24 * 1024 * 1024


def whole(count):
    return [pl.BlockSpec(memory_space=pltpu.VMEM)] * count


def smem():
    return pl.BlockSpec(memory_space=pltpu.SMEM)


def params():
    return pltpu.CompilerParams(vmem_limit_bytes=VMEM_LIMIT)


def cost(flops, moved, exps=0):
    return pl.CostEstimate(flops=int(flops), bytes_accessed=int(moved), transcendentals=int(exps))


def dot_t(a, b):
    return lax.dot_general(a, b, (((1,), (1,)), ((), ())), preferred_element_type=f32)


def dot_n(a, b):
    return lax.dot_general(a, b, (((1,), (0,)), ((), ())), preferred_element_type=f32)


def dot_l(a, b):
    return lax.dot_general(a, b, (((0,), (0,)), ((), ())), preferred_element_type=f32)


def exact(a, b, dims=((1,), (0,))):
    return lax.dot_general(
        a, b, (dims, ((), ())), precision=lax.Precision.HIGHEST, preferred_element_type=f32
    )


class Plan:
    def __init__(self, head_count):
        self.seq = lax.axis_size("seq")
        self.dp = lax.axis_size("dp")
        self.per_target = head_count // self.dp
        self.high = self.per_target // 2
        self.col = self.seq // self.per_target
        self.col_bits = self.col.bit_length() - 1
        self.pairs = self.seq // 2

    def row_part(self, place):
        return (place >> (1 + self.col_bits)) * 2 + (place & 1)

    def row_mask(self, part):
        return ((part >> 1) << (1 + self.col_bits)) | (part & 1)

    def col_part(self, place):
        return (place >> 1) & (self.col - 1)


def after(value, *others):
    return lax.optimization_barrier((value, *others))[0]


def shift(value, axis, mask):
    return lax.ppermute(value, axis, [(i, i ^ mask) for i in range(lax.axis_size(axis))])


def head_slice(index):
    return pl.ds(pl.multiple_of(index * HEAD_DIM, HEAD_DIM), HEAD_DIM)


def softmax_keys(query, keys):
    scores = dot_t(keys, query)
    top = jnp.max(scores, axis=0, keepdims=True)
    powers = jnp.exp2((scores - top) * (SCALE * LOG2E))
    return powers * (1.0 / jnp.sum(powers, axis=0, keepdims=True))


def choose_far(near_ref, key_mate, value_mate, key_next, value_next, far):
    place = lax.axis_index("seq")
    is_mate = near_ref[0, place] == (place ^ 1)

    @pl.when(is_mate)
    def _():
        far[0] = key_mate[...]
        far[1] = value_mate[...]

    @pl.when(jnp.logical_not(is_mate))
    def _():
        far[0] = key_next[...]
        far[1] = value_next[...]


def forward_kernel(plan, near_ref, q, ko, vo, km, vm, kn, vn, out, far):
    layer = lax.axis_index("dp")
    choose_far(near_ref, km, vm, kn, vn, far)
    mine = plan.row_part(lax.axis_index("seq"))
    jobs = [(j, i) for j in range(plan.per_target) for i in range(plan.dp)]
    for first in range(0, len(jobs), GROUP):
        group = jobs[first : first + GROUP]
        spots = [head_slice((layer ^ i) * plan.per_target + (mine ^ j)) for j, i in group]
        weights = [
            softmax_keys(q[:, at], jnp.concatenate([ko[:, at], far[0, :, at]], 0)).astype(bf16)
            for at in spots
        ]
        for (j, i), at, p in zip(group, spots, weights, strict=True):
            values = jnp.concatenate([vo[:, at], far[1, :, at]], 0)
            rows = slice(i * HEAD_DIM, (i + 1) * HEAD_DIM)
            out[j >> 1, j & 1, rows, :] = dot_l(values, p).astype(bf16)


def backward_kernel(near_ref, q, ko, vo, km, vm, kn, vn, g, dq, dko, dvo, dkf, dvf, dfar, far):
    choose_far(near_ref, km, vm, kn, vn, far)
    tile = q.shape[0]
    count = q.shape[1] // HEAD_DIM
    for first in range(0, count, GROUP):
        spots = [
            slice(h * HEAD_DIM, (h + 1) * HEAD_DIM)
            for h in range(first, min(first + GROUP, count))
        ]
        weights, slopes = [], []
        for at in spots:
            values = jnp.concatenate([vo[:, at], far[1, :, at]], 0)
            keys = jnp.concatenate([ko[:, at], far[0, :, at]], 0)
            weights.append(softmax_keys(q[:, at], keys))
            slopes.append(dot_t(values, g[:, at]))
        for at, p, dp in zip(spots, weights, slopes, strict=True):
            pb = p.astype(bf16)
            delta = jnp.sum(pb.astype(f32) * dp, axis=0, keepdims=True)
            ds = (p * (dp - delta)).astype(bf16)
            keys = jnp.concatenate([ko[:, at], far[0, :, at]], 0)
            dk = dot_n(ds, q[:, at]) * SCALE
            dv = dot_n(pb, g[:, at])
            dq[:, at] = (dot_l(ds, keys) * SCALE).astype(bf16)
            dko[:, at] = dk[:tile]
            dvo[:, at] = dv[:tile]
            for which, (one, term) in enumerate(((dkf, dk), (dvf, dv))):
                rounded = term[tile:].astype(bf16)
                one[:, at] = rounded
                dfar[which, :, at] = rounded


def combine_kernel(near_ref, dko, dvo, mate, kn, vn, dk, dv):
    place = lax.axis_index("seq")
    last = lax.axis_size("seq") - 1
    other = place + 2 * (place & 1) - 1
    inside = (other >= 0) & (other <= last)
    from_mate = near_ref[0, place ^ 1] == place
    from_other = inside & (near_ref[0, jnp.clip(other, 0, last)] == place)
    for which, (own, beyond, out) in enumerate(((dko, kn, dk), (dvo, vn, dv))):
        total = own[...] + jnp.where(from_mate, mate[which].astype(f32), 0.0)
        out[...] = (total + jnp.where(from_other, beyond[...].astype(f32), 0.0)).astype(bf16)


def product_kernel(plan, layers, *refs):
    att = refs[: plan.pairs]
    cols, *outs, for_mate, gathered = refs[plan.pairs :]
    for t in range(plan.pairs):
        at = slice(t * HEAD_DIM, (t + 1) * HEAD_DIM)
        for core in range(2):
            for n, i in enumerate(layers):
                block = att[t][core, i * HEAD_DIM : (i + 1) * HEAD_DIM, :]
                gathered[core, n * HEAD_DIM : (n + 1) * HEAD_DIM, at] = block
    tokens, width = gathered.shape[2], cols.shape[2]
    step = 512 if width % 512 == 0 else width
    for c in range(0, width, step):
        block = cols[:, :, c : c + step].reshape(tokens, step)
        for n, out in enumerate(outs):
            rows = slice(n * HEAD_DIM, (n + 1) * HEAD_DIM)
            out[:, c : c + step] = dot_n(gathered[0, rows, :], block)
            for_mate[n, :, c : c + step] = dot_n(gathered[1, rows, :], block).astype(bf16)


def piece(ref, lead, start, size):
    at = slice(start, start + size)
    return (ref[:, at] if lead is None else ref[lead, :, at]).astype(f32)


def sum_kernel(spots, start, *refs):
    *parts, out = refs
    size = out.shape[1]
    total = None
    for (lead, first), part in zip(spots, parts, strict=True):
        value = piece(part, lead, start - first, size)
        total = value if total is None else total + value
    out[...] = total.astype(bf16)


def gram_kernel(spots, own, *refs):
    *parts, x, gram = refs
    x[...] = own[...]
    for (lead, first), part in zip(spots, parts, strict=True):
        size = part.shape[-1]
        x[:, first : first + size] += piece(part, lead, 0, size)
    gram[...] = exact(x[...], x[...], ((1,), (1,)))


def polynomial(gram):
    eye = (
        lax.broadcasted_iota(jnp.int32, gram.shape, 0)
        == lax.broadcasted_iota(jnp.int32, gram.shape, 1)
    ).astype(f32)
    square = jnp.sum(jnp.sum(gram * eye, axis=1, keepdims=True), axis=0, keepdims=True)
    inverse = 1.0 / (jnp.sqrt(square) + 1e-07)
    a = gram * inverse * inverse
    p = None
    for turn in range(NS_STEPS):
        q = coeff_a * eye + coeff_b * a + coeff_c * exact(a, a)
        p = q if p is None else exact(q, p)
        if turn + 1 < NS_STEPS:
            a = exact(exact(q, a), q)
    return p, inverse


def update_kernel(plan, factor, x, gram, gram_other, *outs):
    mine = plan.row_part(lax.axis_index("seq"))
    p, inverse = polynomial(gram[...] + gram_other[...])
    p = p * (inverse * factor)
    width = outs[0].shape[1]
    for j in range(plan.per_target):
        if width % HEAD_DIM == 0:
            block = x[:, pl.ds(pl.multiple_of((mine ^ j) * width, width), width)]
        else:
            block = jnp.zeros((HEAD_DIM, width), f32)
            for r in range(plan.per_target):
                part = x[:, r * width : (r + 1) * width]
                block = jnp.where((mine ^ j) == r, part, block)
        outs[j][...] = exact(p, block).astype(outs[j].dtype)


def place_kernel(plan, *refs):
    *parts, out = refs
    mine = plan.row_part(lax.axis_index("seq"))
    for j, part in enumerate(parts):
        at = pl.ds(pl.multiple_of((mine ^ j) * HEAD_DIM, HEAD_DIM), HEAD_DIM)
        out[at, :] = part[...].astype(f32)


def local(query_tiles, key_tiles, value_tiles, attn_grad, proj_grad, neighbour):
    tile, width = query_tiles.shape[2:]
    depth = proj_grad.shape[3]
    head_count = width // HEAD_DIM
    plan = Plan(head_count)
    n, m, per = plan.seq, plan.dp, plan.per_target
    place = lax.axis_index("seq")
    struct = jax.ShapeDtypeStruct
    query, key, value, grad = (
        a.reshape(tile, width) for a in (query_tiles, key_tiles, value_tiles, attn_grad)
    )

    steps = [(i, i + 1) for i in range(1, n - 1, 2)]
    back = [(j, i) for i, j in steps]
    takes = [(i, j) for i, j in steps if j != n - 2] + [(j, i) for j, i in back if i != 1]
    gives = [(i, j) for i, j in steps if i != 1] + [(j, i) for j, i in back if j != n - 2]
    key_next = lax.ppermute(key, "seq", takes)
    value_next = lax.ppermute(value, "seq", takes)
    key_mate = shift(key, "seq", 1)
    value_mate = shift(value, "seq", 1)
    beside = (key_mate, value_mate, key_next, value_next)

    slot = depth // n
    flat = proj_grad.reshape(tile, depth)
    mine = plan.col_part(place)
    mine_width = per * slot

    def column_part(part):
        return jnp.concatenate(
            [
                lax.dynamic_slice_in_dim(flat, (high * plan.col + part) * 2 * slot, 2 * slot, 1)
                for high in range(plan.high)
            ],
            1,
        )

    own_columns = column_part(mine)
    columns = [own_columns] + [
        shift(after(column_part(mine ^ q), key_next, value_next), "seq", q << 1)
        for q in range(1, plan.col)
    ]
    high_columns = [
        shift(after(own_columns, key_next), "seq", high << (1 + plan.col_bits))
        for high in range(1, plan.high)
    ]

    attended = pl.pallas_call(
        functools.partial(forward_kernel, plan),
        out_shape=struct((plan.high, 2, m * HEAD_DIM, tile), bf16),
        in_specs=[smem()] + whole(7),
        out_specs=pl.BlockSpec(memory_space=pltpu.VMEM),
        scratch_shapes=[pltpu.VMEM((2, tile, width), bf16)],
        compiler_params=params(),
        cost_estimate=cost(8 * tile * tile * width, 16 * tile * width, 2 * tile * tile * head_count),
        name="attention_forward",
    )(neighbour, query, key, value, *beside)

    by_high = [attended[0]] + [
        shift(attended[high], "seq", high << (1 + plan.col_bits)) for high in range(1, plan.high)
    ]
    pairs = [attended[0]] + [shift(attended[0], "seq", q << 1) for q in range(1, plan.col)]
    for came_high in by_high[1:]:
        there = after(came_high, *pairs[1 : plan.col])
        pairs += [came_high] + [shift(there, "seq", q << 1) for q in range(1, plan.col)]

    through = lax.optimization_barrier((attended, *high_columns, jnp.stack(columns[1:])))[-1]
    held = [jnp.stack(columns)]
    late = []
    for high in range(1, plan.high):
        halves = [shift(part, "seq", high << (1 + plan.col_bits)) for part in jnp.split(through, 2, 2)]
        late.append(halves[0])
        rest = jnp.concatenate(halves, 2)
        held.append(jnp.concatenate([high_columns[high - 1][None], rest], 0))
    held = jnp.concatenate(held, 0)

    dq, dko, dvo, dkf, dvf, dfar = pl.pallas_call(
        backward_kernel,
        out_shape=[
            struct((tile, width), bf16),
            struct((tile, width), f32),
            struct((tile, width), f32),
            struct((tile, width), bf16),
            struct((tile, width), bf16),
            struct((2, tile, width), bf16),
        ],
        in_specs=[smem()] + whole(8),
        out_specs=whole(6),
        scratch_shapes=[pltpu.VMEM((2, tile, width), bf16)],
        compiler_params=params(),
        cost_estimate=cost(28 * tile * tile * width, 30 * tile * width, 2 * tile * tile * head_count),
        name="attention_backward",
    )(neighbour, query, key, value, *beside, after(grad, *late))

    def product(name, layers, *operands):
        *blocks, for_mate = pl.pallas_call(
            functools.partial(product_kernel, plan, layers),
            out_shape=[struct((HEAD_DIM, mine_width), f32)] * len(layers)
            + [struct((len(layers), HEAD_DIM, mine_width), bf16)],
            in_specs=whole(plan.pairs + 1),
            out_specs=whole(len(layers) + 1),
            scratch_shapes=[pltpu.VMEM((2, len(layers) * HEAD_DIM, plan.pairs * tile), bf16)],
            compiler_params=params(),
            cost_estimate=cost(
                2 * len(layers) * HEAD_DIM * n * tile * mine_width, n * tile * mine_width
            ),
            name=name,
        )(*operands)
        mate = shift(for_mate, "seq", 1)
        return {i: [(block, None, 0), (mate, k, 0)] for k, (i, block) in enumerate(zip(layers, blocks))}

    def added(parts, start, size):
        return pl.pallas_call(
            functools.partial(sum_kernel, [spot for _, *spot in parts], start),
            out_shape=struct((HEAD_DIM, size), bf16),
            in_specs=whole(len(parts)),
            out_specs=pl.BlockSpec(memory_space=pltpu.VMEM),
            compiler_params=params(),
            cost_estimate=cost(len(parts) * HEAD_DIM * size, 4 * len(parts) * HEAD_DIM * size),
            name="block_sum",
        )(*[array for array, *_ in parts])

    first = [i for i in range(m - 1, 1, -1) if i & 1]
    middle = [i for i in range(m - 1, 1, -1) if not i & 1]
    blocks = product("product_first", first, after(pairs[0], dq), *pairs[1:], held)
    going = {i: added(blocks[i], 0, mine_width) for i in first}
    blocks |= product("product_middle", middle, after(pairs[0], *going.values()), *pairs[1:], held)

    blocks |= product("product_near", [1], after(pairs[0], dq), *pairs[1:], held)
    blocks |= product("product_own", [0], after(pairs[0], dq), *pairs[1:], held)

    extra = {i: [] for i in range(m)}
    sent = []
    bit = 1
    while bit < m:
        for i in range(m - 1, 1, -1):
            if i & -i == bit:
                if bit == 1:
                    sent.append(going[i])
                else:
                    (block, *where), *others = blocks[i] + extra[i]
                    sent.append(added([(after(block, dq), *where)] + others, 0, mine_width))
                extra[i ^ bit].append((shift(sent[-1], "dp", bit), None, 0))
        bit *= 2
    far = [
        shift(after(dfar, dq), "seq", 1),
        lax.ppermute(after(dkf, dq), "seq", gives),
        lax.ppermute(after(dvf, dq), "seq", gives),
    ]
    own = blocks[0][0][0]
    came = [blocks[0][1]] + extra[0]
    parts = 1
    size = mine_width // parts
    for start in range(0, mine_width, size):
        near = after(added(blocks[1], start, size), sent[-1], blocks[0][1][0], far[0])
        came.append((shift(near, "dp", 1), None, start))
    dk, dv = pl.pallas_call(
        combine_kernel,
        out_shape=[struct((tile, width), bf16)] * 2,
        in_specs=[smem()] + whole(5),
        out_specs=whole(2),
        compiler_params=params(),
        cost_estimate=cost(6 * tile * width, 20 * tile * width),
        name="key_value_sum",
    )(
        neighbour,
        dko,
        dvo,
        *far,
    )

    x, gram = pl.pallas_call(
        functools.partial(gram_kernel, [spot for _, *spot in came]),
        out_shape=[struct((HEAD_DIM, mine_width), f32), struct((HEAD_DIM, HEAD_DIM), f32)],
        in_specs=whole(1 + len(came)),
        out_specs=whole(2),
        compiler_params=params(),
        cost_estimate=cost(12 * HEAD_DIM * HEAD_DIM * mine_width, 14 * HEAD_DIM * mine_width),
        name="gradient_sum",
    )(own, *[array for array, *_ in came])

    gram_other = jnp.zeros_like(gram)
    for b in range(plan.col_bits):
        gram = gram + gram_other
        gram_other = shift(gram, "seq", 2 << b)

    factor = 0.2 * depth**0.5
    pieces = pl.pallas_call(
        functools.partial(update_kernel, plan, factor),
        out_shape=[struct((HEAD_DIM, slot), f32)] + [struct((HEAD_DIM, slot), bf16)] * (per - 1),
        in_specs=whole(3),
        out_specs=whole(per),
        compiler_params=params(),
        cost_estimate=cost(12 * HEAD_DIM * HEAD_DIM * mine_width, 8 * HEAD_DIM * mine_width),
        name="newton_schulz",
    )(after(x, dk), gram, gram_other)
    pieces = [pieces[0]] + [
        shift(pieces[j], "seq", plan.row_mask(j)) for j in range(1, per)
    ]
    update = pl.pallas_call(
        functools.partial(place_kernel, plan),
        out_shape=struct((per * HEAD_DIM, slot), f32),
        in_specs=whole(per),
        out_specs=pl.BlockSpec(memory_space=pltpu.VMEM),
        compiler_params=params(),
        cost_estimate=cost(1, 8 * per * HEAD_DIM * slot),
        name="update_rows",
    )(*pieces)

    shape = query_tiles.shape
    return dq.reshape(shape), dk.reshape(shape), dv.reshape(shape), update


def solution(mesh):
    tiles = P("dp", "seq", None, None)
    return jax.shard_map(
        local,
        mesh=mesh,
        in_specs=(tiles, tiles, tiles, tiles, tiles, P("dp", None)),
        out_specs=(tiles, tiles, tiles, P("dp", "seq")),
        check_vma=False,
    )
```

```python
import functools
import math

import jax
import jax.numpy as jnp
from jax import lax
from jax.experimental import pallas as pl
from jax.experimental.pallas import tpu as pltpu
from jax.sharding import PartitionSpec as P

HEAD_DIM = 128
NS_STEPS = 5
SCALE = HEAD_DIM ** (-0.5)
LOG2E = math.log2(math.e)
GROUP = 4
coeff_a = 3.4445
coeff_b = -4.775
coeff_c = 2.0315
f32 = jnp.float32
bf16 = jnp.bfloat16
VMEM_LIMIT = 24 * 1024 * 1024


def whole(count):
    return [pl.BlockSpec(memory_space=pltpu.VMEM)] * count


def smem():
    return pl.BlockSpec(memory_space=pltpu.SMEM)


def params():
    return pltpu.CompilerParams(vmem_limit_bytes=VMEM_LIMIT)


def cost(flops, moved, exps=0):
    return pl.CostEstimate(flops=int(flops), bytes_accessed=int(moved), transcendentals=int(exps))


def dot_t(a, b):
    return lax.dot_general(a, b, (((1,), (1,)), ((), ())), preferred_element_type=f32)


def dot_n(a, b):
    return lax.dot_general(a, b, (((1,), (0,)), ((), ())), preferred_element_type=f32)


def dot_l(a, b):
    return lax.dot_general(a, b, (((0,), (0,)), ((), ())), preferred_element_type=f32)


def exact(a, b, dims=((1,), (0,))):
    return lax.dot_general(
        a, b, (dims, ((), ())), precision=lax.Precision.HIGHEST, preferred_element_type=f32
    )


class Plan:
    def __init__(self, head_count):
        self.seq = lax.axis_size("seq")
        self.dp = lax.axis_size("dp")
        self.per_target = head_count // self.dp
        self.high = self.per_target // 2
        self.col = self.seq // self.per_target
        self.col_bits = self.col.bit_length() - 1
        self.pairs = self.seq // 2

    def row_part(self, place):
        return (place >> (1 + self.col_bits)) * 2 + (place & 1)

    def row_mask(self, part):
        return ((part >> 1) << (1 + self.col_bits)) | (part & 1)

    def col_part(self, place):
        return (place >> 1) & (self.col - 1)


def after(value, *others):
    return lax.optimization_barrier((value, *others))[0]


def shift(value, axis, mask):
    return lax.ppermute(value, axis, [(i, i ^ mask) for i in range(lax.axis_size(axis))])


def head_slice(index):
    return pl.ds(pl.multiple_of(index * HEAD_DIM, HEAD_DIM), HEAD_DIM)


def softmax_keys(query, keys):
    scores = dot_t(keys, query)
    top = jnp.max(scores, axis=0, keepdims=True)
    powers = jnp.exp2((scores - top) * (SCALE * LOG2E))
    return powers * (1.0 / jnp.sum(powers, axis=0, keepdims=True))


def choose_far(near_ref, key_mate, value_mate, key_next, value_next, far):
    place = lax.axis_index("seq")
    is_mate = near_ref[0, place] == (place ^ 1)

    @pl.when(is_mate)
    def _():
        far[0] = key_mate[...]
        far[1] = value_mate[...]

    @pl.when(jnp.logical_not(is_mate))
    def _():
        far[0] = key_next[...]
        far[1] = value_next[...]


def forward_kernel(plan, near_ref, q, ko, vo, km, vm, kn, vn, out, far):
    layer = lax.axis_index("dp")
    choose_far(near_ref, km, vm, kn, vn, far)
    mine = plan.row_part(lax.axis_index("seq"))
    jobs = [(j, i) for j in range(plan.per_target) for i in range(plan.dp)]
    for first in range(0, len(jobs), GROUP):
        group = jobs[first : first + GROUP]
        spots = [head_slice((layer ^ i) * plan.per_target + (mine ^ j)) for j, i in group]
        weights = [
            softmax_keys(q[:, at], jnp.concatenate([ko[:, at], far[0, :, at]], 0)).astype(bf16)
            for at in spots
        ]
        for (j, i), at, p in zip(group, spots, weights, strict=True):
            values = jnp.concatenate([vo[:, at], far[1, :, at]], 0)
            rows = slice(i * HEAD_DIM, (i + 1) * HEAD_DIM)
            out[j >> 1, j & 1, rows, :] = dot_l(values, p).astype(bf16)


def backward_kernel(near_ref, q, ko, vo, km, vm, kn, vn, g, dq, dko, dvo, dkf, dvf, dfar, far):
    choose_far(near_ref, km, vm, kn, vn, far)
    tile = q.shape[0]
    count = q.shape[1] // HEAD_DIM
    for first in range(0, count, GROUP):
        spots = [
            slice(h * HEAD_DIM, (h + 1) * HEAD_DIM)
            for h in range(first, min(first + GROUP, count))
        ]
        weights, slopes = [], []
        for at in spots:
            values = jnp.concatenate([vo[:, at], far[1, :, at]], 0)
            keys = jnp.concatenate([ko[:, at], far[0, :, at]], 0)
            weights.append(softmax_keys(q[:, at], keys))
            slopes.append(dot_t(values, g[:, at]))
        for at, p, dp in zip(spots, weights, slopes, strict=True):
            pb = p.astype(bf16)
            delta = jnp.sum(pb.astype(f32) * dp, axis=0, keepdims=True)
            ds = (p * (dp - delta)).astype(bf16)
            keys = jnp.concatenate([ko[:, at], far[0, :, at]], 0)
            dk = dot_n(ds, q[:, at]) * SCALE
            dv = dot_n(pb, g[:, at])
            dq[:, at] = (dot_l(ds, keys) * SCALE).astype(bf16)
            dko[:, at] = dk[:tile]
            dvo[:, at] = dv[:tile]
            for which, (one, term) in enumerate(((dkf, dk), (dvf, dv))):
                rounded = term[tile:].astype(bf16)
                one[:, at] = rounded
                dfar[which, :, at] = rounded


def combine_kernel(near_ref, dko, dvo, mate, kn, vn, dk, dv):
    place = lax.axis_index("seq")
    last = lax.axis_size("seq") - 1
    other = place + 2 * (place & 1) - 1
    inside = (other >= 0) & (other <= last)
    from_mate = near_ref[0, place ^ 1] == place
    from_other = inside & (near_ref[0, jnp.clip(other, 0, last)] == place)
    for which, (own, beyond, out) in enumerate(((dko, kn, dk), (dvo, vn, dv))):
        total = own[...] + jnp.where(from_mate, mate[which].astype(f32), 0.0)
        out[...] = (total + jnp.where(from_other, beyond[...].astype(f32), 0.0)).astype(bf16)


def product_kernel(plan, layers, *refs):
    att = refs[: plan.pairs]
    cols, *outs, for_mate, gathered = refs[plan.pairs :]
    for t in range(plan.pairs):
        at = slice(t * HEAD_DIM, (t + 1) * HEAD_DIM)
        for core in range(2):
            for n, i in enumerate(layers):
                block = att[t][core, i * HEAD_DIM : (i + 1) * HEAD_DIM, :]
                gathered[core, n * HEAD_DIM : (n + 1) * HEAD_DIM, at] = block
    tokens, width = gathered.shape[2], cols.shape[2]
    step = 512 if width % 512 == 0 else width
    for c in range(0, width, step):
        block = cols[:, :, c : c + step].reshape(tokens, step)
        for n, out in enumerate(outs):
            rows = slice(n * HEAD_DIM, (n + 1) * HEAD_DIM)
            out[:, c : c + step] = dot_n(gathered[0, rows, :], block)
            for_mate[n, :, c : c + step] = dot_n(gathered[1, rows, :], block).astype(bf16)


def piece(ref, lead, start, size):
    at = slice(start, start + size)
    return (ref[:, at] if lead is None else ref[lead, :, at]).astype(f32)


def sum_kernel(spots, start, *refs):
    *parts, out = refs
    size = out.shape[1]
    total = None
    for (lead, first), part in zip(spots, parts, strict=True):
        value = piece(part, lead, start - first, size)
        total = value if total is None else total + value
    out[...] = total.astype(bf16)


def gram_kernel(spots, own, *refs):
    *parts, x, gram = refs
    x[...] = own[...]
    for (lead, first), part in zip(spots, parts, strict=True):
        size = part.shape[-1]
        x[:, first : first + size] += piece(part, lead, 0, size)
    gram[...] = exact(x[...], x[...], ((1,), (1,)))


def polynomial(gram):
    eye = (
        lax.broadcasted_iota(jnp.int32, gram.shape, 0)
        == lax.broadcasted_iota(jnp.int32, gram.shape, 1)
    ).astype(f32)
    square = jnp.sum(jnp.sum(gram * eye, axis=1, keepdims=True), axis=0, keepdims=True)
    inverse = 1.0 / (jnp.sqrt(square) + 1e-07)
    a = gram * inverse * inverse
    p = None
    for turn in range(NS_STEPS):
        q = coeff_a * eye + coeff_b * a + coeff_c * exact(a, a)
        p = q if p is None else exact(q, p)
        if turn + 1 < NS_STEPS:
            a = exact(exact(q, a), q)
    return p, inverse


def update_kernel(plan, factor, x, gram, gram_other, *outs):
    mine = plan.row_part(lax.axis_index("seq"))
    p, inverse = polynomial(gram[...] + gram_other[...])
    p = p * (inverse * factor)
    width = outs[0].shape[1]
    for j in range(plan.per_target):
        if width % HEAD_DIM == 0:
            block = x[:, pl.ds(pl.multiple_of((mine ^ j) * width, width), width)]
        else:
            block = jnp.zeros((HEAD_DIM, width), f32)
            for r in range(plan.per_target):
                part = x[:, r * width : (r + 1) * width]
                block = jnp.where((mine ^ j) == r, part, block)
        outs[j][...] = exact(p, block).astype(outs[j].dtype)


def place_kernel(plan, *refs):
    *parts, out = refs
    mine = plan.row_part(lax.axis_index("seq"))
    for j, part in enumerate(parts):
        at = pl.ds(pl.multiple_of((mine ^ j) * HEAD_DIM, HEAD_DIM), HEAD_DIM)
        out[at, :] = part[...].astype(f32)


def local(query_tiles, key_tiles, value_tiles, attn_grad, proj_grad, neighbour):
    tile, width = query_tiles.shape[2:]
    depth = proj_grad.shape[3]
    head_count = width // HEAD_DIM
    plan = Plan(head_count)
    n, m, per = plan.seq, plan.dp, plan.per_target
    place = lax.axis_index("seq")
    struct = jax.ShapeDtypeStruct
    query, key, value, grad = (
        a.reshape(tile, width) for a in (query_tiles, key_tiles, value_tiles, attn_grad)
    )

    steps = [(i, i + 1) for i in range(1, n - 1, 2)]
    back = [(j, i) for i, j in steps]
    takes = [(i, j) for i, j in steps if j != n - 2] + [(j, i) for j, i in back if i != 1]
    gives = [(i, j) for i, j in steps if i != 1] + [(j, i) for j, i in back if j != n - 2]
    key_next = lax.ppermute(key, "seq", takes)
    value_next = lax.ppermute(value, "seq", takes)
    key_mate = shift(key, "seq", 1)
    value_mate = shift(value, "seq", 1)
    beside = (key_mate, value_mate, key_next, value_next)

    slot = depth // n
    flat = proj_grad.reshape(tile, depth)
    mine = plan.col_part(place)
    mine_width = per * slot

    def column_part(part):
        return jnp.concatenate(
            [
                lax.dynamic_slice_in_dim(flat, (high * plan.col + part) * 2 * slot, 2 * slot, 1)
                for high in range(plan.high)
            ],
            1,
        )

    own_columns = column_part(mine)
    columns = [own_columns] + [
        shift(after(column_part(mine ^ q), key_next, value_next), "seq", q << 1)
        for q in range(1, plan.col)
    ]
    high_columns = [
        shift(own_columns, "seq", high << (1 + plan.col_bits))
        for high in range(1, plan.high)
    ]

    attended = pl.pallas_call(
        functools.partial(forward_kernel, plan),
        out_shape=struct((plan.high, 2, m * HEAD_DIM, tile), bf16),
        in_specs=[smem()] + whole(7),
        out_specs=pl.BlockSpec(memory_space=pltpu.VMEM),
        scratch_shapes=[pltpu.VMEM((2, tile, width), bf16)],
        compiler_params=params(),
        cost_estimate=cost(8 * tile * tile * width, 16 * tile * width, 2 * tile * tile * head_count),
        name="attention_forward",
    )(neighbour, query, key, value, *beside)

    by_high = [attended[0]] + [
        shift(attended[high], "seq", high << (1 + plan.col_bits)) for high in range(1, plan.high)
    ]
    pairs = [attended[0]] + [shift(attended[0], "seq", q << 1) for q in range(1, plan.col)]
    for came_high in by_high[1:]:
        there = after(came_high, *pairs[1 : plan.col])
        pairs += [came_high] + [shift(there, "seq", q << 1) for q in range(1, plan.col)]

    dq, dko, dvo, dkf, dvf, dfar = pl.pallas_call(
        backward_kernel,
        out_shape=[
            struct((tile, width), bf16),
            struct((tile, width), f32),
            struct((tile, width), f32),
            struct((tile, width), bf16),
            struct((tile, width), bf16),
            struct((2, tile, width), bf16),
        ],
        in_specs=[smem()] + whole(8),
        out_specs=whole(6),
        scratch_shapes=[pltpu.VMEM((2, tile, width), bf16)],
        compiler_params=params(),
        cost_estimate=cost(1, 1),
        name="attention_backward",
    )(neighbour, query, key, value, *beside, after(grad, attended))

    through = lax.optimization_barrier((dq, *high_columns, jnp.stack(columns[1:])))[-1]
    held = [jnp.stack(columns)]
    late = []
    for high in range(1, plan.high):
        halves = [shift(part, "seq", high << (1 + plan.col_bits)) for part in jnp.split(through, 2, 2)]
        late.append(halves[0])
        rest = jnp.concatenate(halves, 2)
        held.append(jnp.concatenate([high_columns[high - 1][None], rest], 0))
    held = jnp.concatenate(held, 0)

    def product(name, layers, *operands):
        *blocks, for_mate = pl.pallas_call(
            functools.partial(product_kernel, plan, layers),
            out_shape=[struct((HEAD_DIM, mine_width), f32)] * len(layers)
            + [struct((len(layers), HEAD_DIM, mine_width), bf16)],
            in_specs=whole(plan.pairs + 1),
            out_specs=whole(len(layers) + 1),
            scratch_shapes=[pltpu.VMEM((2, len(layers) * HEAD_DIM, plan.pairs * tile), bf16)],
            compiler_params=params(),
            cost_estimate=cost(
                2 * len(layers) * HEAD_DIM * n * tile * mine_width, n * tile * mine_width
            ),
            name=name,
        )(*operands)
        mate = shift(for_mate, "seq", 1)
        return {i: [(block, None, 0), (mate, k, 0)] for k, (i, block) in enumerate(zip(layers, blocks))}

    def added(parts, start, size):
        return pl.pallas_call(
            functools.partial(sum_kernel, [spot for _, *spot in parts], start),
            out_shape=struct((HEAD_DIM, size), bf16),
            in_specs=whole(len(parts)),
            out_specs=pl.BlockSpec(memory_space=pltpu.VMEM),
            compiler_params=params(),
            cost_estimate=cost(len(parts) * HEAD_DIM * size, 4 * len(parts) * HEAD_DIM * size),
            name="block_sum",
        )(*[array for array, *_ in parts])

    first = [i for i in range(m - 1, 1, -1) if i & 1]
    middle = [i for i in range(m - 1, 1, -1) if not i & 1]
    blocks = product("product_first", first, after(pairs[0], dq), *pairs[1:], held)
    going = {i: added(blocks[i], 0, mine_width) for i in first}
    blocks |= product("product_middle", middle, after(pairs[0], *going.values()), *pairs[1:], held)

    blocks |= product("product_near", [1], after(pairs[0], dq), *pairs[1:], held)
    blocks |= product("product_own", [0], after(pairs[0], dq), *pairs[1:], held)

    extra = {i: [] for i in range(m)}
    sent = []
    bit = 1
    while bit < m:
        for i in range(m - 1, 1, -1):
            if i & -i == bit:
                if bit == 1:
                    sent.append(going[i])
                else:
                    (block, *where), *others = blocks[i] + extra[i]
                    sent.append(added([(after(block, dq), *where)] + others, 0, mine_width))
                extra[i ^ bit].append((shift(sent[-1], "dp", bit), None, 0))
        bit *= 2
    far = [
        shift(after(dfar, dq), "seq", 1),
        lax.ppermute(after(dkf, dq), "seq", gives),
        lax.ppermute(after(dvf, dq), "seq", gives),
    ]
    own = blocks[0][0][0]
    came = [blocks[0][1]] + extra[0]
    parts = 1
    size = mine_width // parts
    for start in range(0, mine_width, size):
        near = after(added(blocks[1], start, size), sent[-1], blocks[0][1][0], far[0])
        came.append((shift(near, "dp", 1), None, start))
    dk, dv = pl.pallas_call(
        combine_kernel,
        out_shape=[struct((tile, width), bf16)] * 2,
        in_specs=[smem()] + whole(5),
        out_specs=whole(2),
        compiler_params=params(),
        cost_estimate=cost(6 * tile * width, 20 * tile * width),
        name="key_value_sum",
    )(
        neighbour,
        dko,
        dvo,
        *far,
    )

    x, gram = pl.pallas_call(
        functools.partial(gram_kernel, [spot for _, *spot in came]),
        out_shape=[struct((HEAD_DIM, mine_width), f32), struct((HEAD_DIM, HEAD_DIM), f32)],
        in_specs=whole(1 + len(came)),
        out_specs=whole(2),
        compiler_params=params(),
        cost_estimate=cost(12 * HEAD_DIM * HEAD_DIM * mine_width, 14 * HEAD_DIM * mine_width),
        name="gradient_sum",
    )(own, *[array for array, *_ in came])

    gram_other = jnp.zeros_like(gram)
    for b in range(plan.col_bits):
        gram = gram + gram_other
        gram_other = shift(gram, "seq", 2 << b)

    factor = 0.2 * depth**0.5
    pieces = pl.pallas_call(
        functools.partial(update_kernel, plan, factor),
        out_shape=[struct((HEAD_DIM, slot), f32)] + [struct((HEAD_DIM, slot), bf16)] * (per - 1),
        in_specs=whole(3),
        out_specs=whole(per),
        compiler_params=params(),
        cost_estimate=cost(12 * HEAD_DIM * HEAD_DIM * mine_width, 8 * HEAD_DIM * mine_width),
        name="newton_schulz",
    )(after(x, dk), gram, gram_other)
    pieces = [pieces[0]] + [
        shift(pieces[j], "seq", plan.row_mask(j)) for j in range(1, per)
    ]
    update = pl.pallas_call(
        functools.partial(place_kernel, plan),
        out_shape=struct((per * HEAD_DIM, slot), f32),
        in_specs=whole(per),
        out_specs=pl.BlockSpec(memory_space=pltpu.VMEM),
        compiler_params=params(),
        cost_estimate=cost(1, 8 * per * HEAD_DIM * slot),
        name="update_rows",
    )(*pieces)

    shape = query_tiles.shape
    return dq.reshape(shape), dk.reshape(shape), dv.reshape(shape), update


def solution(mesh):
    tiles = P("dp", "seq", None, None)
    return jax.shard_map(
        local,
        mesh=mesh,
        in_specs=(tiles, tiles, tiles, tiles, tiles, P("dp", None)),
        out_specs=(tiles, tiles, tiles, P("dp", "seq")),
        check_vma=False,
    )
```

```python
import functools
import math

import jax
import jax.numpy as jnp
from jax import lax
from jax.experimental import pallas as pl
from jax.experimental.pallas import tpu as pltpu
from jax.sharding import PartitionSpec as P

HEAD_DIM = 128
NS_STEPS = 5
SCALE = HEAD_DIM ** (-0.5)
LOG2E = math.log2(math.e)
GROUP = 4
coeff_a = 3.4445
coeff_b = -4.775
coeff_c = 2.0315
f32 = jnp.float32
bf16 = jnp.bfloat16
VMEM_LIMIT = 24 * 1024 * 1024


def whole(count):
    return [pl.BlockSpec(memory_space=pltpu.VMEM)] * count


def smem():
    return pl.BlockSpec(memory_space=pltpu.SMEM)


def params():
    return pltpu.CompilerParams(vmem_limit_bytes=VMEM_LIMIT)


def cost(flops, moved, exps=0):
    return pl.CostEstimate(flops=int(flops), bytes_accessed=int(moved), transcendentals=int(exps))


def dot_t(a, b):
    return lax.dot_general(a, b, (((1,), (1,)), ((), ())), preferred_element_type=f32)


def dot_n(a, b):
    return lax.dot_general(a, b, (((1,), (0,)), ((), ())), preferred_element_type=f32)


def dot_l(a, b):
    return lax.dot_general(a, b, (((0,), (0,)), ((), ())), preferred_element_type=f32)


def exact(a, b, dims=((1,), (0,))):
    return lax.dot_general(
        a, b, (dims, ((), ())), precision=lax.Precision.HIGHEST, preferred_element_type=f32
    )


class Plan:
    def __init__(self, head_count):
        self.seq = lax.axis_size("seq")
        self.dp = lax.axis_size("dp")
        self.per_target = head_count // self.dp
        self.high = self.per_target // 2
        self.col = self.seq // self.per_target
        self.col_bits = self.col.bit_length() - 1
        self.pairs = self.seq // 2

    def row_part(self, place):
        return (place >> (1 + self.col_bits)) * 2 + (place & 1)

    def row_mask(self, part):
        return ((part >> 1) << (1 + self.col_bits)) | (part & 1)

    def col_part(self, place):
        return (place >> 1) & (self.col - 1)


def after(value, *others):
    return lax.optimization_barrier((value, *others))[0]


def shift(value, axis, mask):
    return lax.ppermute(value, axis, [(i, i ^ mask) for i in range(lax.axis_size(axis))])


def head_slice(index):
    return pl.ds(pl.multiple_of(index * HEAD_DIM, HEAD_DIM), HEAD_DIM)


def softmax_keys(query, keys):
    scores = dot_t(keys, query)
    top = jnp.max(scores, axis=0, keepdims=True)
    powers = jnp.exp2((scores - top) * (SCALE * LOG2E))
    return powers * (1.0 / jnp.sum(powers, axis=0, keepdims=True))


def choose_far(near_ref, key_mate, value_mate, key_next, value_next, far):
    place = lax.axis_index("seq")
    is_mate = near_ref[0, place] == (place ^ 1)

    @pl.when(is_mate)
    def _():
        far[0] = key_mate[...]
        far[1] = value_mate[...]

    @pl.when(jnp.logical_not(is_mate))
    def _():
        far[0] = key_next[...]
        far[1] = value_next[...]


def forward_kernel(plan, near_ref, q, ko, vo, km, vm, kn, vn, out, far):
    layer = lax.axis_index("dp")
    choose_far(near_ref, km, vm, kn, vn, far)
    mine = plan.row_part(lax.axis_index("seq"))
    jobs = [(j, i) for j in range(plan.per_target) for i in range(plan.dp)]
    for first in range(0, len(jobs), GROUP):
        group = jobs[first : first + GROUP]
        spots = [head_slice((layer ^ i) * plan.per_target + (mine ^ j)) for j, i in group]
        weights = [
            softmax_keys(q[:, at], jnp.concatenate([ko[:, at], far[0, :, at]], 0)).astype(bf16)
            for at in spots
        ]
        for (j, i), at, p in zip(group, spots, weights, strict=True):
            values = jnp.concatenate([vo[:, at], far[1, :, at]], 0)
            rows = slice(i * HEAD_DIM, (i + 1) * HEAD_DIM)
            out[j >> 1, j & 1, rows, :] = dot_l(values, p).astype(bf16)


def backward_kernel(near_ref, q, ko, vo, km, vm, kn, vn, g, dq, dko, dvo, dkf, dvf, dfar, far):
    choose_far(near_ref, km, vm, kn, vn, far)
    tile = q.shape[0]
    count = q.shape[1] // HEAD_DIM
    for first in range(0, count, GROUP):
        spots = [
            slice(h * HEAD_DIM, (h + 1) * HEAD_DIM)
            for h in range(first, min(first + GROUP, count))
        ]
        weights, slopes = [], []
        for at in spots:
            values = jnp.concatenate([vo[:, at], far[1, :, at]], 0)
            keys = jnp.concatenate([ko[:, at], far[0, :, at]], 0)
            weights.append(softmax_keys(q[:, at], keys))
            slopes.append(dot_t(values, g[:, at]))
        for at, p, dp in zip(spots, weights, slopes, strict=True):
            pb = p.astype(bf16)
            delta = jnp.sum(pb.astype(f32) * dp, axis=0, keepdims=True)
            ds = (p * (dp - delta)).astype(bf16)
            keys = jnp.concatenate([ko[:, at], far[0, :, at]], 0)
            dk = dot_n(ds, q[:, at]) * SCALE
            dv = dot_n(pb, g[:, at])
            dq[:, at] = (dot_l(ds, keys) * SCALE).astype(bf16)
            dko[:, at] = dk[:tile]
            dvo[:, at] = dv[:tile]
            for which, (one, term) in enumerate(((dkf, dk), (dvf, dv))):
                rounded = term[tile:].astype(bf16)
                one[:, at] = rounded
                dfar[which, :, at] = rounded


def combine_kernel(near_ref, dko, dvo, mate, kn, vn, dk, dv):
    place = lax.axis_index("seq")
    last = lax.axis_size("seq") - 1
    other = place + 2 * (place & 1) - 1
    inside = (other >= 0) & (other <= last)
    from_mate = near_ref[0, place ^ 1] == place
    from_other = inside & (near_ref[0, jnp.clip(other, 0, last)] == place)
    for which, (own, beyond, out) in enumerate(((dko, kn, dk), (dvo, vn, dv))):
        total = own[...] + jnp.where(from_mate, mate[which].astype(f32), 0.0)
        out[...] = (total + jnp.where(from_other, beyond[...].astype(f32), 0.0)).astype(bf16)


def product_kernel(counts, layers, *refs):
    att = list(refs[: sum(counts)])
    cols, *outs, for_mate, gathered = refs[sum(counts) :]
    for t, count in enumerate(counts):
        at = slice(t * HEAD_DIM, (t + 1) * HEAD_DIM)
        parts, att = att[:count], att[count:]
        for core in range(2):
            part, row = (parts[0], core) if count == 1 else (parts[core], 0)
            for n, i in enumerate(layers):
                block = part[row, i * HEAD_DIM : (i + 1) * HEAD_DIM, :]
                gathered[core, n * HEAD_DIM : (n + 1) * HEAD_DIM, at] = block
    tokens, width = gathered.shape[2], cols.shape[2]
    step = 512 if width % 512 == 0 else width
    for c in range(0, width, step):
        block = cols[:, :, c : c + step].reshape(tokens, step)
        for n, out in enumerate(outs):
            rows = slice(n * HEAD_DIM, (n + 1) * HEAD_DIM)
            out[:, c : c + step] = dot_n(gathered[0, rows, :], block)
            for_mate[n, :, c : c + step] = dot_n(gathered[1, rows, :], block).astype(bf16)


def piece(ref, lead, start, size):
    at = slice(start, start + size)
    return (ref[:, at] if lead is None else ref[lead, :, at]).astype(f32)


def sum_kernel(spots, start, *refs):
    *parts, out = refs
    size = out.shape[1]
    total = None
    for (lead, first), part in zip(spots, parts, strict=True):
        value = piece(part, lead, start - first, size)
        total = value if total is None else total + value
    out[...] = total.astype(bf16)


def gram_kernel(spots, own, *refs):
    *parts, x, gram = refs
    x[...] = own[...]
    for (lead, first), part in zip(spots, parts, strict=True):
        size = part.shape[-1]
        x[:, first : first + size] += piece(part, lead, 0, size)
    gram[...] = exact(x[...], x[...], ((1,), (1,)))


def polynomial(gram):
    eye = (
        lax.broadcasted_iota(jnp.int32, gram.shape, 0)
        == lax.broadcasted_iota(jnp.int32, gram.shape, 1)
    ).astype(f32)
    square = jnp.sum(jnp.sum(gram * eye, axis=1, keepdims=True), axis=0, keepdims=True)
    inverse = 1.0 / (jnp.sqrt(square) + 1e-07)
    a = gram * inverse * inverse
    p = None
    for turn in range(NS_STEPS):
        q = coeff_a * eye + coeff_b * a + coeff_c * exact(a, a)
        p = q if p is None else exact(q, p)
        if turn + 1 < NS_STEPS:
            a = exact(exact(q, a), q)
    return p, inverse


def update_kernel(plan, factor, x, gram, gram_other, *outs):
    mine = plan.row_part(lax.axis_index("seq"))
    p, inverse = polynomial(gram[...] + gram_other[...])
    p = p * (inverse * factor)
    width = outs[0].shape[1]
    for j in range(plan.per_target):
        if width % HEAD_DIM == 0:
            block = x[:, pl.ds(pl.multiple_of((mine ^ j) * width, width), width)]
        else:
            block = jnp.zeros((HEAD_DIM, width), f32)
            for r in range(plan.per_target):
                part = x[:, r * width : (r + 1) * width]
                block = jnp.where((mine ^ j) == r, part, block)
        outs[j][...] = exact(p, block).astype(outs[j].dtype)


def place_kernel(plan, *refs):
    *parts, out = refs
    mine = plan.row_part(lax.axis_index("seq"))
    for j, part in enumerate(parts):
        at = pl.ds(pl.multiple_of((mine ^ j) * HEAD_DIM, HEAD_DIM), HEAD_DIM)
        out[at, :] = part[...].astype(f32)


def local(query_tiles, key_tiles, value_tiles, attn_grad, proj_grad, neighbour):
    tile, width = query_tiles.shape[2:]
    depth = proj_grad.shape[3]
    head_count = width // HEAD_DIM
    plan = Plan(head_count)
    n, m, per = plan.seq, plan.dp, plan.per_target
    place = lax.axis_index("seq")
    struct = jax.ShapeDtypeStruct
    query, key, value, grad = (
        a.reshape(tile, width) for a in (query_tiles, key_tiles, value_tiles, attn_grad)
    )

    steps = [(i, i + 1) for i in range(1, n - 1, 2)]
    back = [(j, i) for i, j in steps]
    takes = [(i, j) for i, j in steps if j != n - 2] + [(j, i) for j, i in back if i != 1]
    gives = [(i, j) for i, j in steps if i != 1] + [(j, i) for j, i in back if j != n - 2]
    key_next = lax.ppermute(key, "seq", takes)
    value_next = lax.ppermute(value, "seq", takes)
    key_mate = shift(key, "seq", 1)
    value_mate = shift(value, "seq", 1)
    beside = (key_mate, value_mate, key_next, value_next)

    slot = depth // n
    flat = proj_grad.reshape(tile, depth)
    mine = plan.col_part(place)
    mine_width = per * slot

    def column_part(part):
        return jnp.concatenate(
            [
                lax.dynamic_slice_in_dim(flat, (high * plan.col + part) * 2 * slot, 2 * slot, 1)
                for high in range(plan.high)
            ],
            1,
        )

    own_columns = column_part(mine)
    columns = [own_columns] + [
        shift(after(column_part(mine ^ q), key_next, value_next), "seq", q << 1)
        for q in range(1, plan.col)
    ]
    high_columns = [
        shift(own_columns, "seq", high << (1 + plan.col_bits))
        for high in range(1, plan.high)
    ]

    attended = pl.pallas_call(
        functools.partial(forward_kernel, plan),
        out_shape=struct((plan.high, 2, m * HEAD_DIM, tile), bf16),
        in_specs=[smem()] + whole(7),
        out_specs=pl.BlockSpec(memory_space=pltpu.VMEM),
        scratch_shapes=[pltpu.VMEM((2, tile, width), bf16)],
        compiler_params=params(),
        cost_estimate=cost(8 * tile * tile * width, 16 * tile * width, 2 * tile * tile * head_count),
        name="attention_forward",
    )(neighbour, query, key, value, *beside)

    by_high = [attended[0]] + [
        shift(attended[high], "seq", high << (1 + plan.col_bits)) for high in range(1, plan.high)
    ]
    pairs = [(attended[0],)] + [
        (shift(attended[0], "seq", q << 1),) for q in range(1, plan.col)
    ]
    for came_high in by_high[1:]:
        pairs.append((came_high,))
        pairs += [
            tuple(shift(came_high[core : core + 1], "seq", q << 1) for core in range(2))
            for q in range(1, plan.col)
        ]
    counts = [len(pair) for pair in pairs]
    pairs = [part for pair in pairs for part in pair]

    dq, dko, dvo, dkf, dvf, dfar = pl.pallas_call(
        backward_kernel,
        out_shape=[
            struct((tile, width), bf16),
            struct((tile, width), f32),
            struct((tile, width), f32),
            struct((tile, width), bf16),
            struct((tile, width), bf16),
            struct((2, tile, width), bf16),
        ],
        in_specs=[smem()] + whole(8),
        out_specs=whole(6),
        scratch_shapes=[pltpu.VMEM((2, tile, width), bf16)],
        compiler_params=params(),
        cost_estimate=cost(1, 1),
        name="attention_backward",
    )(neighbour, query, key, value, *beside, after(grad, attended))

    through = lax.optimization_barrier((dq, *high_columns, jnp.stack(columns[1:])))[-1]
    held = [jnp.stack(columns)]
    late = []
    for high in range(1, plan.high):
        halves = [shift(part, "seq", high << (1 + plan.col_bits)) for part in jnp.split(through, 2, 2)]
        late.append(halves[0])
        rest = jnp.concatenate(halves, 2)
        held.append(jnp.concatenate([high_columns[high - 1][None], rest], 0))
    held = jnp.concatenate(held, 0)

    def product(name, layers, *operands):
        *blocks, for_mate = pl.pallas_call(
            functools.partial(product_kernel, counts, layers),
            out_shape=[struct((HEAD_DIM, mine_width), f32)] * len(layers)
            + [struct((len(layers), HEAD_DIM, mine_width), bf16)],
            in_specs=whole(len(pairs) + 1),
            out_specs=whole(len(layers) + 1),
            scratch_shapes=[pltpu.VMEM((2, len(layers) * HEAD_DIM, plan.pairs * tile), bf16)],
            compiler_params=params(),
            cost_estimate=cost(
                2 * len(layers) * HEAD_DIM * n * tile * mine_width, n * tile * mine_width
            ),
            name=name,
        )(*operands)
        mate = shift(for_mate, "seq", 1)
        return {i: [(block, None, 0), (mate, k, 0)] for k, (i, block) in enumerate(zip(layers, blocks))}

    def added(parts, start, size):
        return pl.pallas_call(
            functools.partial(sum_kernel, [spot for _, *spot in parts], start),
            out_shape=struct((HEAD_DIM, size), bf16),
            in_specs=whole(len(parts)),
            out_specs=pl.BlockSpec(memory_space=pltpu.VMEM),
            compiler_params=params(),
            cost_estimate=cost(len(parts) * HEAD_DIM * size, 4 * len(parts) * HEAD_DIM * size),
            name="block_sum",
        )(*[array for array, *_ in parts])

    first = [i for i in range(m - 1, 1, -1) if i & 1]
    middle = [i for i in range(m - 1, 1, -1) if not i & 1]
    blocks = product("product_first", first, after(pairs[0], dq), *pairs[1:], held)
    going = {i: added(blocks[i], 0, mine_width) for i in first}
    blocks |= product("product_middle", middle, after(pairs[0], *going.values()), *pairs[1:], held)

    blocks |= product("product_near", [1], after(pairs[0], dq), *pairs[1:], held)
    blocks |= product("product_own", [0], after(pairs[0], dq), *pairs[1:], held)

    extra = {i: [] for i in range(m)}
    sent = []
    bit = 1
    while bit < m:
        for i in range(m - 1, 1, -1):
            if i & -i == bit:
                if bit == 1:
                    sent.append(going[i])
                else:
                    (block, *where), *others = blocks[i] + extra[i]
                    sent.append(added([(after(block, dq), *where)] + others, 0, mine_width))
                extra[i ^ bit].append((shift(sent[-1], "dp", bit), None, 0))
        bit *= 2
    far = [
        shift(after(dfar, dq, *late), "seq", 1),
        lax.ppermute(after(dkf, dq), "seq", gives),
        lax.ppermute(after(dvf, dq), "seq", gives),
    ]
    own = blocks[0][0][0]
    came = [blocks[0][1]] + extra[0]
    parts = 1
    size = mine_width // parts
    for start in range(0, mine_width, size):
        near = after(added(blocks[1], start, size), sent[-1], blocks[0][1][0], far[0])
        came.append((shift(near, "dp", 1), None, start))
    dk, dv = pl.pallas_call(
        combine_kernel,
        out_shape=[struct((tile, width), bf16)] * 2,
        in_specs=[smem()] + whole(5),
        out_specs=whole(2),
        compiler_params=params(),
        cost_estimate=cost(6 * tile * width, 20 * tile * width),
        name="key_value_sum",
    )(
        neighbour,
        dko,
        dvo,
        *far,
    )

    x, gram = pl.pallas_call(
        functools.partial(gram_kernel, [spot for _, *spot in came]),
        out_shape=[struct((HEAD_DIM, mine_width), f32), struct((HEAD_DIM, HEAD_DIM), f32)],
        in_specs=whole(1 + len(came)),
        out_specs=whole(2),
        compiler_params=params(),
        cost_estimate=cost(12 * HEAD_DIM * HEAD_DIM * mine_width, 14 * HEAD_DIM * mine_width),
        name="gradient_sum",
    )(own, *[array for array, *_ in came])

    gram_other = jnp.zeros_like(gram)
    for b in range(plan.col_bits):
        gram = gram + gram_other
        gram_other = shift(gram, "seq", 2 << b)

    factor = 0.2 * depth**0.5
    pieces = pl.pallas_call(
        functools.partial(update_kernel, plan, factor),
        out_shape=[struct((HEAD_DIM, slot), f32)] + [struct((HEAD_DIM, slot), bf16)] * (per - 1),
        in_specs=whole(3),
        out_specs=whole(per),
        compiler_params=params(),
        cost_estimate=cost(12 * HEAD_DIM * HEAD_DIM * mine_width, 8 * HEAD_DIM * mine_width),
        name="newton_schulz",
    )(after(x, dk), gram, gram_other)
    pieces = [pieces[0]] + [
        shift(pieces[j], "seq", plan.row_mask(j)) for j in range(1, per)
    ]
    update = pl.pallas_call(
        functools.partial(place_kernel, plan),
        out_shape=struct((per * HEAD_DIM, slot), f32),
        in_specs=whole(per),
        out_specs=pl.BlockSpec(memory_space=pltpu.VMEM),
        compiler_params=params(),
        cost_estimate=cost(1, 8 * per * HEAD_DIM * slot),
        name="update_rows",
    )(*pieces)

    shape = query_tiles.shape
    return dq.reshape(shape), dk.reshape(shape), dv.reshape(shape), update


def solution(mesh):
    tiles = P("dp", "seq", None, None)
    return jax.shard_map(
        local,
        mesh=mesh,
        in_specs=(tiles, tiles, tiles, tiles, tiles, P("dp", None)),
        out_specs=(tiles, tiles, tiles, P("dp", "seq")),
        check_vma=False,
    )
```

```python
import functools
import math

import jax
import jax.numpy as jnp
from jax import lax
from jax.experimental import pallas as pl
from jax.experimental.pallas import tpu as pltpu
from jax.sharding import PartitionSpec as P

HEAD_DIM = 128
NS_STEPS = 5
SCALE = HEAD_DIM ** (-0.5)
LOG2E = math.log2(math.e)
GROUP = 4
coeff_a = 3.4445
coeff_b = -4.775
coeff_c = 2.0315
f32 = jnp.float32
bf16 = jnp.bfloat16
VMEM_LIMIT = 24 * 1024 * 1024


def whole(count):
    return [pl.BlockSpec(memory_space=pltpu.VMEM)] * count


def smem():
    return pl.BlockSpec(memory_space=pltpu.SMEM)


def params():
    return pltpu.CompilerParams(vmem_limit_bytes=VMEM_LIMIT)


def cost(flops, moved, exps=0):
    return pl.CostEstimate(flops=int(flops), bytes_accessed=int(moved), transcendentals=int(exps))


def dot_t(a, b):
    return lax.dot_general(a, b, (((1,), (1,)), ((), ())), preferred_element_type=f32)


def dot_n(a, b):
    return lax.dot_general(a, b, (((1,), (0,)), ((), ())), preferred_element_type=f32)


def dot_l(a, b):
    return lax.dot_general(a, b, (((0,), (0,)), ((), ())), preferred_element_type=f32)


def exact(a, b, dims=((1,), (0,))):
    return lax.dot_general(
        a, b, (dims, ((), ())), precision=lax.Precision.HIGHEST, preferred_element_type=f32
    )


def parts_of(value):
    high = value.astype(bf16)
    rest = value - high.astype(f32)
    middle = rest.astype(bf16)
    return high, middle, (rest - middle.astype(f32)).astype(bf16)


def square_dot(a, b):
    a_high, a_middle, a_low = a
    b_high, b_middle, b_low = b
    size = a_high.shape[0]
    left = jnp.concatenate([a_high, a_middle], 1)
    right = jnp.concatenate(
        [jnp.concatenate([b_high, b_high], 0), jnp.concatenate([b_middle, b_middle], 0)], 1
    )
    wide = dot_n(left, right)
    small = dot_n(jnp.concatenate([a_high, a_low], 1), jnp.concatenate([b_low, b_high], 0))
    return wide[:, :size] + (wide[:, size:] + small)


class Plan:
    def __init__(self, head_count):
        self.seq = lax.axis_size("seq")
        self.dp = lax.axis_size("dp")
        self.per_target = head_count // self.dp
        self.high = self.per_target // 2
        self.col = self.seq // self.per_target
        self.col_bits = self.col.bit_length() - 1
        self.pairs = self.seq // 2

    def row_part(self, place):
        return (place >> (1 + self.col_bits)) * 2 + (place & 1)

    def row_mask(self, part):
        return ((part >> 1) << (1 + self.col_bits)) | (part & 1)

    def col_part(self, place):
        return (place >> 1) & (self.col - 1)


def after(value, *others):
    return lax.optimization_barrier((value, *others))[0]


def shift(value, axis, mask):
    return lax.ppermute(value, axis, [(i, i ^ mask) for i in range(lax.axis_size(axis))])


def head_slice(index):
    return pl.ds(pl.multiple_of(index * HEAD_DIM, HEAD_DIM), HEAD_DIM)


def softmax_keys(query, keys):
    scores = dot_t(keys, query)
    top = jnp.max(scores, axis=0, keepdims=True)
    powers = jnp.exp2((scores - top) * (SCALE * LOG2E))
    return powers * (1.0 / jnp.sum(powers, axis=0, keepdims=True))


def choose_far(near_ref, key_mate, value_mate, key_next, value_next, far):
    place = lax.axis_index("seq")
    is_mate = near_ref[0, place] == (place ^ 1)

    @pl.when(is_mate)
    def _():
        far[0] = key_mate[...]
        far[1] = value_mate[...]

    @pl.when(jnp.logical_not(is_mate))
    def _():
        far[0] = key_next[...]
        far[1] = value_next[...]


def forward_kernel(plan, near_ref, q, ko, vo, km, vm, kn, vn, out, far):
    layer = lax.axis_index("dp")
    choose_far(near_ref, km, vm, kn, vn, far)
    mine = plan.row_part(lax.axis_index("seq"))
    jobs = [(j, i) for j in range(plan.per_target) for i in range(plan.dp)]
    for first in range(0, len(jobs), GROUP):
        group = jobs[first : first + GROUP]
        spots = [head_slice((layer ^ i) * plan.per_target + (mine ^ j)) for j, i in group]
        weights = [
            softmax_keys(q[:, at], jnp.concatenate([ko[:, at], far[0, :, at]], 0)).astype(bf16)
            for at in spots
        ]
        for (j, i), at, p in zip(group, spots, weights, strict=True):
            values = jnp.concatenate([vo[:, at], far[1, :, at]], 0)
            rows = slice(i * HEAD_DIM, (i + 1) * HEAD_DIM)
            out[j >> 1, j & 1, rows, :] = dot_l(values, p).astype(bf16)


def backward_kernel(near_ref, q, ko, vo, km, vm, kn, vn, g, dq, dko, dvo, dkf, dvf, dfar, far):
    choose_far(near_ref, km, vm, kn, vn, far)
    tile = q.shape[0]
    count = q.shape[1] // HEAD_DIM
    for first in range(0, count, GROUP):
        spots = [
            slice(h * HEAD_DIM, (h + 1) * HEAD_DIM)
            for h in range(first, min(first + GROUP, count))
        ]
        weights, slopes = [], []
        for at in spots:
            values = jnp.concatenate([vo[:, at], far[1, :, at]], 0)
            keys = jnp.concatenate([ko[:, at], far[0, :, at]], 0)
            weights.append(softmax_keys(q[:, at], keys))
            slopes.append(dot_t(values, g[:, at]))
        for at, p, dp in zip(spots, weights, slopes, strict=True):
            pb = p.astype(bf16)
            delta = jnp.sum(pb.astype(f32) * dp, axis=0, keepdims=True)
            ds = (p * (dp - delta)).astype(bf16)
            keys = jnp.concatenate([ko[:, at], far[0, :, at]], 0)
            dk = dot_n(ds, q[:, at]) * SCALE
            dv = dot_n(pb, g[:, at])
            dq[:, at] = (dot_l(ds, keys) * SCALE).astype(bf16)
            dko[:, at] = dk[:tile]
            dvo[:, at] = dv[:tile]
            for which, (one, term) in enumerate(((dkf, dk), (dvf, dv))):
                rounded = term[tile:].astype(bf16)
                one[:, at] = rounded
                dfar[which, :, at] = rounded


def combine_kernel(near_ref, dko, dvo, mate, kn, vn, dk, dv):
    place = lax.axis_index("seq")
    last = lax.axis_size("seq") - 1
    other = place + 2 * (place & 1) - 1
    inside = (other >= 0) & (other <= last)
    from_mate = near_ref[0, place ^ 1] == place
    from_other = inside & (near_ref[0, jnp.clip(other, 0, last)] == place)
    for which, (own, beyond, out) in enumerate(((dko, kn, dk), (dvo, vn, dv))):
        total = own[...] + jnp.where(from_mate, mate[which].astype(f32), 0.0)
        out[...] = (total + jnp.where(from_other, beyond[...].astype(f32), 0.0)).astype(bf16)


def product_kernel(counts, layers, *refs):
    att = list(refs[: sum(counts)])
    cols, *outs, for_mate, gathered = refs[sum(counts) :]
    for t, count in enumerate(counts):
        at = slice(t * HEAD_DIM, (t + 1) * HEAD_DIM)
        parts, att = att[:count], att[count:]
        for core in range(2):
            part, row = (parts[0], core) if count == 1 else (parts[core], 0)
            for n, i in enumerate(layers):
                block = part[row, i * HEAD_DIM : (i + 1) * HEAD_DIM, :]
                gathered[core, n * HEAD_DIM : (n + 1) * HEAD_DIM, at] = block
    tokens, width = gathered.shape[2], cols.shape[2]
    step = 512 if width % 512 == 0 else width
    for c in range(0, width, step):
        block = cols[:, :, c : c + step].reshape(tokens, step)
        for n, out in enumerate(outs):
            rows = slice(n * HEAD_DIM, (n + 1) * HEAD_DIM)
            out[:, c : c + step] = dot_n(gathered[0, rows, :], block)
            for_mate[n, :, c : c + step] = dot_n(gathered[1, rows, :], block).astype(bf16)


def piece(ref, lead, start, size):
    at = slice(start, start + size)
    return (ref[:, at] if lead is None else ref[lead, :, at]).astype(f32)


def sum_kernel(spots, start, *refs):
    *parts, out = refs
    size = out.shape[1]
    total = None
    for (lead, first), part in zip(spots, parts, strict=True):
        value = piece(part, lead, start - first, size)
        total = value if total is None else total + value
    out[...] = total.astype(bf16)


def gram_kernel(spots, own, *refs):
    *parts, x, gram = refs
    x[...] = own[...]
    for (lead, first), part in zip(spots, parts, strict=True):
        size = part.shape[-1]
        x[:, first : first + size] += piece(part, lead, 0, size)
    gram[...] = exact(x[...], x[...], ((1,), (1,)))


def polynomial(gram):
    eye = (
        lax.broadcasted_iota(jnp.int32, gram.shape, 0)
        == lax.broadcasted_iota(jnp.int32, gram.shape, 1)
    ).astype(f32)
    square = jnp.sum(jnp.sum(gram * eye, axis=1, keepdims=True), axis=0, keepdims=True)
    inverse = 1.0 / (jnp.sqrt(square) + 1e-07)
    a = gram * inverse * inverse
    p = None
    for turn in range(NS_STEPS):
        a_parts = parts_of(a)
        q = coeff_a * eye + coeff_b * a + coeff_c * square_dot(a_parts, a_parts)
        q_parts = parts_of(q)
        p = q if p is None else square_dot(q_parts, parts_of(p))
        if turn + 1 < NS_STEPS:
            a = square_dot(parts_of(square_dot(q_parts, a_parts)), q_parts)
    return p, inverse


def update_kernel(plan, factor, x, gram, gram_other, *outs):
    mine = plan.row_part(lax.axis_index("seq"))
    p, inverse = polynomial(gram[...] + gram_other[...])
    p = p * (inverse * factor)
    width = outs[0].shape[1]
    for j in range(plan.per_target):
        if width % HEAD_DIM == 0:
            block = x[:, pl.ds(pl.multiple_of((mine ^ j) * width, width), width)]
        else:
            block = jnp.zeros((HEAD_DIM, width), f32)
            for r in range(plan.per_target):
                part = x[:, r * width : (r + 1) * width]
                block = jnp.where((mine ^ j) == r, part, block)
        outs[j][...] = exact(p, block).astype(outs[j].dtype)


def place_kernel(plan, *refs):
    *parts, out = refs
    mine = plan.row_part(lax.axis_index("seq"))
    for j, part in enumerate(parts):
        at = pl.ds(pl.multiple_of((mine ^ j) * HEAD_DIM, HEAD_DIM), HEAD_DIM)
        out[at, :] = part[...].astype(f32)


def local(query_tiles, key_tiles, value_tiles, attn_grad, proj_grad, neighbour):
    tile, width = query_tiles.shape[2:]
    depth = proj_grad.shape[3]
    head_count = width // HEAD_DIM
    plan = Plan(head_count)
    n, m, per = plan.seq, plan.dp, plan.per_target
    place = lax.axis_index("seq")
    struct = jax.ShapeDtypeStruct
    query, key, value, grad = (
        a.reshape(tile, width) for a in (query_tiles, key_tiles, value_tiles, attn_grad)
    )

    steps = [(i, i + 1) for i in range(1, n - 1, 2)]
    back = [(j, i) for i, j in steps]
    takes = [(i, j) for i, j in steps if j != n - 2] + [(j, i) for j, i in back if i != 1]
    gives = [(i, j) for i, j in steps if i != 1] + [(j, i) for j, i in back if j != n - 2]
    key_next = lax.ppermute(key, "seq", takes)
    value_next = lax.ppermute(value, "seq", takes)
    slot = depth // n
    flat = proj_grad.reshape(tile, depth)
    mine = plan.col_part(place)
    mine_width = per * slot

    def column_part(part):
        return jnp.concatenate(
            [
                lax.dynamic_slice_in_dim(flat, (high * plan.col + part) * 2 * slot, 2 * slot, 1)
                for high in range(plan.high)
            ],
            1,
        )

    own_columns = column_part(mine)
    key_mate = shift(after(key, own_columns), "seq", 1)
    value_mate = shift(after(value, own_columns), "seq", 1)
    beside = (key_mate, value_mate, key_next, value_next)
    columns = [own_columns] + [
        shift(after(column_part(mine ^ q), key_next, value_next), "seq", q << 1)
        for q in range(1, plan.col)
    ]
    high_columns = [
        shift(own_columns, "seq", high << (1 + plan.col_bits))
        for high in range(1, plan.high)
    ]

    attended = pl.pallas_call(
        functools.partial(forward_kernel, plan),
        out_shape=struct((plan.high, 2, m * HEAD_DIM, tile), bf16),
        in_specs=[smem()] + whole(7),
        out_specs=pl.BlockSpec(memory_space=pltpu.VMEM),
        scratch_shapes=[pltpu.VMEM((2, tile, width), bf16)],
        compiler_params=params(),
        cost_estimate=cost(8 * tile * tile * width, 16 * tile * width, 2 * tile * tile * head_count),
        name="attention_forward",
    )(neighbour, query, key, value, *beside)

    by_high = [attended[0]] + [
        shift(attended[high], "seq", high << (1 + plan.col_bits)) for high in range(1, plan.high)
    ]
    pairs = [(attended[0],)] + [
        (shift(attended[0], "seq", q << 1),) for q in range(1, plan.col)
    ]
    for came_high in by_high[1:]:
        pairs.append((came_high,))
        pairs += [
            tuple(shift(came_high[core : core + 1], "seq", q << 1) for core in range(2))
            for q in range(1, plan.col)
        ]
    counts = [len(pair) for pair in pairs]
    pairs = [part for pair in pairs for part in pair]

    dq, dko, dvo, dkf, dvf, dfar = pl.pallas_call(
        backward_kernel,
        out_shape=[
            struct((tile, width), bf16),
            struct((tile, width), f32),
            struct((tile, width), f32),
            struct((tile, width), bf16),
            struct((tile, width), bf16),
            struct((2, tile, width), bf16),
        ],
        in_specs=[smem()] + whole(8),
        out_specs=whole(6),
        scratch_shapes=[pltpu.VMEM((2, tile, width), bf16)],
        compiler_params=params(),
        cost_estimate=cost(1, 1),
        name="attention_backward",
    )(neighbour, query, key, value, *beside, after(grad, attended))

    through = lax.optimization_barrier((dq, *high_columns, jnp.stack(columns[1:])))[-1]
    held = [jnp.stack(columns)]
    late = []
    for high in range(1, plan.high):
        halves = [shift(part, "seq", high << (1 + plan.col_bits)) for part in jnp.split(through, 2, 2)]
        late.append(halves[0])
        rest = jnp.concatenate(halves, 2)
        held.append(jnp.concatenate([high_columns[high - 1][None], rest], 0))
    held = jnp.concatenate(held, 0)

    def product(name, layers, *operands):
        *blocks, for_mate = pl.pallas_call(
            functools.partial(product_kernel, counts, layers),
            out_shape=[struct((HEAD_DIM, mine_width), f32)] * len(layers)
            + [struct((len(layers), HEAD_DIM, mine_width), bf16)],
            in_specs=whole(len(pairs) + 1),
            out_specs=whole(len(layers) + 1),
            scratch_shapes=[pltpu.VMEM((2, len(layers) * HEAD_DIM, plan.pairs * tile), bf16)],
            compiler_params=params(),
            cost_estimate=cost(
                2 * len(layers) * HEAD_DIM * n * tile * mine_width, n * tile * mine_width
            ),
            name=name,
        )(*operands)
        mate = shift(for_mate, "seq", 1)
        return {i: [(block, None, 0), (mate, k, 0)] for k, (i, block) in enumerate(zip(layers, blocks))}

    def added(parts, start, size):
        return pl.pallas_call(
            functools.partial(sum_kernel, [spot for _, *spot in parts], start),
            out_shape=struct((HEAD_DIM, size), bf16),
            in_specs=whole(len(parts)),
            out_specs=pl.BlockSpec(memory_space=pltpu.VMEM),
            compiler_params=params(),
            cost_estimate=cost(len(parts) * HEAD_DIM * size, 4 * len(parts) * HEAD_DIM * size),
            name="block_sum",
        )(*[array for array, *_ in parts])

    first = [i for i in range(m - 1, 1, -1) if i & 1]
    middle = [i for i in range(m - 1, 1, -1) if not i & 1]
    blocks = product("product_first", first, after(pairs[0], dq), *pairs[1:], held)
    going = {i: added(blocks[i], 0, mine_width) for i in first}
    blocks |= product("product_middle", middle, after(pairs[0], *going.values()), *pairs[1:], held)

    blocks |= product("product_near", [1], after(pairs[0], dq), *pairs[1:], held)
    blocks |= product("product_own", [0], after(pairs[0], dq), *pairs[1:], held)

    extra = {i: [] for i in range(m)}
    sent = []
    bit = 1
    while bit < m:
        for i in range(m - 1, 1, -1):
            if i & -i == bit:
                if bit == 1:
                    sent.append(going[i])
                else:
                    (block, *where), *others = blocks[i] + extra[i]
                    sent.append(added([(after(block, dq), *where)] + others, 0, mine_width))
                extra[i ^ bit].append((shift(sent[-1], "dp", bit), None, 0))
        bit *= 2
    far = [
        shift(after(dfar, dq, *late), "seq", 1),
        lax.ppermute(after(dkf, dq), "seq", gives),
        lax.ppermute(after(dvf, dq), "seq", gives),
    ]
    own = blocks[0][0][0]
    came = [blocks[0][1]] + extra[0]
    parts = 1
    size = mine_width // parts
    for start in range(0, mine_width, size):
        near = after(added(blocks[1], start, size), sent[-1], blocks[0][1][0], far[0])
        came.append((shift(near, "dp", 1), None, start))
    dk, dv = pl.pallas_call(
        combine_kernel,
        out_shape=[struct((tile, width), bf16)] * 2,
        in_specs=[smem()] + whole(5),
        out_specs=whole(2),
        compiler_params=params(),
        cost_estimate=cost(6 * tile * width, 20 * tile * width),
        name="key_value_sum",
    )(
        neighbour,
        dko,
        dvo,
        *far,
    )

    x, gram = pl.pallas_call(
        functools.partial(gram_kernel, [spot for _, *spot in came]),
        out_shape=[struct((HEAD_DIM, mine_width), f32), struct((HEAD_DIM, HEAD_DIM), f32)],
        in_specs=whole(1 + len(came)),
        out_specs=whole(2),
        compiler_params=params(),
        cost_estimate=cost(12 * HEAD_DIM * HEAD_DIM * mine_width, 14 * HEAD_DIM * mine_width),
        name="gradient_sum",
    )(own, *[array for array, *_ in came])

    gram_other = jnp.zeros_like(gram)
    for b in range(plan.col_bits):
        gram = gram + gram_other
        gram_other = shift(gram, "seq", 2 << b)

    factor = 0.2 * depth**0.5
    pieces = pl.pallas_call(
        functools.partial(update_kernel, plan, factor),
        out_shape=[struct((HEAD_DIM, slot), f32)] + [struct((HEAD_DIM, slot), bf16)] * (per - 1),
        in_specs=whole(3),
        out_specs=whole(per),
        compiler_params=params(),
        cost_estimate=cost(12 * HEAD_DIM * HEAD_DIM * mine_width, 8 * HEAD_DIM * mine_width),
        name="newton_schulz",
    )(after(x, dk), gram, gram_other)
    pieces = [pieces[0]] + [
        shift(pieces[j], "seq", plan.row_mask(j)) for j in range(1, per)
    ]
    update = pl.pallas_call(
        functools.partial(place_kernel, plan),
        out_shape=struct((per * HEAD_DIM, slot), f32),
        in_specs=whole(per),
        out_specs=pl.BlockSpec(memory_space=pltpu.VMEM),
        compiler_params=params(),
        cost_estimate=cost(1, 8 * per * HEAD_DIM * slot),
        name="update_rows",
    )(*pieces)

    shape = query_tiles.shape
    return dq.reshape(shape), dk.reshape(shape), dv.reshape(shape), update


def solution(mesh):
    tiles = P("dp", "seq", None, None)
    return jax.shard_map(
        local,
        mesh=mesh,
        in_specs=(tiles, tiles, tiles, tiles, tiles, P("dp", None)),
        out_specs=(tiles, tiles, tiles, P("dp", "seq")),
        check_vma=False,
    )
```

```python
import functools
import math

import jax
import jax.numpy as jnp
from jax import lax
from jax.experimental import pallas as pl
from jax.experimental.pallas import tpu as pltpu
from jax.sharding import PartitionSpec as P

HEAD_DIM = 128
NS_STEPS = 5
SCALE = HEAD_DIM ** (-0.5)
LOG2E = math.log2(math.e)
GROUP = 4
coeff_a = 3.4445
coeff_b = -4.775
coeff_c = 2.0315
f32 = jnp.float32
bf16 = jnp.bfloat16
VMEM_LIMIT = 24 * 1024 * 1024


def whole(count):
    return [pl.BlockSpec(memory_space=pltpu.VMEM)] * count


def smem():
    return pl.BlockSpec(memory_space=pltpu.SMEM)


def params():
    return pltpu.CompilerParams(vmem_limit_bytes=VMEM_LIMIT)


def cost(flops, moved, exps=0):
    return pl.CostEstimate(flops=int(flops), bytes_accessed=int(moved), transcendentals=int(exps))


def dot_t(a, b):
    return lax.dot_general(a, b, (((1,), (1,)), ((), ())), preferred_element_type=f32)


def dot_n(a, b):
    return lax.dot_general(a, b, (((1,), (0,)), ((), ())), preferred_element_type=f32)


def dot_l(a, b):
    return lax.dot_general(a, b, (((0,), (0,)), ((), ())), preferred_element_type=f32)


def exact(a, b, dims=((1,), (0,))):
    return lax.dot_general(
        a, b, (dims, ((), ())), precision=lax.Precision.HIGHEST, preferred_element_type=f32
    )


def parts_of(value):
    high = value.astype(bf16)
    rest = value - high.astype(f32)
    middle = rest.astype(bf16)
    return high, middle, (rest - middle.astype(f32)).astype(bf16)


def split_dot(a, b):
    a_high, a_middle, a_low = a
    b_high, b_middle, b_low = b
    size = b_high.shape[1]
    left = jnp.concatenate([a_high, a_middle], 1)
    right = jnp.concatenate(
        [jnp.concatenate([b_high, b_high], 0), jnp.concatenate([b_middle, b_middle], 0)], 1
    )
    wide = dot_n(left, right)
    small = dot_n(jnp.concatenate([a_high, a_low], 1), jnp.concatenate([b_low, b_high], 0))
    return wide[:, :size] + (wide[:, size:] + small)


class Plan:
    def __init__(self, head_count):
        self.seq = lax.axis_size("seq")
        self.dp = lax.axis_size("dp")
        self.per_target = head_count // self.dp
        self.high = self.per_target // 2
        self.col = self.seq // self.per_target
        self.col_bits = self.col.bit_length() - 1
        self.pairs = self.seq // 2

    def row_part(self, place):
        return (place >> (1 + self.col_bits)) * 2 + (place & 1)

    def row_mask(self, part):
        return ((part >> 1) << (1 + self.col_bits)) | (part & 1)

    def col_part(self, place):
        return (place >> 1) & (self.col - 1)


def after(value, *others):
    return lax.optimization_barrier((value, *others))[0]


def shift(value, axis, mask):
    return lax.ppermute(value, axis, [(i, i ^ mask) for i in range(lax.axis_size(axis))])


def head_slice(index):
    return pl.ds(pl.multiple_of(index * HEAD_DIM, HEAD_DIM), HEAD_DIM)


def softmax_keys(query, keys):
    scores = dot_t(keys, query)
    top = jnp.max(scores, axis=0, keepdims=True)
    powers = jnp.exp2((scores - top) * (SCALE * LOG2E))
    return powers * (1.0 / jnp.sum(powers, axis=0, keepdims=True))


def choose_far(near_ref, key_mate, value_mate, key_next, value_next, far):
    place = lax.axis_index("seq")
    is_mate = near_ref[0, place] == (place ^ 1)

    @pl.when(is_mate)
    def _():
        far[0] = key_mate[...]
        far[1] = value_mate[...]

    @pl.when(jnp.logical_not(is_mate))
    def _():
        far[0] = key_next[...]
        far[1] = value_next[...]


def forward_kernel(plan, near_ref, q, ko, vo, km, vm, kn, vn, out, far):
    layer = lax.axis_index("dp")
    choose_far(near_ref, km, vm, kn, vn, far)
    mine = plan.row_part(lax.axis_index("seq"))
    jobs = [(j, i) for j in range(plan.per_target) for i in range(plan.dp)]
    for first in range(0, len(jobs), GROUP):
        group = jobs[first : first + GROUP]
        spots = [head_slice((layer ^ i) * plan.per_target + (mine ^ j)) for j, i in group]
        weights = [
            softmax_keys(q[:, at], jnp.concatenate([ko[:, at], far[0, :, at]], 0)).astype(bf16)
            for at in spots
        ]
        for (j, i), at, p in zip(group, spots, weights, strict=True):
            values = jnp.concatenate([vo[:, at], far[1, :, at]], 0)
            rows = slice(i * HEAD_DIM, (i + 1) * HEAD_DIM)
            out[j >> 1, j & 1, rows, :] = dot_l(values, p).astype(bf16)


def backward_kernel(near_ref, q, ko, vo, km, vm, kn, vn, g, dq, dko, dvo, dkf, dvf, dfar, far):
    choose_far(near_ref, km, vm, kn, vn, far)
    tile = q.shape[0]
    count = q.shape[1] // HEAD_DIM
    for first in range(0, count, GROUP):
        spots = [
            slice(h * HEAD_DIM, (h + 1) * HEAD_DIM)
            for h in range(first, min(first + GROUP, count))
        ]
        weights, slopes = [], []
        for at in spots:
            values = jnp.concatenate([vo[:, at], far[1, :, at]], 0)
            keys = jnp.concatenate([ko[:, at], far[0, :, at]], 0)
            weights.append(softmax_keys(q[:, at], keys))
            slopes.append(dot_t(values, g[:, at]))
        for at, p, dp in zip(spots, weights, slopes, strict=True):
            pb = p.astype(bf16)
            delta = jnp.sum(pb.astype(f32) * dp, axis=0, keepdims=True)
            ds = (p * (dp - delta)).astype(bf16)
            keys = jnp.concatenate([ko[:, at], far[0, :, at]], 0)
            dk = dot_n(ds, q[:, at]) * SCALE
            dv = dot_n(pb, g[:, at])
            dq[:, at] = (dot_l(ds, keys) * SCALE).astype(bf16)
            dko[:, at] = dk[:tile]
            dvo[:, at] = dv[:tile]
            for which, (one, term) in enumerate(((dkf, dk), (dvf, dv))):
                rounded = term[tile:].astype(bf16)
                one[:, at] = rounded
                dfar[which, :, at] = rounded


def combine_kernel(near_ref, dko, dvo, mate, kn, vn, dk, dv):
    place = lax.axis_index("seq")
    last = lax.axis_size("seq") - 1
    other = place + 2 * (place & 1) - 1
    inside = (other >= 0) & (other <= last)
    from_mate = near_ref[0, place ^ 1] == place
    from_other = inside & (near_ref[0, jnp.clip(other, 0, last)] == place)
    for which, (own, beyond, out) in enumerate(((dko, kn, dk), (dvo, vn, dv))):
        total = own[...] + jnp.where(from_mate, mate[which].astype(f32), 0.0)
        out[...] = (total + jnp.where(from_other, beyond[...].astype(f32), 0.0)).astype(bf16)


def product_kernel(counts, layers, cores, *refs):
    att = list(refs[: sum(counts)])
    cols, *outs, gathered = refs[sum(counts) :]
    owns, for_mate = outs[: len(layers) * (0 in cores)], outs[-1]
    for t, count in enumerate(counts):
        at = slice(t * HEAD_DIM, (t + 1) * HEAD_DIM)
        parts, att = att[:count], att[count:]
        for core in cores:
            part, row = (parts[0], core) if count == 1 else (parts[core], 0)
            for n, i in enumerate(layers):
                block = part[row, i * HEAD_DIM : (i + 1) * HEAD_DIM, :]
                gathered[core, n * HEAD_DIM : (n + 1) * HEAD_DIM, at] = block
    tokens, width = gathered.shape[2], cols.shape[2]
    step = 512 if width % 512 == 0 else width
    for c in range(0, width, step):
        block = cols[:, :, c : c + step].reshape(tokens, step)
        for n in range(len(layers)):
            rows = slice(n * HEAD_DIM, (n + 1) * HEAD_DIM)
            if 0 in cores:
                owns[n][:, c : c + step] = dot_n(gathered[0, rows, :], block)
            if 1 in cores:
                for_mate[n, :, c : c + step] = dot_n(gathered[1, rows, :], block).astype(bf16)


def piece(ref, lead, start, size):
    at = slice(start, start + size)
    return (ref[:, at] if lead is None else ref[lead, :, at]).astype(f32)


def sum_kernel(spots, start, *refs):
    *parts, out = refs
    size = out.shape[1]
    total = None
    for (lead, first), part in zip(spots, parts, strict=True):
        value = piece(part, lead, start - first, size)
        total = value if total is None else total + value
    out[...] = total.astype(bf16)


def gram_kernel(spots, own, *refs):
    *parts, x, gram = refs
    x[...] = own[...]
    for (lead, first), part in zip(spots, parts, strict=True):
        size = part.shape[-1]
        x[:, first : first + size] += piece(part, lead, 0, size)
    gram[...] = exact(x[...], x[...], ((1,), (1,)))


def polynomial(gram):
    eye = (
        lax.broadcasted_iota(jnp.int32, gram.shape, 0)
        == lax.broadcasted_iota(jnp.int32, gram.shape, 1)
    ).astype(f32)
    square = jnp.sum(jnp.sum(gram * eye, axis=1, keepdims=True), axis=0, keepdims=True)
    inverse = 1.0 / (jnp.sqrt(square) + 1e-07)
    a = gram * inverse * inverse
    p = None
    for turn in range(NS_STEPS):
        a_parts = parts_of(a)
        q = coeff_a * eye + coeff_b * a + coeff_c * split_dot(a_parts, a_parts)
        q_parts = parts_of(q)
        p = q if p is None else split_dot(q_parts, parts_of(p))
        if turn + 1 < NS_STEPS:
            a = split_dot(parts_of(split_dot(q_parts, a_parts)), q_parts)
    return p, inverse


def update_kernel(plan, factor, x, gram, gram_other, *outs):
    mine = plan.row_part(lax.axis_index("seq"))
    p, inverse = polynomial(gram[...] + gram_other[...])
    p = p * (inverse * factor)
    p_parts = parts_of(p)
    width = outs[0].shape[1]
    wide = width % HEAD_DIM == 0
    for j in range(plan.per_target):
        if width % HEAD_DIM == 0:
            block = x[:, pl.ds(pl.multiple_of((mine ^ j) * width, width), width)]
        else:
            block = jnp.zeros((HEAD_DIM, width), f32)
            for r in range(plan.per_target):
                part = x[:, r * width : (r + 1) * width]
                block = jnp.where((mine ^ j) == r, part, block)
        piece_out = split_dot(p_parts, parts_of(block)) if wide else exact(p, block)
        outs[j][...] = piece_out.astype(outs[j].dtype)


def place_kernel(plan, *refs):
    *parts, out = refs
    parts = parts[::-1]
    mine = plan.row_part(lax.axis_index("seq"))
    for j, part in enumerate(parts):
        at = pl.ds(pl.multiple_of((mine ^ j) * HEAD_DIM, HEAD_DIM), HEAD_DIM)
        out[at, :] = part[...].astype(f32)


def local(query_tiles, key_tiles, value_tiles, attn_grad, proj_grad, neighbour):
    tile, width = query_tiles.shape[2:]
    depth = proj_grad.shape[3]
    head_count = width // HEAD_DIM
    plan = Plan(head_count)
    n, m, per = plan.seq, plan.dp, plan.per_target
    place = lax.axis_index("seq")
    struct = jax.ShapeDtypeStruct
    query, key, value, grad = (
        a.reshape(tile, width) for a in (query_tiles, key_tiles, value_tiles, attn_grad)
    )

    steps = [(i, i + 1) for i in range(1, n - 1, 2)]
    back = [(j, i) for i, j in steps]
    takes = [(i, j) for i, j in steps if j != n - 2] + [(j, i) for j, i in back if i != 1]
    gives = [(i, j) for i, j in steps if i != 1] + [(j, i) for j, i in back if j != n - 2]
    key_next = lax.ppermute(key, "seq", takes)
    value_next = lax.ppermute(value, "seq", takes)
    slot = depth // n
    flat = proj_grad.reshape(tile, depth)
    mine = plan.col_part(place)
    mine_width = per * slot

    def column_part(part):
        return jnp.concatenate(
            [
                lax.dynamic_slice_in_dim(flat, (high * plan.col + part) * 2 * slot, 2 * slot, 1)
                for high in range(plan.high)
            ],
            1,
        )

    own_columns = column_part(mine)
    key_mate = shift(after(key, own_columns), "seq", 1)
    value_mate = shift(after(value, own_columns), "seq", 1)
    beside = (key_mate, value_mate, key_next, value_next)
    columns = [own_columns] + [
        shift(after(column_part(mine ^ q), key_next, value_next), "seq", q << 1)
        for q in range(1, plan.col)
    ]
    high_columns = [
        shift(own_columns, "seq", high << (1 + plan.col_bits))
        for high in range(1, plan.high)
    ]

    attended = pl.pallas_call(
        functools.partial(forward_kernel, plan),
        out_shape=struct((plan.high, 2, m * HEAD_DIM, tile), bf16),
        in_specs=[smem()] + whole(7),
        out_specs=pl.BlockSpec(memory_space=pltpu.VMEM),
        scratch_shapes=[pltpu.VMEM((2, tile, width), bf16)],
        compiler_params=params(),
        cost_estimate=cost(8 * tile * tile * width, 16 * tile * width, 2 * tile * tile * head_count),
        name="attention_forward",
    )(neighbour, query, key, value, *beside)

    by_high = [attended[0]] + [
        shift(attended[high], "seq", high << (1 + plan.col_bits)) for high in range(1, plan.high)
    ]
    pairs = [(attended[0],)] + [
        (shift(attended[0], "seq", q << 1),) for q in range(1, plan.col)
    ]
    for came_high in by_high[1:]:
        pairs.append((came_high,))
        pairs += [
            tuple(shift(came_high[core : core + 1], "seq", q << 1) for core in range(2))
            for q in range(1, plan.col)
        ]
    counts = [len(pair) for pair in pairs]
    pairs = [part for pair in pairs for part in pair]

    dq, dko, dvo, dkf, dvf, dfar = pl.pallas_call(
        backward_kernel,
        out_shape=[
            struct((tile, width), bf16),
            struct((tile, width), f32),
            struct((tile, width), f32),
            struct((tile, width), bf16),
            struct((tile, width), bf16),
            struct((2, tile, width), bf16),
        ],
        in_specs=[smem()] + whole(8),
        out_specs=whole(6),
        scratch_shapes=[pltpu.VMEM((2, tile, width), bf16)],
        compiler_params=params(),
        cost_estimate=cost(1, 1),
        name="attention_backward",
    )(neighbour, query, key, value, *beside, after(grad, attended))

    through = lax.optimization_barrier((dq, *high_columns, jnp.stack(columns[1:])))[-1]
    held = [jnp.stack(columns)]
    late = []
    for high in range(1, plan.high):
        halves = [shift(part, "seq", high << (1 + plan.col_bits)) for part in jnp.split(through, 2, 2)]
        late.append(halves[0])
        rest = jnp.concatenate(halves, 2)
        held.append(jnp.concatenate([high_columns[high - 1][None], rest], 0))
    held = jnp.concatenate(held, 0)

    def product(name, layers, cores, *operands):
        shapes = [struct((HEAD_DIM, mine_width), f32)] * (len(layers) * (0 in cores))
        shapes += [struct((len(layers), HEAD_DIM, mine_width), bf16)] * (1 in cores)
        return pl.pallas_call(
            functools.partial(product_kernel, counts, layers, cores),
            out_shape=shapes,
            in_specs=whole(len(pairs) + 1),
            out_specs=whole(len(shapes)),
            scratch_shapes=[pltpu.VMEM((2, len(layers) * HEAD_DIM, plan.pairs * tile), bf16)],
            compiler_params=params(),
            cost_estimate=cost(
                len(cores) * len(layers) * HEAD_DIM * n * tile * mine_width,
                n * tile * mine_width,
            ),
            name=name,
        )(*operands)

    def swapped(layers, blocks, for_mate):
        mate = shift(for_mate, "seq", 1)
        return {
            i: [(block, None, 0), (mate, k, 0)]
            for k, (i, block) in enumerate(zip(layers, blocks, strict=True))
        }

    def product_pair(name, layers, *operands):
        *blocks, for_mate = product(name, layers, (0, 1), *operands)
        return swapped(layers, blocks, for_mate)

    def added(parts, start, size):
        return pl.pallas_call(
            functools.partial(sum_kernel, [spot for _, *spot in parts], start),
            out_shape=struct((HEAD_DIM, size), bf16),
            in_specs=whole(len(parts)),
            out_specs=pl.BlockSpec(memory_space=pltpu.VMEM),
            compiler_params=params(),
            cost_estimate=cost(len(parts) * HEAD_DIM * size, 4 * len(parts) * HEAD_DIM * size),
            name="block_sum",
        )(*[array for array, *_ in parts])

    first = [i for i in range(m - 1, 1, -1) if i & 1]
    middle = [i for i in range(m - 1, 1, -1) if not i & 1]
    (for_mate,) = product("product_mate", first, (1,), after(pairs[0], dq), *pairs[1:], held)
    own_first = product("product_first", first, (0,), after(pairs[0], for_mate), *pairs[1:], held)
    blocks = swapped(first, own_first, for_mate)
    going = {i: added(blocks[i], 0, mine_width) for i in first}
    blocks |= product_pair("product_middle", middle, after(pairs[0], *going.values()), *pairs[1:], held)

    blocks |= product_pair("product_near", [1], after(pairs[0], dq), *pairs[1:], held)
    blocks |= product_pair("product_own", [0], after(pairs[0], dq), *pairs[1:], held)

    extra = {i: [] for i in range(m)}
    sent = []
    bit = 1
    while bit < m:
        for i in range(m - 1, 1, -1):
            if i & -i == bit:
                if bit == 1:
                    sent.append(going[i])
                else:
                    (block, *where), *others = blocks[i] + extra[i]
                    sent.append(added([(after(block, dq), *where)] + others, 0, mine_width))
                extra[i ^ bit].append((shift(sent[-1], "dp", bit), None, 0))
        bit *= 2
    far = [
        shift(after(dfar, dq, *late), "seq", 1),
        lax.ppermute(after(dkf, dq), "seq", gives),
        lax.ppermute(after(dvf, dq), "seq", gives),
    ]
    own = blocks[0][0][0]
    came = [blocks[0][1]] + extra[0]
    parts = 1
    size = mine_width // parts
    for start in range(0, mine_width, size):
        near = after(added(blocks[1], start, size), sent[-1], blocks[0][1][0], far[0])
        came.append((shift(near, "dp", 1), None, start))
    dk, dv = pl.pallas_call(
        combine_kernel,
        out_shape=[struct((tile, width), bf16)] * 2,
        in_specs=[smem()] + whole(5),
        out_specs=whole(2),
        compiler_params=params(),
        cost_estimate=cost(6 * tile * width, 20 * tile * width),
        name="key_value_sum",
    )(
        neighbour,
        dko,
        dvo,
        *far,
    )

    x, gram = pl.pallas_call(
        functools.partial(gram_kernel, [spot for _, *spot in came]),
        out_shape=[struct((HEAD_DIM, mine_width), f32), struct((HEAD_DIM, HEAD_DIM), f32)],
        in_specs=whole(1 + len(came)),
        out_specs=whole(2),
        compiler_params=params(),
        cost_estimate=cost(12 * HEAD_DIM * HEAD_DIM * mine_width, 14 * HEAD_DIM * mine_width),
        name="gradient_sum",
    )(own, *[array for array, *_ in came])

    gram_other = jnp.zeros_like(gram)
    for b in range(plan.col_bits):
        gram = gram + gram_other
        gram_other = shift(gram, "seq", 2 << b)

    factor = 0.2 * depth**0.5
    pieces = pl.pallas_call(
        functools.partial(update_kernel, plan, factor),
        out_shape=[struct((HEAD_DIM, slot), f32)] + [struct((HEAD_DIM, slot), bf16)] * (per - 1),
        in_specs=whole(3),
        out_specs=whole(per),
        compiler_params=params(),
        cost_estimate=cost(12 * HEAD_DIM * HEAD_DIM * mine_width, 8 * HEAD_DIM * mine_width),
        name="newton_schulz",
    )(after(x, dk), gram, gram_other)
    pieces = [pieces[0]] + [
        shift(pieces[j], "seq", plan.row_mask(j)) for j in range(1, per)
    ]
    update = pl.pallas_call(
        functools.partial(place_kernel, plan),
        out_shape=struct((per * HEAD_DIM, slot), f32),
        in_specs=whole(per),
        out_specs=pl.BlockSpec(memory_space=pltpu.VMEM),
        compiler_params=params(),
        cost_estimate=cost(1, 8 * per * HEAD_DIM * slot),
        name="update_rows",
    )(*reversed(pieces))

    shape = query_tiles.shape
    return dq.reshape(shape), dk.reshape(shape), dv.reshape(shape), update


def solution(mesh):
    tiles = P("dp", "seq", None, None)
    return jax.shard_map(
        local,
        mesh=mesh,
        in_specs=(tiles, tiles, tiles, tiles, tiles, P("dp", None)),
        out_specs=(tiles, tiles, tiles, P("dp", "seq")),
        check_vma=False,
    )
```

```python
import functools
import math

import jax
import jax.numpy as jnp
from jax import lax
from jax.experimental import pallas as pl
from jax.experimental.pallas import tpu as pltpu
from jax.sharding import PartitionSpec as P

HEAD_DIM = 128
NS_STEPS = 5
SCALE = HEAD_DIM ** (-0.5)
LOG2E = math.log2(math.e)
GROUP = 4
coeff_a = 3.4445
coeff_b = -4.775
coeff_c = 2.0315
f32 = jnp.float32
bf16 = jnp.bfloat16
VMEM_LIMIT = 24 * 1024 * 1024


def whole(count):
    return [pl.BlockSpec(memory_space=pltpu.VMEM)] * count


def smem():
    return pl.BlockSpec(memory_space=pltpu.SMEM)


def params():
    return pltpu.CompilerParams(vmem_limit_bytes=VMEM_LIMIT)


def cost(flops, moved, exps=0):
    return pl.CostEstimate(flops=int(flops), bytes_accessed=int(moved), transcendentals=int(exps))


def dot_t(a, b):
    return lax.dot_general(a, b, (((1,), (1,)), ((), ())), preferred_element_type=f32)


def dot_n(a, b):
    return lax.dot_general(a, b, (((1,), (0,)), ((), ())), preferred_element_type=f32)


def dot_l(a, b):
    return lax.dot_general(a, b, (((0,), (0,)), ((), ())), preferred_element_type=f32)


def exact(a, b, dims=((1,), (0,))):
    return lax.dot_general(
        a, b, (dims, ((), ())), precision=lax.Precision.HIGHEST, preferred_element_type=f32
    )


def parts_of(value):
    high = value.astype(bf16)
    rest = value - high.astype(f32)
    middle = rest.astype(bf16)
    return high, middle, (rest - middle.astype(f32)).astype(bf16)


def split_dot(a, b):
    a_high, a_middle, a_low = a
    b_high, b_middle, b_low = b
    size = b_high.shape[1]
    left = jnp.concatenate([a_high, a_middle], 1)
    right = jnp.concatenate(
        [jnp.concatenate([b_high, b_high], 0), jnp.concatenate([b_middle, b_middle], 0)], 1
    )
    wide = dot_n(left, right)
    small = dot_n(jnp.concatenate([a_high, a_low], 1), jnp.concatenate([b_low, b_high], 0))
    return wide[:, :size] + (wide[:, size:] + small)


class Plan:
    def __init__(self, head_count):
        self.seq = lax.axis_size("seq")
        self.dp = lax.axis_size("dp")
        self.per_target = head_count // self.dp
        self.high = self.per_target // 2
        self.col = self.seq // self.per_target
        self.col_bits = self.col.bit_length() - 1
        self.pairs = self.seq // 2

    def row_part(self, place):
        return (place >> (1 + self.col_bits)) * 2 + (place & 1)

    def row_mask(self, part):
        return ((part >> 1) << (1 + self.col_bits)) | (part & 1)

    def col_part(self, place):
        return (place >> 1) & (self.col - 1)


def after(value, *others):
    return lax.optimization_barrier((value, *others))[0]


def shift(value, axis, mask):
    return lax.ppermute(value, axis, [(i, i ^ mask) for i in range(lax.axis_size(axis))])


def head_slice(index):
    return pl.ds(pl.multiple_of(index * HEAD_DIM, HEAD_DIM), HEAD_DIM)


def softmax_keys(query, keys):
    scores = dot_t(keys, query)
    top = jnp.max(scores, axis=0, keepdims=True)
    powers = jnp.exp2((scores - top) * (SCALE * LOG2E))
    return powers * (1.0 / jnp.sum(powers, axis=0, keepdims=True))


def choose_far(near_ref, key_mate, value_mate, key_next, value_next, far):
    place = lax.axis_index("seq")
    is_mate = near_ref[0, place] == (place ^ 1)

    @pl.when(is_mate)
    def _():
        far[0] = key_mate[...]
        far[1] = value_mate[...]

    @pl.when(jnp.logical_not(is_mate))
    def _():
        far[0] = key_next[...]
        far[1] = value_next[...]


def forward_kernel(plan, near_ref, q, ko, vo, km, vm, kn, vn, out, far):
    layer = lax.axis_index("dp")
    choose_far(near_ref, km, vm, kn, vn, far)
    mine = plan.row_part(lax.axis_index("seq"))
    jobs = [(j, i) for j in range(plan.per_target) for i in range(plan.dp)]
    for first in range(0, len(jobs), GROUP):
        group = jobs[first : first + GROUP]
        spots = [head_slice((layer ^ i) * plan.per_target + (mine ^ j)) for j, i in group]
        weights = [
            softmax_keys(q[:, at], jnp.concatenate([ko[:, at], far[0, :, at]], 0)).astype(bf16)
            for at in spots
        ]
        for (j, i), at, p in zip(group, spots, weights, strict=True):
            values = jnp.concatenate([vo[:, at], far[1, :, at]], 0)
            rows = slice(i * HEAD_DIM, (i + 1) * HEAD_DIM)
            out[j >> 1, j & 1, rows, :] = dot_l(values, p).astype(bf16)


def backward_kernel(near_ref, q, ko, vo, km, vm, kn, vn, g, dq, dko, dvo, dkf, dvf, dfar, far):
    choose_far(near_ref, km, vm, kn, vn, far)
    tile = q.shape[0]
    count = q.shape[1] // HEAD_DIM
    for first in range(0, count, GROUP):
        spots = [
            slice(h * HEAD_DIM, (h + 1) * HEAD_DIM)
            for h in range(first, min(first + GROUP, count))
        ]
        weights, slopes = [], []
        for at in spots:
            values = jnp.concatenate([vo[:, at], far[1, :, at]], 0)
            keys = jnp.concatenate([ko[:, at], far[0, :, at]], 0)
            weights.append(softmax_keys(q[:, at], keys))
            slopes.append(dot_t(values, g[:, at]))
        for at, p, dp in zip(spots, weights, slopes, strict=True):
            pb = p.astype(bf16)
            delta = jnp.sum(pb.astype(f32) * dp, axis=0, keepdims=True)
            ds = (p * (dp - delta)).astype(bf16)
            keys = jnp.concatenate([ko[:, at], far[0, :, at]], 0)
            dk = dot_n(ds, q[:, at]) * SCALE
            dv = dot_n(pb, g[:, at])
            dq[:, at] = (dot_l(ds, keys) * SCALE).astype(bf16)
            dko[:, at] = dk[:tile]
            dvo[:, at] = dv[:tile]
            for which, (one, term) in enumerate(((dkf, dk), (dvf, dv))):
                rounded = term[tile:].astype(bf16)
                one[:, at] = rounded
                dfar[which, :, at] = rounded


def combine_kernel(near_ref, dko, dvo, mate, kn, vn, dk, dv):
    place = lax.axis_index("seq")
    last = lax.axis_size("seq") - 1
    other = place + 2 * (place & 1) - 1
    inside = (other >= 0) & (other <= last)
    from_mate = near_ref[0, place ^ 1] == place
    from_other = inside & (near_ref[0, jnp.clip(other, 0, last)] == place)
    for which, (own, beyond, out) in enumerate(((dko, kn, dk), (dvo, vn, dv))):
        total = own[...] + jnp.where(from_mate, mate[which].astype(f32), 0.0)
        out[...] = (total + jnp.where(from_other, beyond[...].astype(f32), 0.0)).astype(bf16)


def product_kernel(counts, layers, cores, *refs):
    att = list(refs[: sum(counts)])
    cols, *outs, gathered = refs[sum(counts) :]
    owns, for_mate = outs[: len(layers) * (0 in cores)], outs[-1]
    for t, count in enumerate(counts):
        at = slice(t * HEAD_DIM, (t + 1) * HEAD_DIM)
        parts, att = att[:count], att[count:]
        for core in cores:
            part, row = (parts[0], core) if count == 1 else (parts[core], 0)
            for n, i in enumerate(layers):
                block = part[row, i * HEAD_DIM : (i + 1) * HEAD_DIM, :]
                gathered[core, n * HEAD_DIM : (n + 1) * HEAD_DIM, at] = block
    tokens, width = gathered.shape[2], cols.shape[2]
    step = 512 if width % 512 == 0 else width
    for c in range(0, width, step):
        block = cols[:, :, c : c + step].reshape(tokens, step)
        for n in range(len(layers)):
            rows = slice(n * HEAD_DIM, (n + 1) * HEAD_DIM)
            if 0 in cores:
                owns[n][:, c : c + step] = dot_n(gathered[0, rows, :], block)
            if 1 in cores:
                for_mate[n, :, c : c + step] = dot_n(gathered[1, rows, :], block).astype(bf16)


def piece(ref, lead, start, size):
    at = slice(start, start + size)
    return (ref[:, at] if lead is None else ref[lead, :, at]).astype(f32)


def sum_kernel(spots, start, *refs):
    *parts, out = refs
    size = out.shape[1]
    total = None
    for (lead, first), part in zip(spots, parts, strict=True):
        value = piece(part, lead, start - first, size)
        total = value if total is None else total + value
    out[...] = total.astype(bf16)


def gram_kernel(spots, own, *refs):
    *parts, x, gram = refs
    x[...] = own[...]
    for (lead, first), part in zip(spots, parts, strict=True):
        size = part.shape[-1]
        x[:, first : first + size] += piece(part, lead, 0, size)
    high, middle, low = parts_of(x[...])
    pair = jnp.concatenate([high, middle], 0)
    size = gram.shape[0]
    wide = dot_t(pair, pair)
    cross = wide[:size, size:] + dot_t(high, low)
    gram[...] = wide[:size, :size] + (wide[size:, size:] + (cross + cross.T))


def polynomial(gram):
    eye = (
        lax.broadcasted_iota(jnp.int32, gram.shape, 0)
        == lax.broadcasted_iota(jnp.int32, gram.shape, 1)
    ).astype(f32)
    square = jnp.sum(jnp.sum(gram * eye, axis=1, keepdims=True), axis=0, keepdims=True)
    inverse = 1.0 / (jnp.sqrt(square) + 1e-07)
    a = gram * inverse * inverse
    p = None
    for turn in range(NS_STEPS):
        a_parts = parts_of(a)
        q = coeff_a * eye + coeff_b * a + coeff_c * split_dot(a_parts, a_parts)
        q_parts = parts_of(q)
        p = q if p is None else split_dot(q_parts, parts_of(p))
        if turn + 1 < NS_STEPS:
            a = split_dot(parts_of(split_dot(q_parts, a_parts)), q_parts)
    return p, inverse


def update_kernel(plan, factor, x, gram, gram_other, *outs):
    mine = plan.row_part(lax.axis_index("seq"))
    p, inverse = polynomial(gram[...] + gram_other[...])
    p = p * (inverse * factor)
    p_parts = parts_of(p)
    width = outs[0].shape[1]
    wide = width % HEAD_DIM == 0
    for j in range(plan.per_target):
        if width % HEAD_DIM == 0:
            block = x[:, pl.ds(pl.multiple_of((mine ^ j) * width, width), width)]
        else:
            block = jnp.zeros((HEAD_DIM, width), f32)
            for r in range(plan.per_target):
                part = x[:, r * width : (r + 1) * width]
                block = jnp.where((mine ^ j) == r, part, block)
        piece_out = split_dot(p_parts, parts_of(block)) if wide else exact(p, block)
        outs[j][...] = piece_out.astype(outs[j].dtype)


def place_kernel(plan, *refs):
    *parts, out = refs
    parts = parts[::-1]
    mine = plan.row_part(lax.axis_index("seq"))
    for j, part in enumerate(parts):
        at = pl.ds(pl.multiple_of((mine ^ j) * HEAD_DIM, HEAD_DIM), HEAD_DIM)
        out[at, :] = part[...].astype(f32)


def local(query_tiles, key_tiles, value_tiles, attn_grad, proj_grad, neighbour):
    tile, width = query_tiles.shape[2:]
    depth = proj_grad.shape[3]
    head_count = width // HEAD_DIM
    plan = Plan(head_count)
    n, m, per = plan.seq, plan.dp, plan.per_target
    place = lax.axis_index("seq")
    struct = jax.ShapeDtypeStruct
    query, key, value, grad = (
        a.reshape(tile, width) for a in (query_tiles, key_tiles, value_tiles, attn_grad)
    )

    steps = [(i, i + 1) for i in range(1, n - 1, 2)]
    back = [(j, i) for i, j in steps]
    takes = [(i, j) for i, j in steps if j != n - 2] + [(j, i) for j, i in back if i != 1]
    gives = [(i, j) for i, j in steps if i != 1] + [(j, i) for j, i in back if j != n - 2]
    key_next = lax.ppermute(key, "seq", takes)
    value_next = lax.ppermute(value, "seq", takes)
    slot = depth // n
    flat = proj_grad.reshape(tile, depth)
    mine = plan.col_part(place)
    mine_width = per * slot

    def column_part(part):
        return jnp.concatenate(
            [
                lax.dynamic_slice_in_dim(flat, (high * plan.col + part) * 2 * slot, 2 * slot, 1)
                for high in range(plan.high)
            ],
            1,
        )

    own_columns = column_part(mine)
    key_mate = shift(after(key, own_columns), "seq", 1)
    value_mate = shift(after(value, own_columns), "seq", 1)
    beside = (key_mate, value_mate, key_next, value_next)
    columns = [own_columns] + [
        shift(after(column_part(mine ^ q), key_next, value_next), "seq", q << 1)
        for q in range(1, plan.col)
    ]
    high_columns = [
        shift(own_columns, "seq", high << (1 + plan.col_bits))
        for high in range(1, plan.high)
    ]

    attended = pl.pallas_call(
        functools.partial(forward_kernel, plan),
        out_shape=struct((plan.high, 2, m * HEAD_DIM, tile), bf16),
        in_specs=[smem()] + whole(7),
        out_specs=pl.BlockSpec(memory_space=pltpu.VMEM),
        scratch_shapes=[pltpu.VMEM((2, tile, width), bf16)],
        compiler_params=params(),
        cost_estimate=cost(8 * tile * tile * width, 16 * tile * width, 2 * tile * tile * head_count),
        name="attention_forward",
    )(neighbour, query, key, value, *beside)

    by_high = [attended[0]] + [
        shift(attended[high], "seq", high << (1 + plan.col_bits)) for high in range(1, plan.high)
    ]
    pairs = [(attended[0],)] + [
        (shift(attended[0], "seq", q << 1),) for q in range(1, plan.col)
    ]
    for came_high in by_high[1:]:
        pairs.append((came_high,))
        pairs += [
            tuple(shift(came_high[core : core + 1], "seq", q << 1) for core in range(2))
            for q in range(1, plan.col)
        ]
    counts = [len(pair) for pair in pairs]
    pairs = [part for pair in pairs for part in pair]

    dq, dko, dvo, dkf, dvf, dfar = pl.pallas_call(
        backward_kernel,
        out_shape=[
            struct((tile, width), bf16),
            struct((tile, width), f32),
            struct((tile, width), f32),
            struct((tile, width), bf16),
            struct((tile, width), bf16),
            struct((2, tile, width), bf16),
        ],
        in_specs=[smem()] + whole(8),
        out_specs=whole(6),
        scratch_shapes=[pltpu.VMEM((2, tile, width), bf16)],
        compiler_params=params(),
        cost_estimate=cost(1, 1),
        name="attention_backward",
    )(neighbour, query, key, value, *beside, after(grad, attended))

    through = lax.optimization_barrier((dq, *high_columns, jnp.stack(columns[1:])))[-1]
    held = [jnp.stack(columns)]
    late = []
    for high in range(1, plan.high):
        halves = [shift(part, "seq", high << (1 + plan.col_bits)) for part in jnp.split(through, 2, 2)]
        late.append(halves[0])
        rest = jnp.concatenate(halves, 2)
        held.append(jnp.concatenate([high_columns[high - 1][None], rest], 0))
    held = jnp.concatenate(held, 0)

    def product(name, layers, cores, *operands):
        shapes = [struct((HEAD_DIM, mine_width), f32)] * (len(layers) * (0 in cores))
        shapes += [struct((len(layers), HEAD_DIM, mine_width), bf16)] * (1 in cores)
        return pl.pallas_call(
            functools.partial(product_kernel, counts, layers, cores),
            out_shape=shapes,
            in_specs=whole(len(pairs) + 1),
            out_specs=whole(len(shapes)),
            scratch_shapes=[pltpu.VMEM((2, len(layers) * HEAD_DIM, plan.pairs * tile), bf16)],
            compiler_params=params(),
            cost_estimate=cost(
                len(cores) * len(layers) * HEAD_DIM * n * tile * mine_width,
                n * tile * mine_width,
            ),
            name=name,
        )(*operands)

    def swapped(layers, blocks, for_mate):
        mate = shift(for_mate, "seq", 1)
        return {
            i: [(block, None, 0), (mate, k, 0)]
            for k, (i, block) in enumerate(zip(layers, blocks, strict=True))
        }

    def product_pair(name, layers, *operands):
        *blocks, for_mate = product(name, layers, (0, 1), *operands)
        return swapped(layers, blocks, for_mate)

    def added(parts, start, size):
        return pl.pallas_call(
            functools.partial(sum_kernel, [spot for _, *spot in parts], start),
            out_shape=struct((HEAD_DIM, size), bf16),
            in_specs=whole(len(parts)),
            out_specs=pl.BlockSpec(memory_space=pltpu.VMEM),
            compiler_params=params(),
            cost_estimate=cost(len(parts) * HEAD_DIM * size, 4 * len(parts) * HEAD_DIM * size),
            name="block_sum",
        )(*[array for array, *_ in parts])

    first = [i for i in range(m - 1, 1, -1) if i & 1]
    middle = [i for i in range(m - 1, 1, -1) if not i & 1]
    (for_mate,) = product("product_mate", first, (1,), after(pairs[0], dq), *pairs[1:], held)
    own_first = product("product_first", first, (0,), after(pairs[0], for_mate), *pairs[1:], held)
    blocks = swapped(first, own_first, for_mate)
    going = {i: added(blocks[i], 0, mine_width) for i in first}
    blocks |= product_pair("product_middle", middle, after(pairs[0], *going.values()), *pairs[1:], held)

    blocks |= product_pair("product_near", [1], after(pairs[0], dq), *pairs[1:], held)
    blocks |= product_pair("product_own", [0], after(pairs[0], dq), *pairs[1:], held)

    extra = {i: [] for i in range(m)}
    sent = []
    bit = 1
    while bit < m:
        for i in range(m - 1, 1, -1):
            if i & -i == bit:
                if bit == 1:
                    sent.append(going[i])
                else:
                    (block, *where), *others = blocks[i] + extra[i]
                    sent.append(added([(after(block, dq), *where)] + others, 0, mine_width))
                extra[i ^ bit].append((shift(sent[-1], "dp", bit), None, 0))
        bit *= 2
    far = [
        shift(after(dfar, dq, *late), "seq", 1),
        lax.ppermute(after(dkf, dq), "seq", gives),
        lax.ppermute(after(dvf, dq), "seq", gives),
    ]
    own = blocks[0][0][0]
    came = [blocks[0][1]] + extra[0]
    parts = 1
    size = mine_width // parts
    for start in range(0, mine_width, size):
        near = after(added(blocks[1], start, size), sent[-1], blocks[0][1][0], far[0])
        came.append((shift(near, "dp", 1), None, start))
    dk, dv = pl.pallas_call(
        combine_kernel,
        out_shape=[struct((tile, width), bf16)] * 2,
        in_specs=[smem()] + whole(5),
        out_specs=whole(2),
        compiler_params=params(),
        cost_estimate=cost(6 * tile * width, 20 * tile * width),
        name="key_value_sum",
    )(
        neighbour,
        dko,
        dvo,
        *far,
    )

    x, gram = pl.pallas_call(
        functools.partial(gram_kernel, [spot for _, *spot in came]),
        out_shape=[struct((HEAD_DIM, mine_width), f32), struct((HEAD_DIM, HEAD_DIM), f32)],
        in_specs=whole(1 + len(came)),
        out_specs=whole(2),
        compiler_params=params(),
        cost_estimate=cost(12 * HEAD_DIM * HEAD_DIM * mine_width, 14 * HEAD_DIM * mine_width),
        name="gradient_sum",
    )(own, *[array for array, *_ in came])

    gram_other = jnp.zeros_like(gram)
    for b in range(plan.col_bits):
        gram = gram + gram_other
        gram_other = shift(gram, "seq", 2 << b)

    factor = 0.2 * depth**0.5
    pieces = pl.pallas_call(
        functools.partial(update_kernel, plan, factor),
        out_shape=[struct((HEAD_DIM, slot), f32)] + [struct((HEAD_DIM, slot), bf16)] * (per - 1),
        in_specs=whole(3),
        out_specs=whole(per),
        compiler_params=params(),
        cost_estimate=cost(12 * HEAD_DIM * HEAD_DIM * mine_width, 8 * HEAD_DIM * mine_width),
        name="newton_schulz",
    )(after(x, dk), gram, gram_other)
    pieces = [pieces[0]] + [
        shift(pieces[j], "seq", plan.row_mask(j)) for j in range(1, per)
    ]
    update = pl.pallas_call(
        functools.partial(place_kernel, plan),
        out_shape=struct((per * HEAD_DIM, slot), f32),
        in_specs=whole(per),
        out_specs=pl.BlockSpec(memory_space=pltpu.VMEM),
        compiler_params=params(),
        cost_estimate=cost(1, 8 * per * HEAD_DIM * slot),
        name="update_rows",
    )(*reversed(pieces))

    shape = query_tiles.shape
    return dq.reshape(shape), dk.reshape(shape), dv.reshape(shape), update


def solution(mesh):
    tiles = P("dp", "seq", None, None)
    return jax.shard_map(
        local,
        mesh=mesh,
        in_specs=(tiles, tiles, tiles, tiles, tiles, P("dp", None)),
        out_specs=(tiles, tiles, tiles, P("dp", "seq")),
        check_vma=False,
    )
```

```python
import functools
import math

import jax
import jax.numpy as jnp
from jax import lax
from jax.experimental import pallas as pl
from jax.experimental.pallas import tpu as pltpu
from jax.sharding import PartitionSpec as P

HEAD_DIM = 128
NS_STEPS = 5
SCALE = HEAD_DIM ** (-0.5)
LOG2E = math.log2(math.e)
GROUP = 4
coeff_a = 3.4445
coeff_b = -4.775
coeff_c = 2.0315
f32 = jnp.float32
bf16 = jnp.bfloat16
VMEM_LIMIT = 24 * 1024 * 1024


def whole(count):
    return [pl.BlockSpec(memory_space=pltpu.VMEM)] * count


def smem():
    return pl.BlockSpec(memory_space=pltpu.SMEM)


def params():
    return pltpu.CompilerParams(vmem_limit_bytes=VMEM_LIMIT)


def cost(flops, moved, exps=0):
    return pl.CostEstimate(flops=int(flops), bytes_accessed=int(moved), transcendentals=int(exps))


def dot_t(a, b):
    return lax.dot_general(a, b, (((1,), (1,)), ((), ())), preferred_element_type=f32)


def dot_n(a, b):
    return lax.dot_general(a, b, (((1,), (0,)), ((), ())), preferred_element_type=f32)


def dot_l(a, b):
    return lax.dot_general(a, b, (((0,), (0,)), ((), ())), preferred_element_type=f32)


def exact(a, b, dims=((1,), (0,))):
    return lax.dot_general(
        a, b, (dims, ((), ())), precision=lax.Precision.HIGHEST, preferred_element_type=f32
    )


def parts_of(value):
    high = value.astype(bf16)
    rest = value - high.astype(f32)
    middle = rest.astype(bf16)
    return high, middle, (rest - middle.astype(f32)).astype(bf16)


def split_dot(a, b):
    a_high, a_middle, a_low = a
    b_high, b_middle, b_low = b
    size = b_high.shape[1]
    left = jnp.concatenate([a_high, a_middle], 1)
    right = jnp.concatenate(
        [jnp.concatenate([b_high, b_high], 0), jnp.concatenate([b_middle, b_middle], 0)], 1
    )
    wide = dot_n(left, right)
    small = dot_n(jnp.concatenate([a_high, a_low], 1), jnp.concatenate([b_low, b_high], 0))
    return wide[:, :size] + (wide[:, size:] + small)


class Plan:
    def __init__(self, head_count):
        self.seq = lax.axis_size("seq")
        self.dp = lax.axis_size("dp")
        self.per_target = head_count // self.dp
        self.high = self.per_target // 2
        self.col = self.seq // self.per_target
        self.col_bits = self.col.bit_length() - 1
        self.pairs = self.seq // 2

    def row_part(self, place):
        return (place >> (1 + self.col_bits)) * 2 + (place & 1)

    def row_mask(self, part):
        return ((part >> 1) << (1 + self.col_bits)) | (part & 1)

    def col_part(self, place):
        return (place >> 1) & (self.col - 1)


def after(value, *others):
    return lax.optimization_barrier((value, *others))[0]


def shift(value, axis, mask):
    return lax.ppermute(value, axis, [(i, i ^ mask) for i in range(lax.axis_size(axis))])


def head_slice(index):
    return pl.ds(pl.multiple_of(index * HEAD_DIM, HEAD_DIM), HEAD_DIM)


def softmax_keys(query, keys):
    scores = dot_t(keys, query)
    top = jnp.max(scores, axis=0, keepdims=True)
    powers = jnp.exp2((scores - top) * (SCALE * LOG2E))
    return powers * (1.0 / jnp.sum(powers, axis=0, keepdims=True))


def choose_far(near_ref, key_mate, value_mate, key_next, value_next, far):
    place = lax.axis_index("seq")
    is_mate = near_ref[0, place] == (place ^ 1)

    @pl.when(is_mate)
    def _():
        far[0] = key_mate[...]
        far[1] = value_mate[...]

    @pl.when(jnp.logical_not(is_mate))
    def _():
        far[0] = key_next[...]
        far[1] = value_next[...]


def forward_kernel(plan, near_ref, q, ko, vo, km, vm, kn, vn, out, far):
    layer = lax.axis_index("dp")
    choose_far(near_ref, km, vm, kn, vn, far)
    mine = plan.row_part(lax.axis_index("seq"))
    jobs = [(j, i) for j in range(plan.per_target) for i in range(plan.dp)]
    for first in range(0, len(jobs), GROUP):
        group = jobs[first : first + GROUP]
        spots = [head_slice((layer ^ i) * plan.per_target + (mine ^ j)) for j, i in group]
        weights = [
            softmax_keys(q[:, at], jnp.concatenate([ko[:, at], far[0, :, at]], 0)).astype(bf16)
            for at in spots
        ]
        for (j, i), at, p in zip(group, spots, weights, strict=True):
            values = jnp.concatenate([vo[:, at], far[1, :, at]], 0)
            rows = slice(i * HEAD_DIM, (i + 1) * HEAD_DIM)
            out[j >> 1, j & 1, rows, :] = dot_l(values, p).astype(bf16)


def backward_kernel(near_ref, q, ko, vo, km, vm, kn, vn, g, dq, dko, dvo, dkf, dvf, dfar, far):
    choose_far(near_ref, km, vm, kn, vn, far)
    tile = q.shape[0]
    count = q.shape[1] // HEAD_DIM
    for first in range(0, count, GROUP):
        spots = [
            slice(h * HEAD_DIM, (h + 1) * HEAD_DIM)
            for h in range(first, min(first + GROUP, count))
        ]
        weights, slopes = [], []
        for at in spots:
            values = jnp.concatenate([vo[:, at], far[1, :, at]], 0)
            keys = jnp.concatenate([ko[:, at], far[0, :, at]], 0)
            weights.append(softmax_keys(q[:, at], keys))
            slopes.append(dot_t(values, g[:, at]))
        for at, p, dp in zip(spots, weights, slopes, strict=True):
            pb = p.astype(bf16)
            delta = jnp.sum(pb.astype(f32) * dp, axis=0, keepdims=True)
            ds = (p * (dp - delta)).astype(bf16)
            keys = jnp.concatenate([ko[:, at], far[0, :, at]], 0)
            dk = dot_n(ds, q[:, at]) * SCALE
            dv = dot_n(pb, g[:, at])
            dq[:, at] = (dot_l(ds, keys) * SCALE).astype(bf16)
            dko[:, at] = dk[:tile]
            dvo[:, at] = dv[:tile]
            for which, (one, term) in enumerate(((dkf, dk), (dvf, dv))):
                rounded = term[tile:].astype(bf16)
                one[:, at] = rounded
                dfar[which, :, at] = rounded


def combine_kernel(near_ref, dko, dvo, mate, kn, vn, dk, dv):
    place = lax.axis_index("seq")
    last = lax.axis_size("seq") - 1
    other = place + 2 * (place & 1) - 1
    inside = (other >= 0) & (other <= last)
    from_mate = near_ref[0, place ^ 1] == place
    from_other = inside & (near_ref[0, jnp.clip(other, 0, last)] == place)
    for which, (own, beyond, out) in enumerate(((dko, kn, dk), (dvo, vn, dv))):
        total = own[...] + jnp.where(from_mate, mate[which].astype(f32), 0.0)
        out[...] = (total + jnp.where(from_other, beyond[...].astype(f32), 0.0)).astype(bf16)


def product_kernel(counts, layers, cores, *refs):
    att = list(refs[: sum(counts)])
    cols, *outs, gathered = refs[sum(counts) :]
    owns, for_mate = outs[: len(layers) * (0 in cores)], outs[-1]
    for t, count in enumerate(counts):
        at = slice(t * HEAD_DIM, (t + 1) * HEAD_DIM)
        parts, att = att[:count], att[count:]
        for core in cores:
            part, row = (parts[0], core) if count == 1 else (parts[core], 0)
            for n, i in enumerate(layers):
                block = part[row, i * HEAD_DIM : (i + 1) * HEAD_DIM, :]
                gathered[core, n * HEAD_DIM : (n + 1) * HEAD_DIM, at] = block
    tokens, width = gathered.shape[2], cols.shape[2]
    step = 512 if width % 512 == 0 else width
    for c in range(0, width, step):
        block = cols[:, :, c : c + step].reshape(tokens, step)
        for n in range(len(layers)):
            rows = slice(n * HEAD_DIM, (n + 1) * HEAD_DIM)
            if 0 in cores:
                owns[n][:, c : c + step] = dot_n(gathered[0, rows, :], block)
            if 1 in cores:
                for_mate[n, :, c : c + step] = dot_n(gathered[1, rows, :], block).astype(bf16)


def piece(ref, lead, start, size):
    at = slice(start, start + size)
    return (ref[:, at] if lead is None else ref[lead, :, at]).astype(f32)


def sum_kernel(spots, start, *refs):
    *parts, out = refs
    size = out.shape[1]
    total = None
    for (lead, first), part in zip(spots, parts, strict=True):
        value = piece(part, lead, start - first, size)
        total = value if total is None else total + value
    out[...] = total.astype(bf16)


def gram_kernel(spots, own, *refs):
    *parts, x, gram = refs
    x[...] = own[...]
    for (lead, first), part in zip(spots, parts, strict=True):
        size = part.shape[-1]
        x[:, first : first + size] += piece(part, lead, 0, size)
    high, middle, low = parts_of(x[...])
    pair = jnp.concatenate([high, middle], 0)
    size = gram.shape[0]
    wide = dot_t(pair, pair)
    cross = wide[:size, size:] + dot_t(high, low)
    gram[...] = wide[:size, :size] + (wide[size:, size:] + (cross + cross.T))


def polynomial(gram):
    eye = (
        lax.broadcasted_iota(jnp.int32, gram.shape, 0)
        == lax.broadcasted_iota(jnp.int32, gram.shape, 1)
    ).astype(f32)
    square = jnp.sum(jnp.sum(gram * eye, axis=1, keepdims=True), axis=0, keepdims=True)
    inverse = 1.0 / (jnp.sqrt(square) + 1e-07)
    a = gram * inverse * inverse
    p = None
    for turn in range(NS_STEPS):
        a_parts = parts_of(a)
        q = coeff_a * eye + coeff_b * a + coeff_c * split_dot(a_parts, a_parts)
        q_parts = parts_of(q)
        p = q if p is None else split_dot(q_parts, parts_of(p))
        if turn + 1 < NS_STEPS:
            a = split_dot(parts_of(split_dot(q_parts, a_parts)), q_parts)
    return p, inverse


def update_kernel(plan, factor, x, gram, gram_other, *outs):
    mine = plan.row_part(lax.axis_index("seq"))
    p, inverse = polynomial(gram[...] + gram_other[...])
    p = p * (inverse * factor)
    p_parts = parts_of(p)
    width = outs[0].shape[1]
    wide = width % HEAD_DIM == 0
    for j in range(plan.per_target):
        if width % HEAD_DIM == 0:
            block = x[:, pl.ds(pl.multiple_of((mine ^ j) * width, width), width)]
        else:
            block = jnp.zeros((HEAD_DIM, width), f32)
            for r in range(plan.per_target):
                part = x[:, r * width : (r + 1) * width]
                block = jnp.where((mine ^ j) == r, part, block)
        piece_out = split_dot(p_parts, parts_of(block)) if wide else exact(p, block)
        outs[j][...] = piece_out.astype(outs[j].dtype)


def place_kernel(plan, *refs):
    *parts, out, turned, sems = refs
    parts = parts[::-1]
    mine = plan.row_part(lax.axis_index("seq"))
    copies = []
    for j, part in enumerate(parts):
        source = part
        if j:
            turned[j - 1] = part[...].astype(f32)
            source = turned.at[j - 1]
        at = pl.ds(pl.multiple_of((mine ^ j) * HEAD_DIM, HEAD_DIM), HEAD_DIM)
        copies.append(pltpu.make_async_copy(source, out.at[at, :], sems.at[j]))
        copies[-1].start()
    for copy in copies:
        copy.wait()


def local(query_tiles, key_tiles, value_tiles, attn_grad, proj_grad, neighbour):
    tile, width = query_tiles.shape[2:]
    depth = proj_grad.shape[3]
    head_count = width // HEAD_DIM
    plan = Plan(head_count)
    n, m, per = plan.seq, plan.dp, plan.per_target
    place = lax.axis_index("seq")
    struct = jax.ShapeDtypeStruct
    query, key, value, grad = (
        a.reshape(tile, width) for a in (query_tiles, key_tiles, value_tiles, attn_grad)
    )

    steps = [(i, i + 1) for i in range(1, n - 1, 2)]
    back = [(j, i) for i, j in steps]
    takes = [(i, j) for i, j in steps if j != n - 2] + [(j, i) for j, i in back if i != 1]
    gives = [(i, j) for i, j in steps if i != 1] + [(j, i) for j, i in back if j != n - 2]
    key_next = lax.ppermute(key, "seq", takes)
    value_next = lax.ppermute(value, "seq", takes)
    slot = depth // n
    flat = proj_grad.reshape(tile, depth)
    mine = plan.col_part(place)
    mine_width = per * slot

    def column_part(part):
        return jnp.concatenate(
            [
                lax.dynamic_slice_in_dim(flat, (high * plan.col + part) * 2 * slot, 2 * slot, 1)
                for high in range(plan.high)
            ],
            1,
        )

    own_columns = column_part(mine)
    key_mate = shift(after(key, own_columns), "seq", 1)
    value_mate = shift(after(value, own_columns), "seq", 1)
    beside = (key_mate, value_mate, key_next, value_next)
    columns = [own_columns] + [
        shift(after(column_part(mine ^ q), key_next, value_next), "seq", q << 1)
        for q in range(1, plan.col)
    ]
    high_columns = [
        shift(own_columns, "seq", high << (1 + plan.col_bits))
        for high in range(1, plan.high)
    ]

    attended = pl.pallas_call(
        functools.partial(forward_kernel, plan),
        out_shape=struct((plan.high, 2, m * HEAD_DIM, tile), bf16),
        in_specs=[smem()] + whole(7),
        out_specs=pl.BlockSpec(memory_space=pltpu.VMEM),
        scratch_shapes=[pltpu.VMEM((2, tile, width), bf16)],
        compiler_params=params(),
        cost_estimate=cost(8 * tile * tile * width, 16 * tile * width, 2 * tile * tile * head_count),
        name="attention_forward",
    )(neighbour, query, key, value, *beside)

    by_high = [attended[0]] + [
        shift(attended[high], "seq", high << (1 + plan.col_bits)) for high in range(1, plan.high)
    ]
    pairs = [(attended[0],)] + [
        (shift(attended[0], "seq", q << 1),) for q in range(1, plan.col)
    ]
    for came_high in by_high[1:]:
        pairs.append((came_high,))
        pairs += [
            tuple(shift(came_high[core : core + 1], "seq", q << 1) for core in range(2))
            for q in range(1, plan.col)
        ]
    counts = [len(pair) for pair in pairs]
    pairs = [part for pair in pairs for part in pair]

    dq, dko, dvo, dkf, dvf, dfar = pl.pallas_call(
        backward_kernel,
        out_shape=[
            struct((tile, width), bf16),
            struct((tile, width), f32),
            struct((tile, width), f32),
            struct((tile, width), bf16),
            struct((tile, width), bf16),
            struct((2, tile, width), bf16),
        ],
        in_specs=[smem()] + whole(8),
        out_specs=whole(6),
        scratch_shapes=[pltpu.VMEM((2, tile, width), bf16)],
        compiler_params=params(),
        cost_estimate=cost(1, 1),
        name="attention_backward",
    )(neighbour, query, key, value, *beside, after(grad, attended))

    through = lax.optimization_barrier((dq, *high_columns, jnp.stack(columns[1:])))[-1]
    held = [jnp.stack(columns)]
    late = []
    for high in range(1, plan.high):
        halves = [shift(part, "seq", high << (1 + plan.col_bits)) for part in jnp.split(through, 2, 2)]
        late.append(halves[0])
        rest = jnp.concatenate(halves, 2)
        held.append(jnp.concatenate([high_columns[high - 1][None], rest], 0))
    held = jnp.concatenate(held, 0)

    def product(name, layers, cores, *operands):
        shapes = [struct((HEAD_DIM, mine_width), f32)] * (len(layers) * (0 in cores))
        shapes += [struct((len(layers), HEAD_DIM, mine_width), bf16)] * (1 in cores)
        return pl.pallas_call(
            functools.partial(product_kernel, counts, layers, cores),
            out_shape=shapes,
            in_specs=whole(len(pairs) + 1),
            out_specs=whole(len(shapes)),
            scratch_shapes=[pltpu.VMEM((2, len(layers) * HEAD_DIM, plan.pairs * tile), bf16)],
            compiler_params=params(),
            cost_estimate=cost(
                len(cores) * len(layers) * HEAD_DIM * n * tile * mine_width,
                n * tile * mine_width,
            ),
            name=name,
        )(*operands)

    def swapped(layers, blocks, for_mate):
        mate = shift(for_mate, "seq", 1)
        return {
            i: [(block, None, 0), (mate, k, 0)]
            for k, (i, block) in enumerate(zip(layers, blocks, strict=True))
        }

    def product_pair(name, layers, *operands):
        *blocks, for_mate = product(name, layers, (0, 1), *operands)
        return swapped(layers, blocks, for_mate)

    def added(parts, start, size):
        return pl.pallas_call(
            functools.partial(sum_kernel, [spot for _, *spot in parts], start),
            out_shape=struct((HEAD_DIM, size), bf16),
            in_specs=whole(len(parts)),
            out_specs=pl.BlockSpec(memory_space=pltpu.VMEM),
            compiler_params=params(),
            cost_estimate=cost(len(parts) * HEAD_DIM * size, 4 * len(parts) * HEAD_DIM * size),
            name="block_sum",
        )(*[array for array, *_ in parts])

    first = [i for i in range(m - 1, 1, -1) if i & 1]
    middle = [i for i in range(m - 1, 1, -1) if not i & 1]
    (for_mate,) = product("product_mate", first, (1,), after(pairs[0], dq), *pairs[1:], held)
    own_first = product("product_first", first, (0,), after(pairs[0], for_mate), *pairs[1:], held)
    blocks = swapped(first, own_first, for_mate)
    going = {i: added(blocks[i], 0, mine_width) for i in first}
    blocks |= product_pair("product_middle", middle, after(pairs[0], *going.values()), *pairs[1:], held)

    blocks |= product_pair("product_near", [1], after(pairs[0], dq), *pairs[1:], held)
    blocks |= product_pair("product_own", [0], after(pairs[0], dq), *pairs[1:], held)

    extra = {i: [] for i in range(m)}
    sent = []
    bit = 1
    while bit < m:
        for i in range(m - 1, 1, -1):
            if i & -i == bit:
                if bit == 1:
                    sent.append(going[i])
                else:
                    (block, *where), *others = blocks[i] + extra[i]
                    sent.append(added([(after(block, dq), *where)] + others, 0, mine_width))
                extra[i ^ bit].append((shift(sent[-1], "dp", bit), None, 0))
        bit *= 2
    far = [
        shift(after(dfar, dq, *late), "seq", 1),
        lax.ppermute(after(dkf, dq), "seq", gives),
        lax.ppermute(after(dvf, dq), "seq", gives),
    ]
    own = blocks[0][0][0]
    came = [blocks[0][1]] + extra[0]
    parts = 1
    size = mine_width // parts
    for start in range(0, mine_width, size):
        near = after(added(blocks[1], start, size), sent[-1], blocks[0][1][0], far[0])
        came.append((shift(near, "dp", 1), None, start))
    dk, dv = pl.pallas_call(
        combine_kernel,
        out_shape=[struct((tile, width), bf16)] * 2,
        in_specs=[smem()] + whole(5),
        out_specs=whole(2),
        compiler_params=params(),
        cost_estimate=cost(6 * tile * width, 20 * tile * width),
        name="key_value_sum",
    )(
        neighbour,
        dko,
        dvo,
        *far,
    )

    x, gram = pl.pallas_call(
        functools.partial(gram_kernel, [spot for _, *spot in came]),
        out_shape=[struct((HEAD_DIM, mine_width), f32), struct((HEAD_DIM, HEAD_DIM), f32)],
        in_specs=whole(1 + len(came)),
        out_specs=whole(2),
        compiler_params=params(),
        cost_estimate=cost(12 * HEAD_DIM * HEAD_DIM * mine_width, 14 * HEAD_DIM * mine_width),
        name="gradient_sum",
    )(own, *[array for array, *_ in came])

    gram_other = jnp.zeros_like(gram)
    for b in range(plan.col_bits):
        gram = gram + gram_other
        gram_other = shift(gram, "seq", 2 << b)

    factor = 0.2 * depth**0.5
    pieces = pl.pallas_call(
        functools.partial(update_kernel, plan, factor),
        out_shape=[struct((HEAD_DIM, slot), f32)] + [struct((HEAD_DIM, slot), bf16)] * (per - 1),
        in_specs=whole(3),
        out_specs=whole(per),
        compiler_params=params(),
        cost_estimate=cost(12 * HEAD_DIM * HEAD_DIM * mine_width, 8 * HEAD_DIM * mine_width),
        name="newton_schulz",
    )(after(x, dk), gram, gram_other)
    pieces = [pieces[0]] + [
        shift(pieces[j], "seq", plan.row_mask(j)) for j in range(1, per)
    ]
    update = pl.pallas_call(
        functools.partial(place_kernel, plan),
        out_shape=struct((per * HEAD_DIM, slot), f32),
        in_specs=whole(per),
        out_specs=pl.BlockSpec(memory_space=pl.ANY),
        scratch_shapes=[
            pltpu.VMEM((per - 1, HEAD_DIM, slot), f32),
            pltpu.SemaphoreType.DMA((per,)),
        ],
        compiler_params=params(),
        cost_estimate=cost(1, 8 * per * HEAD_DIM * slot),
        name="update_rows",
    )(*reversed(pieces))

    shape = query_tiles.shape
    return dq.reshape(shape), dk.reshape(shape), dv.reshape(shape), update


def solution(mesh):
    tiles = P("dp", "seq", None, None)
    return jax.shard_map(
        local,
        mesh=mesh,
        in_specs=(tiles, tiles, tiles, tiles, tiles, P("dp", None)),
        out_specs=(tiles, tiles, tiles, P("dp", "seq")),
        check_vma=False,
    )
```

```python
import functools
import math

import jax
import jax.numpy as jnp
from jax import lax
from jax.experimental import pallas as pl
from jax.experimental.pallas import tpu as pltpu
from jax.sharding import PartitionSpec as P

HEAD_DIM = 128
NS_STEPS = 5
SCALE = HEAD_DIM ** (-0.5)
LOG2E = math.log2(math.e)
GROUP = 4
coeff_a = 3.4445
coeff_b = -4.775
coeff_c = 2.0315
f32 = jnp.float32
bf16 = jnp.bfloat16
VMEM_LIMIT = 24 * 1024 * 1024


def whole(count):
    return [pl.BlockSpec(memory_space=pltpu.VMEM)] * count


def smem():
    return pl.BlockSpec(memory_space=pltpu.SMEM)


def params():
    return pltpu.CompilerParams(vmem_limit_bytes=VMEM_LIMIT)


def cost(flops, moved, exps=0):
    return pl.CostEstimate(flops=int(flops), bytes_accessed=int(moved), transcendentals=int(exps))


def dot_t(a, b):
    return lax.dot_general(a, b, (((1,), (1,)), ((), ())), preferred_element_type=f32)


def dot_n(a, b):
    return lax.dot_general(a, b, (((1,), (0,)), ((), ())), preferred_element_type=f32)


def dot_l(a, b):
    return lax.dot_general(a, b, (((0,), (0,)), ((), ())), preferred_element_type=f32)


def exact(a, b, dims=((1,), (0,))):
    return lax.dot_general(
        a, b, (dims, ((), ())), precision=lax.Precision.HIGHEST, preferred_element_type=f32
    )


def parts_of(value):
    high = value.astype(bf16)
    rest = value - high.astype(f32)
    middle = rest.astype(bf16)
    return high, middle, (rest - middle.astype(f32)).astype(bf16)


def split_dot(a, b):
    a_high, a_middle, a_low = a
    b_high, b_middle, b_low = b
    size = b_high.shape[1]
    left = jnp.concatenate([a_high, a_middle], 1)
    right = jnp.concatenate(
        [jnp.concatenate([b_high, b_high], 0), jnp.concatenate([b_middle, b_middle], 0)], 1
    )
    wide = dot_n(left, right)
    small = dot_n(jnp.concatenate([a_high, a_low], 1), jnp.concatenate([b_low, b_high], 0))
    return wide[:, :size] + (wide[:, size:] + small)


class Plan:
    def __init__(self, head_count):
        self.seq = lax.axis_size("seq")
        self.dp = lax.axis_size("dp")
        self.per_target = head_count // self.dp
        self.high = self.per_target // 2
        self.col = self.seq // self.per_target
        self.col_bits = self.col.bit_length() - 1
        self.pairs = self.seq // 2

    def row_part(self, place):
        return (place >> (1 + self.col_bits)) * 2 + (place & 1)

    def row_mask(self, part):
        return ((part >> 1) << (1 + self.col_bits)) | (part & 1)

    def col_part(self, place):
        return (place >> 1) & (self.col - 1)


def after(value, *others):
    return lax.optimization_barrier((value, *others))[0]


def shift(value, axis, mask):
    return lax.ppermute(value, axis, [(i, i ^ mask) for i in range(lax.axis_size(axis))])


def head_slice(index):
    return pl.ds(pl.multiple_of(index * HEAD_DIM, HEAD_DIM), HEAD_DIM)


def softmax_keys(query, keys):
    scores = dot_t(keys, query)
    top = jnp.max(scores, axis=0, keepdims=True)
    powers = jnp.exp2((scores - top) * (SCALE * LOG2E))
    return powers * (1.0 / jnp.sum(powers, axis=0, keepdims=True))


def choose_far(near_ref, key_mate, value_mate, key_next, value_next, far):
    place = lax.axis_index("seq")
    is_mate = near_ref[0, place] == (place ^ 1)

    @pl.when(is_mate)
    def _():
        far[0] = key_mate[...]
        far[1] = value_mate[...]

    @pl.when(jnp.logical_not(is_mate))
    def _():
        far[0] = key_next[...]
        far[1] = value_next[...]


def forward_kernel(plan, near_ref, q, ko, vo, km, vm, kn, vn, out, far):
    layer = lax.axis_index("dp")
    choose_far(near_ref, km, vm, kn, vn, far)
    mine = plan.row_part(lax.axis_index("seq"))
    jobs = [(j, i) for j in range(plan.per_target) for i in range(plan.dp)]
    for first in range(0, len(jobs), GROUP):
        group = jobs[first : first + GROUP]
        spots = [head_slice((layer ^ i) * plan.per_target + (mine ^ j)) for j, i in group]
        weights = [
            softmax_keys(q[:, at], jnp.concatenate([ko[:, at], far[0, :, at]], 0)).astype(bf16)
            for at in spots
        ]
        for (j, i), at, p in zip(group, spots, weights, strict=True):
            values = jnp.concatenate([vo[:, at], far[1, :, at]], 0)
            rows = slice(i * HEAD_DIM, (i + 1) * HEAD_DIM)
            out[j >> 1, j & 1, rows, :] = dot_l(values, p).astype(bf16)


def backward_kernel(near_ref, q, ko, vo, km, vm, kn, vn, g, dq, dko, dvo, dkf, dvf, dfar, far):
    choose_far(near_ref, km, vm, kn, vn, far)
    tile = q.shape[0]
    count = q.shape[1] // HEAD_DIM
    for first in range(0, count, GROUP):
        spots = [
            slice(h * HEAD_DIM, (h + 1) * HEAD_DIM)
            for h in range(first, min(first + GROUP, count))
        ]
        weights, slopes = [], []
        for at in spots:
            values = jnp.concatenate([vo[:, at], far[1, :, at]], 0)
            keys = jnp.concatenate([ko[:, at], far[0, :, at]], 0)
            weights.append(softmax_keys(q[:, at], keys))
            slopes.append(dot_t(values, g[:, at]))
        for at, p, dp in zip(spots, weights, slopes, strict=True):
            pb = p.astype(bf16)
            delta = jnp.sum(pb.astype(f32) * dp, axis=0, keepdims=True)
            ds = (p * (dp - delta)).astype(bf16)
            keys = jnp.concatenate([ko[:, at], far[0, :, at]], 0)
            dk = dot_n(ds, q[:, at]) * SCALE
            dv = dot_n(pb, g[:, at])
            dq[:, at] = (dot_l(ds, keys) * SCALE).astype(bf16)
            dko[:, at] = dk[:tile]
            dvo[:, at] = dv[:tile]
            for which, (one, term) in enumerate(((dkf, dk), (dvf, dv))):
                rounded = term[tile:].astype(bf16)
                one[:, at] = rounded
                dfar[which, :, at] = rounded


def combine_kernel(near_ref, dko, dvo, mate, kn, vn, dk, dv):
    place = lax.axis_index("seq")
    last = lax.axis_size("seq") - 1
    other = place + 2 * (place & 1) - 1
    inside = (other >= 0) & (other <= last)
    from_mate = near_ref[0, place ^ 1] == place
    from_other = inside & (near_ref[0, jnp.clip(other, 0, last)] == place)
    for which, (own, beyond, out) in enumerate(((dko, kn, dk), (dvo, vn, dv))):
        total = own[...] + jnp.where(from_mate, mate[which].astype(f32), 0.0)
        out[...] = (total + jnp.where(from_other, beyond[...].astype(f32), 0.0)).astype(bf16)


def product_kernel(counts, layers, cores, *refs):
    att = list(refs[: sum(counts)])
    cols, *outs, gathered = refs[sum(counts) :]
    owns, for_mate = outs[: len(layers) * (0 in cores)], outs[-1]
    for t, count in enumerate(counts):
        at = slice(t * HEAD_DIM, (t + 1) * HEAD_DIM)
        parts, att = att[:count], att[count:]
        for core in cores:
            part, row = (parts[0], core) if count == 1 else (parts[core], 0)
            for n, i in enumerate(layers):
                block = part[row, i * HEAD_DIM : (i + 1) * HEAD_DIM, :]
                gathered[core, n * HEAD_DIM : (n + 1) * HEAD_DIM, at] = block
    tokens, width = gathered.shape[2], cols.shape[2]
    step = 512 if width % 512 == 0 else width
    for c in range(0, width, step):
        block = cols[:, :, c : c + step].reshape(tokens, step)
        for n in range(len(layers)):
            rows = slice(n * HEAD_DIM, (n + 1) * HEAD_DIM)
            if 0 in cores:
                owns[n][:, c : c + step] = dot_n(gathered[0, rows, :], block)
            if 1 in cores:
                for_mate[n, :, c : c + step] = dot_n(gathered[1, rows, :], block).astype(bf16)


def piece(ref, lead, start, size):
    at = slice(start, start + size)
    return (ref[:, at] if lead is None else ref[lead, :, at]).astype(f32)


def sum_kernel(spots, start, *refs):
    *parts, out = refs
    size = out.shape[1]
    total = None
    for (lead, first), part in zip(spots, parts, strict=True):
        value = piece(part, lead, start - first, size)
        total = value if total is None else total + value
    out[...] = total.astype(bf16)


def column_block(plan, x, part, width):
    if width % HEAD_DIM == 0:
        return x[:, pl.ds(pl.multiple_of(part * width, width), width)]
    block = jnp.zeros((HEAD_DIM, width), f32)
    for r in range(plan.per_target):
        block = jnp.where(part == r, x[:, r * width : (r + 1) * width], block)
    return block


def gram_kernel(plan, spots, own, *refs):
    parts = refs[: len(spots)]
    *outs, gram, x = refs[len(spots) :]
    x[...] = own[...]
    for (lead, first), part in zip(spots, parts, strict=True):
        size = part.shape[-1]
        x[:, first : first + size] += piece(part, lead, 0, size)
    high, middle, low = parts_of(x[...])
    pair = jnp.concatenate([high, middle], 0)
    size = gram.shape[0]
    wide = dot_t(pair, pair)
    cross = wide[:size, size:] + dot_t(high, low)
    gram[...] = wide[:size, :size] + (wide[size:, size:] + (cross + cross.T))
    mine = plan.row_part(lax.axis_index("seq"))
    for j, out in enumerate(outs):
        out[...] = column_block(plan, x, mine ^ j, out.shape[1]).astype(out.dtype)


def polynomial(gram):
    eye = (
        lax.broadcasted_iota(jnp.int32, gram.shape, 0)
        == lax.broadcasted_iota(jnp.int32, gram.shape, 1)
    ).astype(f32)
    square = jnp.sum(jnp.sum(gram * eye, axis=1, keepdims=True), axis=0, keepdims=True)
    inverse = 1.0 / (jnp.sqrt(square) + 1e-07)
    a = gram * inverse * inverse
    p = None
    for turn in range(NS_STEPS):
        a_parts = parts_of(a)
        q = coeff_a * eye + coeff_b * a + coeff_c * split_dot(a_parts, a_parts)
        q_parts = parts_of(q)
        p = q if p is None else split_dot(q_parts, parts_of(p))
        if turn + 1 < NS_STEPS:
            a = split_dot(parts_of(split_dot(q_parts, a_parts)), q_parts)
    return p, inverse


def polynomial_kernel(factor, gram, gram_other, out):
    p, inverse = polynomial(gram[...] + gram_other[...])
    out[...] = p * (inverse * factor)


def update_kernel(plan, *refs):
    *pairs, out = refs
    mine = plan.row_part(lax.axis_index("seq"))
    wide = out.shape[1] % HEAD_DIM == 0
    for j in range(plan.per_target):
        p, block = pairs[2 * j][...], pairs[2 * j + 1][...].astype(f32)
        at = pl.ds(pl.multiple_of((mine ^ j) * HEAD_DIM, HEAD_DIM), HEAD_DIM)
        out[at, :] = split_dot(parts_of(p), parts_of(block)) if wide else exact(p, block)


def local(query_tiles, key_tiles, value_tiles, attn_grad, proj_grad, neighbour):
    tile, width = query_tiles.shape[2:]
    depth = proj_grad.shape[3]
    head_count = width // HEAD_DIM
    plan = Plan(head_count)
    n, m, per = plan.seq, plan.dp, plan.per_target
    place = lax.axis_index("seq")
    struct = jax.ShapeDtypeStruct
    query, key, value, grad = (
        a.reshape(tile, width) for a in (query_tiles, key_tiles, value_tiles, attn_grad)
    )

    steps = [(i, i + 1) for i in range(1, n - 1, 2)]
    back = [(j, i) for i, j in steps]
    takes = [(i, j) for i, j in steps if j != n - 2] + [(j, i) for j, i in back if i != 1]
    gives = [(i, j) for i, j in steps if i != 1] + [(j, i) for j, i in back if j != n - 2]
    key_next = lax.ppermute(key, "seq", takes)
    value_next = lax.ppermute(value, "seq", takes)
    slot = depth // n
    flat = proj_grad.reshape(tile, depth)
    mine = plan.col_part(place)
    mine_width = per * slot

    def column_part(part):
        return jnp.concatenate(
            [
                lax.dynamic_slice_in_dim(flat, (high * plan.col + part) * 2 * slot, 2 * slot, 1)
                for high in range(plan.high)
            ],
            1,
        )

    own_columns = column_part(mine)
    key_mate = shift(after(key, own_columns), "seq", 1)
    value_mate = shift(after(value, own_columns), "seq", 1)
    beside = (key_mate, value_mate, key_next, value_next)
    columns = [own_columns] + [
        shift(after(column_part(mine ^ q), key_next, value_next), "seq", q << 1)
        for q in range(1, plan.col)
    ]
    high_columns = [
        shift(own_columns, "seq", high << (1 + plan.col_bits))
        for high in range(1, plan.high)
    ]

    attended = pl.pallas_call(
        functools.partial(forward_kernel, plan),
        out_shape=struct((plan.high, 2, m * HEAD_DIM, tile), bf16),
        in_specs=[smem()] + whole(7),
        out_specs=pl.BlockSpec(memory_space=pltpu.VMEM),
        scratch_shapes=[pltpu.VMEM((2, tile, width), bf16)],
        compiler_params=params(),
        cost_estimate=cost(8 * tile * tile * width, 16 * tile * width, 2 * tile * tile * head_count),
        name="attention_forward",
    )(neighbour, query, key, value, *beside)

    by_high = [attended[0]] + [
        shift(attended[high], "seq", high << (1 + plan.col_bits)) for high in range(1, plan.high)
    ]
    pairs = [(attended[0],)] + [
        (shift(attended[0], "seq", q << 1),) for q in range(1, plan.col)
    ]
    for came_high in by_high[1:]:
        pairs.append((came_high,))
        pairs += [
            tuple(shift(came_high[core : core + 1], "seq", q << 1) for core in range(2))
            for q in range(1, plan.col)
        ]
    counts = [len(pair) for pair in pairs]
    pairs = [part for pair in pairs for part in pair]

    dq, dko, dvo, dkf, dvf, dfar = pl.pallas_call(
        backward_kernel,
        out_shape=[
            struct((tile, width), bf16),
            struct((tile, width), f32),
            struct((tile, width), f32),
            struct((tile, width), bf16),
            struct((tile, width), bf16),
            struct((2, tile, width), bf16),
        ],
        in_specs=[smem()] + whole(8),
        out_specs=whole(6),
        scratch_shapes=[pltpu.VMEM((2, tile, width), bf16)],
        compiler_params=params(),
        cost_estimate=cost(1, 1),
        name="attention_backward",
    )(neighbour, query, key, value, *beside, after(grad, attended))

    through = lax.optimization_barrier((dq, *high_columns, jnp.stack(columns[1:])))[-1]
    held = [jnp.stack(columns)]
    late = []
    for high in range(1, plan.high):
        halves = [shift(part, "seq", high << (1 + plan.col_bits)) for part in jnp.split(through, 2, 2)]
        late.append(halves[0])
        rest = jnp.concatenate(halves, 2)
        held.append(jnp.concatenate([high_columns[high - 1][None], rest], 0))
    held = jnp.concatenate(held, 0)

    def product(name, layers, cores, *operands):
        shapes = [struct((HEAD_DIM, mine_width), f32)] * (len(layers) * (0 in cores))
        shapes += [struct((len(layers), HEAD_DIM, mine_width), bf16)] * (1 in cores)
        return pl.pallas_call(
            functools.partial(product_kernel, counts, layers, cores),
            out_shape=shapes,
            in_specs=whole(len(pairs) + 1),
            out_specs=whole(len(shapes)),
            scratch_shapes=[pltpu.VMEM((2, len(layers) * HEAD_DIM, plan.pairs * tile), bf16)],
            compiler_params=params(),
            cost_estimate=cost(
                len(cores) * len(layers) * HEAD_DIM * n * tile * mine_width,
                n * tile * mine_width,
            ),
            name=name,
        )(*operands)

    def swapped(layers, blocks, for_mate):
        mate = shift(for_mate, "seq", 1)
        return {
            i: [(block, None, 0), (mate, k, 0)]
            for k, (i, block) in enumerate(zip(layers, blocks, strict=True))
        }

    def product_pair(name, layers, *operands):
        *blocks, for_mate = product(name, layers, (0, 1), *operands)
        return swapped(layers, blocks, for_mate)

    def added(parts, start, size):
        return pl.pallas_call(
            functools.partial(sum_kernel, [spot for _, *spot in parts], start),
            out_shape=struct((HEAD_DIM, size), bf16),
            in_specs=whole(len(parts)),
            out_specs=pl.BlockSpec(memory_space=pltpu.VMEM),
            compiler_params=params(),
            cost_estimate=cost(len(parts) * HEAD_DIM * size, 4 * len(parts) * HEAD_DIM * size),
            name="block_sum",
        )(*[array for array, *_ in parts])

    first = [i for i in range(m - 1, 1, -1) if i & 1]
    middle = [i for i in range(m - 1, 1, -1) if not i & 1]
    (for_mate,) = product("product_mate", first, (1,), after(pairs[0], dq), *pairs[1:], held)
    own_first = product("product_first", first, (0,), after(pairs[0], for_mate), *pairs[1:], held)
    blocks = swapped(first, own_first, for_mate)
    going = {i: added(blocks[i], 0, mine_width) for i in first}
    blocks |= product_pair("product_middle", middle, after(pairs[0], *going.values()), *pairs[1:], held)

    blocks |= product_pair("product_near", [1], after(pairs[0], dq), *pairs[1:], held)
    blocks |= product_pair("product_own", [0], after(pairs[0], dq), *pairs[1:], held)

    extra = {i: [] for i in range(m)}
    sent = []
    bit = 1
    while bit < m:
        for i in range(m - 1, 1, -1):
            if i & -i == bit:
                if bit == 1:
                    sent.append(going[i])
                else:
                    (block, *where), *others = blocks[i] + extra[i]
                    sent.append(added([(after(block, dq), *where)] + others, 0, mine_width))
                extra[i ^ bit].append((shift(sent[-1], "dp", bit), None, 0))
        bit *= 2
    far = [
        shift(after(dfar, dq, *late), "seq", 1),
        lax.ppermute(after(dkf, dq), "seq", gives),
        lax.ppermute(after(dvf, dq), "seq", gives),
    ]
    own = blocks[0][0][0]
    came = [blocks[0][1]] + extra[0]
    parts = 1
    size = mine_width // parts
    for start in range(0, mine_width, size):
        near = after(added(blocks[1], start, size), sent[-1], blocks[0][1][0], far[0])
        came.append((shift(near, "dp", 1), None, start))
    dk, dv = pl.pallas_call(
        combine_kernel,
        out_shape=[struct((tile, width), bf16)] * 2,
        in_specs=[smem()] + whole(5),
        out_specs=whole(2),
        compiler_params=params(),
        cost_estimate=cost(6 * tile * width, 20 * tile * width),
        name="key_value_sum",
    )(
        neighbour,
        dko,
        dvo,
        *far,
    )

    *blocks_out, gram = pl.pallas_call(
        functools.partial(gram_kernel, plan, [spot for _, *spot in came]),
        out_shape=[struct((HEAD_DIM, slot), f32)]
        + [struct((HEAD_DIM, slot), bf16)] * (per - 1)
        + [struct((HEAD_DIM, HEAD_DIM), f32)],
        in_specs=whole(1 + len(came)),
        out_specs=whole(per + 1),
        scratch_shapes=[pltpu.VMEM((HEAD_DIM, mine_width), f32)],
        compiler_params=params(),
        cost_estimate=cost(12 * HEAD_DIM * HEAD_DIM * mine_width, 14 * HEAD_DIM * mine_width),
        name="gradient_sum",
    )(own, *[array for array, *_ in came])

    gram_other = jnp.zeros_like(gram)
    for b in range(plan.col_bits):
        gram = gram + gram_other
        gram_other = shift(gram, "seq", 2 << b)

    factor = 0.2 * depth**0.5
    matrix = pl.BlockSpec(memory_space=pltpu.VMEM)
    p = pl.pallas_call(
        functools.partial(polynomial_kernel, factor),
        out_shape=struct((HEAD_DIM, HEAD_DIM), f32),
        in_specs=whole(2),
        out_specs=matrix,
        compiler_params=params(),
        cost_estimate=cost(12 * HEAD_DIM * HEAD_DIM * mine_width, 8 * HEAD_DIM * mine_width),
        name="newton_schulz",
    )(gram, gram_other)
    moved = [shift(blocks_out[j], "seq", plan.row_mask(j)) for j in range(1, per)]
    operands = [after(p, dk), blocks_out[0]]
    for j in range(1, per):
        operands += [shift(after(p, *moved), "seq", plan.row_mask(j)), moved[j - 1]]
    update = pl.pallas_call(
        functools.partial(update_kernel, plan),
        out_shape=struct((per * HEAD_DIM, slot), f32),
        in_specs=whole(2 * per),
        out_specs=matrix,
        compiler_params=params(),
        cost_estimate=cost(1, 8 * per * HEAD_DIM * slot),
        name="update_rows",
    )(*operands)

    shape = query_tiles.shape
    return dq.reshape(shape), dk.reshape(shape), dv.reshape(shape), update


def solution(mesh):
    tiles = P("dp", "seq", None, None)
    return jax.shard_map(
        local,
        mesh=mesh,
        in_specs=(tiles, tiles, tiles, tiles, tiles, P("dp", None)),
        out_specs=(tiles, tiles, tiles, P("dp", "seq")),
        check_vma=False,
    )
```

```python
import functools
import math

import jax
import jax.numpy as jnp
from jax import lax
from jax.experimental import pallas as pl
from jax.experimental.pallas import tpu as pltpu
from jax.sharding import PartitionSpec as P

HEAD_DIM = 128
NS_STEPS = 5
SCALE = HEAD_DIM ** (-0.5)
LOG2E = math.log2(math.e)
GROUP = 4
coeff_a = 3.4445
coeff_b = -4.775
coeff_c = 2.0315
f32 = jnp.float32
bf16 = jnp.bfloat16
VMEM_LIMIT = 24 * 1024 * 1024


def whole(count):
    return [pl.BlockSpec(memory_space=pltpu.VMEM)] * count


def smem():
    return pl.BlockSpec(memory_space=pltpu.SMEM)


def params():
    return pltpu.CompilerParams(vmem_limit_bytes=VMEM_LIMIT)


def cost(flops, moved, exps=0):
    return pl.CostEstimate(flops=int(flops), bytes_accessed=int(moved), transcendentals=int(exps))


def dot_t(a, b):
    return lax.dot_general(a, b, (((1,), (1,)), ((), ())), preferred_element_type=f32)


def dot_n(a, b):
    return lax.dot_general(a, b, (((1,), (0,)), ((), ())), preferred_element_type=f32)


def dot_l(a, b):
    return lax.dot_general(a, b, (((0,), (0,)), ((), ())), preferred_element_type=f32)


def exact(a, b, dims=((1,), (0,))):
    return lax.dot_general(
        a, b, (dims, ((), ())), precision=lax.Precision.HIGHEST, preferred_element_type=f32
    )


def parts_of(value):
    high = value.astype(bf16)
    rest = value - high.astype(f32)
    middle = rest.astype(bf16)
    return high, middle, (rest - middle.astype(f32)).astype(bf16)


def split_dot(a, b):
    a_high, a_middle, a_low = a
    b_high, b_middle, b_low = b
    size = b_high.shape[1]
    left = jnp.concatenate([a_high, a_middle], 1)
    right = jnp.concatenate(
        [jnp.concatenate([b_high, b_high], 0), jnp.concatenate([b_middle, b_middle], 0)], 1
    )
    wide = dot_n(left, right)
    small = dot_n(jnp.concatenate([a_high, a_low], 1), jnp.concatenate([b_low, b_high], 0))
    return wide[:, :size] + (wide[:, size:] + small)


class Plan:
    def __init__(self, head_count):
        self.seq = lax.axis_size("seq")
        self.dp = lax.axis_size("dp")
        self.per_target = head_count // self.dp
        self.high = self.per_target // 2
        self.col = self.seq // self.per_target
        self.col_bits = self.col.bit_length() - 1
        self.pairs = self.seq // 2

    def row_part(self, place):
        return (place >> (1 + self.col_bits)) * 2 + (place & 1)

    def row_mask(self, part):
        return ((part >> 1) << (1 + self.col_bits)) | (part & 1)

    def col_part(self, place):
        return (place >> 1) & (self.col - 1)


def after(value, *others):
    return lax.optimization_barrier((value, *others))[0]


def shift(value, axis, mask):
    return lax.ppermute(value, axis, [(i, i ^ mask) for i in range(lax.axis_size(axis))])


def head_slice(index):
    return pl.ds(pl.multiple_of(index * HEAD_DIM, HEAD_DIM), HEAD_DIM)


def softmax_keys(query, keys):
    scores = dot_t(keys, query)
    top = jnp.max(scores, axis=0, keepdims=True)
    powers = jnp.exp2((scores - top) * (SCALE * LOG2E))
    return powers * (1.0 / jnp.sum(powers, axis=0, keepdims=True))


def choose_far(near_ref, key_mate, value_mate, key_next, value_next, far):
    place = lax.axis_index("seq")
    is_mate = near_ref[0, place] == (place ^ 1)

    @pl.when(is_mate)
    def _():
        far[0] = key_mate[...]
        far[1] = value_mate[...]

    @pl.when(jnp.logical_not(is_mate))
    def _():
        far[0] = key_next[...]
        far[1] = value_next[...]


def forward_kernel(plan, near_ref, q, ko, vo, km, vm, kn, vn, out, far):
    layer = lax.axis_index("dp")
    choose_far(near_ref, km, vm, kn, vn, far)
    mine = plan.row_part(lax.axis_index("seq"))
    jobs = [(j, i) for j in range(plan.per_target) for i in range(plan.dp)]
    for first in range(0, len(jobs), GROUP):
        group = jobs[first : first + GROUP]
        spots = [head_slice((layer ^ i) * plan.per_target + (mine ^ j)) for j, i in group]
        weights = [
            softmax_keys(q[:, at], jnp.concatenate([ko[:, at], far[0, :, at]], 0)).astype(bf16)
            for at in spots
        ]
        for (j, i), at, p in zip(group, spots, weights, strict=True):
            values = jnp.concatenate([vo[:, at], far[1, :, at]], 0)
            rows = slice(i * HEAD_DIM, (i + 1) * HEAD_DIM)
            out[j >> 1, j & 1, rows, :] = dot_l(values, p).astype(bf16)


def backward_kernel(near_ref, q, ko, vo, km, vm, kn, vn, g, dq, dko, dvo, dkf, dvf, dfar, far):
    choose_far(near_ref, km, vm, kn, vn, far)
    tile = q.shape[0]
    count = q.shape[1] // HEAD_DIM
    for first in range(0, count, GROUP):
        spots = [
            slice(h * HEAD_DIM, (h + 1) * HEAD_DIM)
            for h in range(first, min(first + GROUP, count))
        ]
        weights, slopes = [], []
        for at in spots:
            values = jnp.concatenate([vo[:, at], far[1, :, at]], 0)
            keys = jnp.concatenate([ko[:, at], far[0, :, at]], 0)
            weights.append(softmax_keys(q[:, at], keys))
            slopes.append(dot_t(values, g[:, at]))
        for at, p, dp in zip(spots, weights, slopes, strict=True):
            pb = p.astype(bf16)
            delta = jnp.sum(pb.astype(f32) * dp, axis=0, keepdims=True)
            ds = (p * (dp - delta)).astype(bf16)
            keys = jnp.concatenate([ko[:, at], far[0, :, at]], 0)
            dk = dot_n(ds, q[:, at]) * SCALE
            dv = dot_n(pb, g[:, at])
            dq[:, at] = (dot_l(ds, keys) * SCALE).astype(bf16)
            dko[:, at] = dk[:tile]
            dvo[:, at] = dv[:tile]
            for which, (one, term) in enumerate(((dkf, dk), (dvf, dv))):
                rounded = term[tile:].astype(bf16)
                one[:, at] = rounded
                dfar[which, :, at] = rounded


def combine_kernel(near_ref, dko, dvo, mate, kn, vn, dk, dv):
    place = lax.axis_index("seq")
    last = lax.axis_size("seq") - 1
    other = place + 2 * (place & 1) - 1
    inside = (other >= 0) & (other <= last)
    from_mate = near_ref[0, place ^ 1] == place
    from_other = inside & (near_ref[0, jnp.clip(other, 0, last)] == place)
    for which, (own, beyond, out) in enumerate(((dko, kn, dk), (dvo, vn, dv))):
        total = own[...] + jnp.where(from_mate, mate[which].astype(f32), 0.0)
        out[...] = (total + jnp.where(from_other, beyond[...].astype(f32), 0.0)).astype(bf16)


def product_kernel(counts, layers, cores, *refs):
    att = list(refs[: sum(counts)])
    cols, *outs, gathered = refs[sum(counts) :]
    owns, for_mate = outs[: len(layers) * (0 in cores)], outs[-1]
    for t, count in enumerate(counts):
        at = slice(t * HEAD_DIM, (t + 1) * HEAD_DIM)
        parts, att = att[:count], att[count:]
        for core in cores:
            part, row = (parts[0], core) if count == 1 else (parts[core], 0)
            for n, i in enumerate(layers):
                block = part[row, i * HEAD_DIM : (i + 1) * HEAD_DIM, :]
                gathered[core, n * HEAD_DIM : (n + 1) * HEAD_DIM, at] = block
    tokens, width = gathered.shape[2], cols.shape[2]
    step = 512 if width % 512 == 0 else width
    for c in range(0, width, step):
        block = cols[:, :, c : c + step].reshape(tokens, step)
        for n in range(len(layers)):
            rows = slice(n * HEAD_DIM, (n + 1) * HEAD_DIM)
            if 0 in cores:
                owns[n][:, c : c + step] = dot_n(gathered[0, rows, :], block)
            if 1 in cores:
                for_mate[n, :, c : c + step] = dot_n(gathered[1, rows, :], block).astype(bf16)


def piece(ref, lead, start, size):
    at = slice(start, start + size)
    return (ref[:, at] if lead is None else ref[lead, :, at]).astype(f32)


def sum_kernel(spots, start, *refs):
    *parts, out = refs
    size = out.shape[1]
    total = None
    for (lead, first), part in zip(spots, parts, strict=True):
        value = piece(part, lead, start - first, size)
        total = value if total is None else total + value
    out[...] = total.astype(bf16)


def column_block(plan, x, part, width):
    if width % HEAD_DIM == 0:
        return x[:, pl.ds(pl.multiple_of(part * width, width), width)]
    block = jnp.zeros((HEAD_DIM, width), f32)
    for r in range(plan.per_target):
        block = jnp.where(part == r, x[:, r * width : (r + 1) * width], block)
    return block


def gram_kernel(plan, spots, own, *refs):
    parts = refs[: len(spots)]
    *outs, gram, x = refs[len(spots) :]
    x[...] = own[...]
    for (lead, first), part in zip(spots, parts, strict=True):
        size = part.shape[-1]
        x[:, first : first + size] += piece(part, lead, 0, size)
    high, middle, low = parts_of(x[...])
    pair = jnp.concatenate([high, middle], 0)
    size = gram.shape[0]
    wide = dot_t(pair, pair)
    cross = wide[:size, size:] + dot_t(high, low)
    gram[...] = wide[:size, :size] + (wide[size:, size:] + (cross + cross.T))
    mine = plan.row_part(lax.axis_index("seq"))
    for j, out in enumerate(outs):
        out[...] = column_block(plan, x, mine ^ j, out.shape[1]).astype(out.dtype)


def polynomial(gram):
    eye = (
        lax.broadcasted_iota(jnp.int32, gram.shape, 0)
        == lax.broadcasted_iota(jnp.int32, gram.shape, 1)
    ).astype(f32)
    square = jnp.sum(jnp.sum(gram * eye, axis=1, keepdims=True), axis=0, keepdims=True)
    inverse = 1.0 / (jnp.sqrt(square) + 1e-07)
    a = gram * inverse * inverse
    p = None
    for turn in range(NS_STEPS):
        a_parts = parts_of(a)
        q = coeff_a * eye + coeff_b * a + coeff_c * split_dot(a_parts, a_parts)
        q_parts = parts_of(q)
        p = q if p is None else split_dot(q_parts, parts_of(p))
        if turn + 1 < NS_STEPS:
            a = split_dot(parts_of(split_dot(q_parts, a_parts)), q_parts)
    return p, inverse


def polynomial_kernel(factor, gram, gram_other, out):
    p, inverse = polynomial(gram[...] + gram_other[...])
    out[...] = p * (inverse * factor)


def update_kernel(plan, *refs):
    *pairs, out = refs
    mine = plan.row_part(lax.axis_index("seq"))
    wide = out.shape[1] % HEAD_DIM == 0
    for j in range(plan.per_target):
        p, block = pairs[2 * j][...], pairs[2 * j + 1][...].astype(f32)
        at = pl.ds(pl.multiple_of((mine ^ j) * HEAD_DIM, HEAD_DIM), HEAD_DIM)
        out[at, :] = split_dot(parts_of(p), parts_of(block)) if wide else exact(p, block)


def local(query_tiles, key_tiles, value_tiles, attn_grad, proj_grad, neighbour):
    tile, width = query_tiles.shape[2:]
    depth = proj_grad.shape[3]
    head_count = width // HEAD_DIM
    plan = Plan(head_count)
    n, m, per = plan.seq, plan.dp, plan.per_target
    place = lax.axis_index("seq")
    struct = jax.ShapeDtypeStruct
    query, key, value, grad = (
        a.reshape(tile, width) for a in (query_tiles, key_tiles, value_tiles, attn_grad)
    )

    steps = [(i, i + 1) for i in range(1, n - 1, 2)]
    back = [(j, i) for i, j in steps]
    takes = [(i, j) for i, j in steps if j != n - 2] + [(j, i) for j, i in back if i != 1]
    gives = [(i, j) for i, j in steps if i != 1] + [(j, i) for j, i in back if j != n - 2]
    key_next = lax.ppermute(key, "seq", takes)
    value_next = lax.ppermute(value, "seq", takes)
    slot = depth // n
    flat = proj_grad.reshape(tile, depth)
    mine = plan.col_part(place)
    mine_width = per * slot

    def column_part(part):
        return jnp.concatenate(
            [
                lax.dynamic_slice_in_dim(flat, (high * plan.col + part) * 2 * slot, 2 * slot, 1)
                for high in range(plan.high)
            ],
            1,
        )

    own_columns = column_part(mine)
    key_mate = shift(after(key, own_columns), "seq", 1)
    value_mate = shift(after(value, own_columns), "seq", 1)
    beside = (key_mate, value_mate, key_next, value_next)
    columns = [own_columns] + [
        shift(after(column_part(mine ^ q), key_next, value_next), "seq", q << 1)
        for q in range(1, plan.col)
    ]
    high_columns = [
        shift(own_columns, "seq", high << (1 + plan.col_bits))
        for high in range(1, plan.high)
    ]

    attended = pl.pallas_call(
        functools.partial(forward_kernel, plan),
        out_shape=struct((plan.high, 2, m * HEAD_DIM, tile), bf16),
        in_specs=[smem()] + whole(7),
        out_specs=pl.BlockSpec(memory_space=pltpu.VMEM),
        scratch_shapes=[pltpu.VMEM((2, tile, width), bf16)],
        compiler_params=params(),
        cost_estimate=cost(8 * tile * tile * width, 16 * tile * width, 2 * tile * tile * head_count),
        name="attention_forward",
    )(neighbour, query, key, value, *beside)

    by_high = [attended[0]] + [
        shift(attended[high], "seq", high << (1 + plan.col_bits)) for high in range(1, plan.high)
    ]
    pairs = [(attended[0],)] + [
        (shift(attended[0], "seq", q << 1),) for q in range(1, plan.col)
    ]
    for came_high in by_high[1:]:
        pairs.append((came_high,))
        pairs += [
            tuple(shift(came_high[core : core + 1], "seq", q << 1) for core in range(2))
            for q in range(1, plan.col)
        ]
    counts = [len(pair) for pair in pairs]
    pairs = [part for pair in pairs for part in pair]

    dq, dko, dvo, dkf, dvf, dfar = pl.pallas_call(
        backward_kernel,
        out_shape=[
            struct((tile, width), bf16),
            struct((tile, width), f32),
            struct((tile, width), f32),
            struct((tile, width), bf16),
            struct((tile, width), bf16),
            struct((2, tile, width), bf16),
        ],
        in_specs=[smem()] + whole(8),
        out_specs=whole(6),
        scratch_shapes=[pltpu.VMEM((2, tile, width), bf16)],
        compiler_params=params(),
        cost_estimate=cost(1, 1),
        name="attention_backward",
    )(neighbour, query, key, value, *beside, after(grad, attended))

    through = lax.optimization_barrier((dq, *high_columns, jnp.stack(columns[1:])))[-1]
    held = [jnp.stack(columns)]
    late = []
    for high in range(1, plan.high):
        halves = [shift(part, "seq", high << (1 + plan.col_bits)) for part in jnp.split(through, 2, 2)]
        late.append(halves[0])
        rest = jnp.concatenate(halves, 2)
        held.append(jnp.concatenate([high_columns[high - 1][None], rest], 0))
    held = jnp.concatenate(held, 0)

    def product(name, layers, cores, *operands):
        shapes = [struct((HEAD_DIM, mine_width), f32)] * (len(layers) * (0 in cores))
        shapes += [struct((len(layers), HEAD_DIM, mine_width), bf16)] * (1 in cores)
        return pl.pallas_call(
            functools.partial(product_kernel, counts, layers, cores),
            out_shape=shapes,
            in_specs=whole(len(pairs) + 1),
            out_specs=whole(len(shapes)),
            scratch_shapes=[pltpu.VMEM((2, len(layers) * HEAD_DIM, plan.pairs * tile), bf16)],
            compiler_params=params(),
            cost_estimate=cost(
                len(cores) * len(layers) * HEAD_DIM * n * tile * mine_width,
                n * tile * mine_width,
            ),
            name=name,
        )(*operands)

    def swapped(layers, blocks, for_mate):
        mate = shift(for_mate, "seq", 1)
        return {
            i: [(block, None, 0), (mate, k, 0)]
            for k, (i, block) in enumerate(zip(layers, blocks, strict=True))
        }

    def product_pair(name, layers, *operands):
        *blocks, for_mate = product(name, layers, (0, 1), *operands)
        return swapped(layers, blocks, for_mate)

    def added(parts, start, size):
        return pl.pallas_call(
            functools.partial(sum_kernel, [spot for _, *spot in parts], start),
            out_shape=struct((HEAD_DIM, size), bf16),
            in_specs=whole(len(parts)),
            out_specs=pl.BlockSpec(memory_space=pltpu.VMEM),
            compiler_params=params(),
            cost_estimate=cost(len(parts) * HEAD_DIM * size, 4 * len(parts) * HEAD_DIM * size),
            name="block_sum",
        )(*[array for array, *_ in parts])

    first = [i for i in range(m - 1, 1, -1) if i & 1]
    middle = [i for i in range(m - 1, 1, -1) if not i & 1]
    (for_mate,) = product("product_mate", first, (1,), after(pairs[0], dq), *pairs[1:], held)
    own_first = product("product_first", first, (0,), after(pairs[0], for_mate), *pairs[1:], held)
    blocks = swapped(first, own_first, for_mate)
    going = {i: added(blocks[i], 0, mine_width) for i in first}
    blocks |= product_pair("product_middle", middle, after(pairs[0], *going.values()), *pairs[1:], held)

    blocks |= product_pair("product_near", [1], after(pairs[0], dq), *pairs[1:], held)
    blocks |= product_pair("product_own", [0], after(pairs[0], dq), *pairs[1:], held)

    extra = {i: [] for i in range(m)}
    sent = []
    bit = 1
    while bit < m:
        for i in range(m - 1, 1, -1):
            if i & -i == bit:
                if bit == 1:
                    sent.append(going[i])
                else:
                    (block, *where), *others = blocks[i] + extra[i]
                    sent.append(added([(after(block, dq), *where)] + others, 0, mine_width))
                extra[i ^ bit].append((shift(sent[-1], "dp", bit), None, 0))
        bit *= 2
    far = [
        shift(after(dfar, dq, *late), "seq", 1),
        lax.ppermute(after(dkf, dq), "seq", gives),
        lax.ppermute(after(dvf, dq), "seq", gives),
    ]
    own = blocks[0][0][0]
    came = [blocks[0][1]] + extra[0]
    parts = 1
    size = mine_width // parts
    for start in range(0, mine_width, size):
        near = after(added(blocks[1], start, size), sent[-1], blocks[0][1][0], far[0])
        came.append((shift(near, "dp", 1), None, start))
    dk, dv = pl.pallas_call(
        combine_kernel,
        out_shape=[struct((tile, width), bf16)] * 2,
        in_specs=[smem()] + whole(5),
        out_specs=whole(2),
        compiler_params=params(),
        cost_estimate=cost(6 * tile * width, 20 * tile * width),
        name="key_value_sum",
    )(
        neighbour,
        dko,
        dvo,
        *far,
    )

    *blocks_out, gram = pl.pallas_call(
        functools.partial(gram_kernel, plan, [spot for _, *spot in came]),
        out_shape=[struct((HEAD_DIM, slot), f32)]
        + [struct((HEAD_DIM, slot), bf16)] * (per - 1)
        + [struct((HEAD_DIM, HEAD_DIM), f32)],
        in_specs=whole(1 + len(came)),
        out_specs=whole(per + 1),
        scratch_shapes=[pltpu.VMEM((HEAD_DIM, mine_width), f32)],
        compiler_params=params(),
        cost_estimate=cost(12 * HEAD_DIM * HEAD_DIM * mine_width, 14 * HEAD_DIM * mine_width),
        name="gradient_sum",
    )(own, *[array for array, *_ in came])

    gram_other = jnp.zeros_like(gram)
    for b in range(plan.col_bits):
        gram = gram + gram_other
        gram_other = shift(gram, "seq", 2 << b)

    factor = 0.2 * depth**0.5
    matrix = pl.BlockSpec(memory_space=pltpu.VMEM)
    p = pl.pallas_call(
        functools.partial(polynomial_kernel, factor),
        out_shape=struct((HEAD_DIM, HEAD_DIM), f32),
        in_specs=whole(2),
        out_specs=matrix,
        compiler_params=params(),
        cost_estimate=cost(12 * HEAD_DIM * HEAD_DIM * mine_width, 8 * HEAD_DIM * mine_width),
        name="newton_schulz",
    )(after(gram, dk), gram_other)
    moved = [shift(blocks_out[j], "seq", plan.row_mask(j)) for j in range(1, per)]
    operands = [p, blocks_out[0]]
    for j in range(1, per):
        operands += [shift(after(p, *moved), "seq", plan.row_mask(j)), moved[j - 1]]
    update = pl.pallas_call(
        functools.partial(update_kernel, plan),
        out_shape=struct((per * HEAD_DIM, slot), f32),
        in_specs=whole(2 * per),
        out_specs=matrix,
        compiler_params=params(),
        cost_estimate=cost(1, 8 * per * HEAD_DIM * slot),
        name="update_rows",
    )(*operands)

    shape = query_tiles.shape
    return dq.reshape(shape), dk.reshape(shape), dv.reshape(shape), update


def solution(mesh):
    tiles = P("dp", "seq", None, None)
    return jax.shard_map(
        local,
        mesh=mesh,
        in_specs=(tiles, tiles, tiles, tiles, tiles, P("dp", None)),
        out_specs=(tiles, tiles, tiles, P("dp", "seq")),
        check_vma=False,
    )
```
